32 devices in a mesh: rep: 4 (over y, x), exp: 8 (over z, core).
Axes of the slice: x: 2, y: 2, z: 4, core: 2. Of those that a mesh axis runs over, the one named last changes fastest.
Arguments:
- tokens: bfloat16 [36864, 768], P(('rep', 'exp')), may hold values from -6 to 6
- qkv_weight: float32 [768, 2304], P('exp'), may hold values from -0.21875 to 0.21875
- out_weight: float32 [768, 768], P('exp'), may hold values from -3 to 3
- up_weight: float32 [768, 3072], P('exp'), may hold values from -0.21875 to 0.21875
- down_weight: float32 [3072, 768], P('exp'), may hold values from -0.15625 to 0.15625
- router_weight: float32 [768, 8], P('exp'), may hold values from -0.15625 to 0.15625
- first_gain: float32 [768], P('exp'), may hold values from 0.5 to 1.5
- second_gain: float32 [768], P('exp'), may hold values from 0.5 to 1.5
- third_gain: float32 [768], P('exp'), may hold values from 0.5 to 1.5
- widening: float32 [8, 768, 3072], P('exp'), may hold values from -0.21875 to 0.21875
- narrowing: float32 [8, 3072, 768], P('exp'), may hold values from -0.875 to 0.875
- expert_ids: int32 [36864, 2], P(('rep', 'exp')), may hold values from 0 to 7, all different within a row
- priority: int32 [32, 1152], P(('rep', 'exp')), may hold values from 0 to 1151, each once within a row
- cotangent: bfloat16 [36864, 768], P(('rep', 'exp')), may hold values from -6 to 6
Outputs:
- output: bfloat16 [36864, 768], P(('rep', 'exp'))
- token_grads: bfloat16 [36864, 768], P(('rep', 'exp'))
- qkv_grads: float32 [768, 2304], P('exp')
- out_grads: float32 [768, 768], P('exp')
- up_grads: float32 [768, 3072], P('exp')
- down_grads: float32 [3072, 768], P('exp')
- router_grads: float32 [768, 8], P('exp')
- first_grads: float32 [768], P('exp')
- second_grads: float32 [768], P('exp')
- third_grads: float32 [768], P('exp')
- widening_grads: float32 [8, 768, 3072], P('exp')
- narrowing_grads: float32 [8, 3072, 768], P('exp')
The draws below stay inside these ranges and needn't reach their ends.
Inputs may be any that keep to these rules, and one draw needn't show every extreme that they name: `expert_ids`: each token names 2 different experts, and every expert is named by some token. `priority`: each row holds every rank of its group once.
All inputs are finite; a program needn't handle non-finite values.
Results may differ from the reference program's by a relative error of at most 0.023.
Values may be sent and summed in bfloat16 or wider, within the bound.
No kernel may reach another device: no remote copies, remote signals or barrier semaphores. Data moves between devices by JAX's collectives and lax.ppermute only.
A program may use at most 256 MiB of HBM per device.

```python
import jax
import jax.numpy as jnp
from jax import lax

D = 768
HEADS = 12
HEAD_DIM = 64
FF = 3072
TOPK = 2
PATCHES = 576
EXPERTS = 8
TOK_DEV = 1152
CAP = 144
IMAGES = 64
TOKENS = 36864
N_REP = 4
N_EXP = 8


def block_scale(stream_key, shape, pieces, smallest, largest):
    factor_of, own = 1.0, jax.random.fold_in(stream_key, 6)
    for dim, parts in pieces:
        draws = jnp.exp(jax.random.uniform(jax.random.fold_in(own, dim), (parts,), jnp.float32, smallest / len(pieces), largest / len(pieces)))
        factor_of = factor_of * jnp.repeat(draws, shape[dim] // parts).reshape([-1 if axis == dim else 1 for axis in range(len(shape))])
    return factor_of


def different_ones(rng, rows, amount, top, lift):
    sequence = jax.random.permutation(jax.random.fold_in(rng, 1), amount)
    boost = sequence
    for power in range(3):
        boost = boost * boost // amount
    boost = boost * lift // amount
    lots = jax.random.randint(jax.random.fold_in(rng, 2), (rows, amount), 0, 4096) + boost
    fixed_rows = jax.random.permutation(jax.random.fold_in(rng, 3), rows)[jnp.arange(amount) % rows]
    lots = jnp.where(jnp.arange(rows)[:, None] == fixed_rows[None, :], 1 << 14, lots)
    score = lots * amount + jnp.arange(amount)
    return lax.top_k(score.astype(jnp.int32), top)[1].astype(jnp.int32)


def bell_draw(own_key, dims, spread, limit, pieces=(), held_as=jnp.bfloat16):
    result = spread * jax.random.normal(own_key, dims, jnp.float32)
    if pieces:
        result = result * block_scale(own_key, dims, pieces, -0.22, 0.18)
    return jnp.clip(result, -limit, limit).astype(held_as)


def setup_inputs(seed: int = 0) -> dict:
    streams_of = jax.random.split(jax.random.key(seed), 15)
    tokens = bell_draw(streams_of[0], (TOKENS, D), 1.0, 6.0, ((0, 32),))
    qkv_weight = bell_draw(streams_of[1], (D, 3 * D), D ** -0.5, 0.21875, ((0, 8),), jnp.float32)
    out_weight = bell_draw(streams_of[2], (D, D), 4 ** -0.5, 3.0, ((0, 8),), jnp.float32)
    up_weight = bell_draw(streams_of[3], (D, FF), D ** -0.5, 0.21875, ((0, 8),), jnp.float32)
    down_weight = bell_draw(streams_of[4], (FF, D), (FF // 2) ** -0.5, 0.15625, ((0, 8),), jnp.float32)
    router_weight = bell_draw(streams_of[5], (D, EXPERTS), (2 * D) ** -0.5, 0.15625, ((0, 8),), jnp.float32)
    first_gain = jnp.clip(1.0 + 0.1 * jax.random.normal(streams_of[6], (D,), jnp.float32), 0.5, 1.5)
    second_gain = jnp.clip(1.0 + 0.1 * jax.random.normal(streams_of[7], (D,), jnp.float32), 0.5, 1.5)
    third_gain = jnp.clip(1.0 + 0.1 * jax.random.normal(streams_of[8], (D,), jnp.float32), 0.5, 1.5)
    widening = bell_draw(streams_of[9], (EXPERTS, D, FF), D ** -0.5, 0.21875, ((0, 8),), jnp.float32)
    narrowing = bell_draw(streams_of[10], (EXPERTS, FF, D), (max(FF // (EXPERTS * EXPERTS), 1)) ** -0.5, 0.875, ((0, 8),), jnp.float32)
    expert_ids = different_ones(streams_of[11], TOKENS, EXPERTS, TOPK, 2048)
    priority = jax.vmap(lambda own: jax.random.permutation(own, TOK_DEV))(jax.random.split(streams_of[12], (N_REP * N_EXP))).reshape((N_REP * N_EXP, TOK_DEV)).astype(jnp.int32)
    cotangent = bell_draw(streams_of[13], (TOKENS, D), 1.0, 6.0, ((0, 32),))
    return {"tokens": tokens, "qkv_weight": qkv_weight, "out_weight": out_weight, "up_weight": up_weight, "down_weight": down_weight, "router_weight": router_weight, "first_gain": first_gain, "second_gain": second_gain, "third_gain": third_gain, "widening": widening, "narrowing": narrowing, "expert_ids": expert_ids, "priority": priority, "cotangent": cotangent}


@jax.custom_vjp
def low(v):
    return lax.optimization_barrier(v.astype(jnp.bfloat16)).astype(jnp.float32)

@jax.custom_vjp
def low_back(v):
    return v

def low_keep(v):
    return (low(v), None)

def low_pass(kept, grad):
    return (grad,)

def back_keep(v):
    return (v, None)

def back_low(kept, grad):
    return (low(grad),)
low.defvjp(low_keep, low_pass)
low_back.defvjp(back_keep, back_low)
epsilon = 1e-06

def highest(left_side, right_side):
    return jnp.dot(left_side, right_side, precision=lax.Precision.HIGHEST, preferred_element_type=jnp.float32)

def layer_norm(values, gain_row):
    centred = values - lax.optimization_barrier(jnp.mean(values, axis=-1, keepdims=True))
    variance = lax.optimization_barrier(jnp.mean(centred * centred, axis=-1, keepdims=True))
    return centred * lax.rsqrt(variance + epsilon) * gain_row

def attend_image(joined):
    queries = joined[:, :D].reshape(PATCHES, HEADS, HEAD_DIM)
    key_rows = joined[:, D:2 * D].reshape(PATCHES, HEADS, HEAD_DIM)
    value_rows = joined[:, 2 * D:].reshape(PATCHES, HEADS, HEAD_DIM)
    scores = jnp.einsum('qhd,khd->hqk', queries, key_rows, precision=lax.Precision.HIGHEST) * HEAD_DIM ** (-0.5)
    scores = low_back(scores)
    weights = low(jax.nn.softmax(scores, axis=-1))
    mixed_rows = jnp.einsum('hqk,khd->qhd', weights, value_rows, precision=lax.Precision.HIGHEST)
    return mixed_rows.reshape(PATCHES, D)

def slot_table(expert_ids, priority):
    groups = priority.shape[0]
    choices = expert_ids.reshape(groups, TOK_DEV, TOPK)
    choice_hot = (choices[..., None] == jnp.arange(EXPERTS, dtype=jnp.int32)).astype(jnp.int32)
    order = jnp.argsort(priority, axis=1).astype(jnp.int32)
    sorted_hot = jnp.take_along_axis(choice_hot, order[:, :, None, None], axis=1)
    running = jnp.cumsum(sorted_hot, axis=1) - sorted_hot
    ahead_count = jnp.take_along_axis(running, priority.astype(jnp.int32)[:, :, None, None], axis=1)
    totals = lax.optimization_barrier(jnp.sum(choice_hot, axis=1))
    prior_count = jnp.cumsum(totals, axis=1) - totals
    position = lax.optimization_barrier(jnp.sum((ahead_count + prior_count[:, None]) * choice_hot, axis=-1)).astype(jnp.int32)
    kept_mask = position < CAP
    slot_index = choices * CAP + position
    slot_grid = ((slot_index[..., None] == jnp.arange(EXPERTS * CAP, dtype=jnp.int32)) & kept_mask[..., None]).astype(jnp.float32)
    return (slot_grid, choice_hot.astype(jnp.float32).reshape(TOKENS, TOPK, EXPERTS))

def reference(tokens, qkv_weight, out_weight, up_weight, down_weight, router_weight, first_gain, second_gain, third_gain, widening, narrowing, expert_ids, priority, cotangent):
    slot_grid, choice_flat = slot_table(expert_ids, priority)
    groups = priority.shape[0]

    def forward(token_rows, qkv_master, out_master, up_master, down_master, router_master, gain_first, gain_second, gain_third, widen_master, narrow_master):
        normed = low(layer_norm(token_rows, low(gain_first)))
        joined = low_back(low(highest(normed, low(qkv_master))))
        attended = lax.map(jax.checkpoint(attend_image), joined.reshape(IMAGES, PATCHES, 3 * D))
        attended = low_back(low(attended.reshape(TOKENS, D)))
        hidden = token_rows + low_back(highest(attended, low(out_master)))
        second = low(layer_norm(hidden, low(gain_second)))
        inner_rows = low_back(highest(second, low(up_master)))
        activ_dense = low(jax.nn.gelu(inner_rows, approximate=False))
        middle = hidden + low_back(highest(activ_dense, low(down_master)))
        third_rows = low(layer_norm(middle, low(gain_third)))
        logits = low_back(highest(third_rows, low(router_master)))
        softened = jax.nn.softmax(logits, axis=-1)
        gate_values = lax.optimization_barrier(jnp.sum(softened[:, None, :] * choice_flat, axis=-1))
        grouped = third_rows.reshape(groups, TOK_DEV, D)
        sent_rows = low_back(jnp.einsum('gtks,gtd->gsd', slot_grid, grouped, precision=lax.Precision.HIGHEST))
        sent_rows = sent_rows.reshape(groups, EXPERTS, CAP, D)
        widened = low_back(jnp.einsum('gecd,edf->gecf', sent_rows, low(widen_master), precision=lax.Precision.HIGHEST))
        activated = low(jax.nn.gelu(widened, approximate=False))
        returned = jnp.einsum('gecf,efd->gecd', activated, low(narrow_master), precision=lax.Precision.HIGHEST)
        returned = low_back(low(returned)).reshape(groups, EXPERTS * CAP, D)
        picked = jnp.einsum('gtks,gsd->gtkd', slot_grid, returned, precision=lax.Precision.HIGHEST)
        weighted = picked * gate_values.reshape(groups, TOK_DEV, TOPK, 1)
        mixture = lax.optimization_barrier(jnp.sum(weighted, axis=2)).reshape(TOKENS, D)
        return middle + mixture
    masters = (tokens.astype(jnp.float32), qkv_weight, out_weight, up_weight, down_weight, router_weight, first_gain, second_gain, third_gain, widening, narrowing)
    result_rows, pullback = jax.vjp(forward, *masters)
    gradients = pullback(cotangent.astype(jnp.float32))
    return (result_rows.astype(jnp.bfloat16), gradients[0].astype(jnp.bfloat16), gradients[1], gradients[2], gradients[3], gradients[4], gradients[5], gradients[6], gradients[7], gradients[8], gradients[9], gradients[10])
```

```python
import jax
import jax.numpy as jnp
from jax import lax
from jax.experimental import pallas as pl
from jax.experimental.pallas import tpu as pltpu
from jax.sharding import PartitionSpec as P

PATCHES = 576
HEAD_DIM = 64
EPSILON = 1e-6
LOG2E = 1.4426950408889634
ROOT_HALF = 0.7071067811865476
INV_ROOT_2PI = 0.3989422804014327
bf16 = jnp.bfloat16
f32 = jnp.float32
params = pltpu.CompilerParams(vmem_limit_bytes=58 << 20)


def dot(left, right):
    return jnp.dot(left, right, preferred_element_type=f32)


def dot_nt(left, right):
    return lax.dot_general(left, right, (((1,), (1,)), ((), ())), preferred_element_type=f32)


def dot_tn(left, right):
    return lax.dot_general(left, right, (((0,), (0,)), ((), ())), preferred_element_type=f32)


def unit_norm(values):
    centred = values - jnp.mean(values, axis=-1, keepdims=True)
    inverse = lax.rsqrt(jnp.mean(centred * centred, axis=-1, keepdims=True) + EPSILON)
    return centred * inverse, inverse


def norm_inward(upstream, unit, inverse, gain):
    scaled = upstream * gain
    return inverse * (
        scaled
        - jnp.mean(scaled, axis=-1, keepdims=True)
        - unit * jnp.mean(scaled * unit, axis=-1, keepdims=True)
    )


def gelu_pair(u):
    half = 0.5 + 0.5 * lax.erf(u * ROOT_HALF)
    density = jnp.exp2(u * u * (-0.5 * LOG2E)) * INV_ROOT_2PI
    return u * half, half + u * density


def spec(shape, index):
    return pl.BlockSpec(shape, index)


def fixed(shape):
    zeros = (0,) * len(shape)
    return pl.BlockSpec(shape, lambda *_: zeros, pipeline_mode=pl.Buffered(1))


def shaped(shape, dtype):
    return jax.ShapeDtypeStruct(shape, dtype)


def attention_forward(tokens, qkv_low, gain):
    rows, width = tokens.shape
    images, pairs = rows // PATCHES, width // 128

    def kernel(x_ref, w_ref, g_ref, a_ref, qkv_ref, p_ref, o_ref):
        pair = pl.program_id(1)

        @pl.when(pair == 0)
        def _():
            unit, _ = unit_norm(x_ref[...].astype(f32))
            a = (unit * g_ref[...]).astype(bf16)
            a_ref[...] = a
            for c in range(3):
                cols = slice(c * width, (c + 1) * width)
                qkv_ref[:, cols] = dot(a, w_ref[:, cols]).astype(bf16)

        off = pl.multiple_of(pair * 128, 128)
        q = qkv_ref[:, pl.ds(off, 128)]
        k = qkv_ref[:, pl.ds(width + off, 128)]
        v = qkv_ref[:, pl.ds(2 * width + off, 128)]
        q = (q.astype(f32) * HEAD_DIM ** (-0.5)).astype(bf16)
        low_lane = lax.broadcasted_iota(jnp.int32, (PATCHES, 128), 1) < HEAD_DIM
        v_t = v.T
        outs = []
        for h in range(2):
            k_head = jnp.where(low_lane == (h == 0), k, jnp.zeros_like(k))
            s = dot_nt(k_head, q)
            top = jnp.max(s, axis=0, keepdims=True)
            e = jnp.exp2((s - top) * LOG2E)
            total = jnp.sum(e, axis=0, keepdims=True)
            p = (e * (1.0 / total)).astype(bf16)
            p_ref[0, h] = p
            outs.append(dot(v_t[h * HEAD_DIM : (h + 1) * HEAD_DIM], p))
        o_ref[...] = jnp.concatenate(outs, axis=0).T.astype(bf16)

    return pl.pallas_call(
        kernel,
        name="attention_forward",
        grid=(images, pairs),
        in_specs=[
            spec((PATCHES, width), lambda i, j: (i, 0)),
            fixed((width, 3 * width)),
            fixed((1, width)),
        ],
        out_specs=[
            spec((PATCHES, width), lambda i, j: (i, 0)),
            spec((PATCHES, 3 * width), lambda i, j: (i, 0)),
            spec((1, 2, PATCHES, PATCHES), lambda i, j: (i, j, 0, 0)),
            spec((PATCHES, 128), lambda i, j: (i, j)),
        ],
        out_shape=[
            shaped((rows, width), bf16),
            shaped((rows, 3 * width), bf16),
            shaped((images, 2 * pairs, PATCHES, PATCHES), bf16),
            shaped((rows, width), bf16),
        ],
        compiler_params=params,
    )(tokens, qkv_low, gain)


def attention_backward(dh, out_low, qkv, probs, attended, tokens, qkv_low, gain):
    rows, width = dh.shape
    images, pairs = rows // PATCHES, width // 128

    def kernel(
        dh_ref, wo_ref, qkv_ref, p_ref, o_ref, x_ref, w_ref, g_ref, dq_ref, dx_ref, dg_ref, do_ref
    ):
        image, pair = pl.program_id(0), pl.program_id(1)

        @pl.when(pair == 0)
        def _():
            do_ref[...] = dot_nt(dh_ref[...].astype(bf16), wo_ref[...]).astype(bf16)

        off = pl.multiple_of(pair * 128, 128)
        q = qkv_ref[:, pl.ds(off, 128)]
        k = qkv_ref[:, pl.ds(width + off, 128)]
        v = qkv_ref[:, pl.ds(2 * width + off, 128)]
        q = (q.astype(f32) * HEAD_DIM ** (-0.5)).astype(bf16)
        do = do_ref[:, pl.ds(off, 128)]
        low_lane = lax.broadcasted_iota(jnp.int32, (PATCHES, 128), 1) < HEAD_DIM
        prod = do.astype(f32) * o_ref[...].astype(f32)
        prod_high = prod.astype(bf16)
        prod_low = (prod - prod_high.astype(f32)).astype(bf16)
        pick_row = lax.broadcasted_iota(jnp.int32, (16, 128), 0)
        pick_lane = lax.broadcasted_iota(jnp.int32, (16, 128), 1)
        pick = (pick_lane // HEAD_DIM == pick_row).astype(bf16)
        row_sums = dot_nt(pick, prod_high) + dot_nt(pick, prod_low)
        k_t = k.T
        dqs, dks, dvs = [], [], []
        for h in range(2):
            v_head = jnp.where(low_lane == (h == 0), v, jnp.zeros_like(v))
            dp = dot_nt(v_head, do)
            p = p_ref[0, h]
            ds = (p.astype(f32) * (dp - row_sums[h : h + 1])).astype(bf16)
            dvs.append(dot(p, do))
            dks.append(dot(ds, q))
            dqs.append(dot(k_t[h * HEAD_DIM : (h + 1) * HEAD_DIM], ds))
        dq = (jnp.concatenate(dqs, axis=0) * HEAD_DIM ** (-0.5)).T
        dq_ref[:, pl.ds(off, 128)] = dq.astype(bf16)
        dq_ref[:, pl.ds(width + off, 128)] = jnp.where(low_lane, dks[0], dks[1]).astype(bf16)
        dq_ref[:, pl.ds(2 * width + off, 128)] = jnp.where(low_lane, dvs[0], dvs[1]).astype(bf16)

        @pl.when(pair == pairs - 1)
        def _():
            upstream = dot_nt(dq_ref[...], w_ref[...])
            unit, inverse = unit_norm(x_ref[...].astype(f32))
            inward = norm_inward(upstream, unit, inverse, g_ref[...])
            dx_ref[...] = (dh_ref[...] + inward).astype(bf16)
            part = jnp.sum(upstream * unit, axis=0, keepdims=True)

            @pl.when(image == 0)
            def _():
                dg_ref[...] = part

            @pl.when(image > 0)
            def _():
                dg_ref[...] += part

    return pl.pallas_call(
        kernel,
        name="attention_backward",
        grid=(images, pairs),
        in_specs=[
            spec((PATCHES, width), lambda i, j: (i, 0)),
            fixed((width, width)),
            spec((PATCHES, 3 * width), lambda i, j: (i, 0)),
            spec((1, 2, PATCHES, PATCHES), lambda i, j: (i, j, 0, 0)),
            spec((PATCHES, 128), lambda i, j: (i, j)),
            spec((PATCHES, width), lambda i, j: (i, 0)),
            fixed((width, 3 * width)),
            fixed((1, width)),
        ],
        out_specs=[
            spec((PATCHES, 3 * width), lambda i, j: (i, 0)),
            spec((PATCHES, width), lambda i, j: (i, 0)),
            spec((1, width), lambda i, j: (0, 0)),
        ],
        out_shape=[
            shaped((rows, 3 * width), bf16),
            shaped((rows, width), bf16),
            shaped((1, width), f32),
        ],
        scratch_shapes=[pltpu.VMEM((PATCHES, width), bf16)],
        compiler_params=params,
    )(dh, out_low, qkv, probs, attended, tokens, qkv_low, gain)


def dense_forward(attended, tokens, ids, out_low, up_low, down_low, router_t, gain_two, gain_three):
    rows, width = tokens.shape
    hidden = up_low.shape[1]
    experts = router_t.shape[0]
    block, chunk = 288, 512

    def kernel(
        o_ref, x_ref, id_ref, wo_ref, w1_ref, w2_ref, wr_ref, g2_ref, g3_ref,
        h_ref, b_ref, z_ref, s_ref, y_ref, m_ref, p_ref, gate_ref,
    ):
        h = x_ref[...].astype(f32) + dot(o_ref[...], wo_ref[...])
        h_ref[...] = h
        b = (unit_norm(h)[0] * g2_ref[...]).astype(bf16)
        b_ref[...] = b
        y = h
        for c in range(0, hidden, chunk):
            z, slope = gelu_pair(dot(b, w1_ref[:, c : c + chunk]))
            z = z.astype(bf16)
            z_ref[:, c : c + chunk] = z
            s_ref[:, c : c + chunk] = slope.astype(bf16)
            y = y + dot(z, w2_ref[c : c + chunk, :])
        y_ref[...] = y
        m = (unit_norm(y)[0] * g3_ref[...]).astype(bf16)
        m_ref[...] = m
        logits = dot_nt(m, wr_ref[...])
        e = jnp.exp(logits - jnp.max(logits, axis=-1, keepdims=True))
        p = e / jnp.sum(e, axis=-1, keepdims=True)
        p_ref[...] = p
        lane = lax.broadcasted_iota(jnp.int32, (block, experts), 1)
        for k in range(2):
            hot = lane == id_ref[:, k : k + 1]
            gate_ref[:, k : k + 1] = jnp.sum(jnp.where(hot, p, 0.0), axis=-1, keepdims=True)

    def by_row(cols):
        return spec((block, cols), lambda i: (i, 0))

    return pl.pallas_call(
        kernel,
        name="dense_forward",
        grid=(rows // block,),
        in_specs=[
            by_row(width), by_row(width), by_row(2),
            fixed((width, width)), fixed((width, hidden)), fixed((hidden, width)),
            fixed((experts, width)), fixed((1, width)), fixed((1, width)),
        ],
        out_specs=[
            by_row(width), by_row(width), by_row(hidden), by_row(hidden),
            by_row(width), by_row(width), by_row(experts), by_row(2),
        ],
        out_shape=[
            shaped((rows, width), f32), shaped((rows, width), bf16),
            shaped((rows, hidden), bf16), shaped((rows, hidden), bf16),
            shaped((rows, width), f32), shaped((rows, width), bf16),
            shaped((rows, experts), f32), shaped((rows, 2), f32),
        ],
        compiler_params=params,
    )(attended, tokens, ids, out_low, up_low, down_low, router_t, gain_two, gain_three)


def dense_backward(
    dx_slots, dgate_slots, slots, gates, ids, probs, cotangent, middle, hidden_rows, slope, m_rows,
    up_low, down_low, router_t, gain_two, gain_three,
):
    rows, width = cotangent.shape
    hidden = up_low.shape[1]
    experts = router_t.shape[0]
    count = dx_slots.shape[0]
    block, chunk = 288, 512

    def kernel(
        dx_ref, dgs_ref, slot_ref, gate_ref, id_ref, p_ref, cot_ref, y_ref, h_ref, s_ref, m_ref,
        w1_ref, w2_ref, wr_ref, g2_ref, g3_ref,
        dzl_ref, du_ref, dh_ref, dhl_ref, dwr_ref, dg3_ref, dg2_ref,
    ):
        first = pl.program_id(0) == 0
        slot_lane = lax.broadcasted_iota(jnp.int32, (block, count), 1)
        lane = lax.broadcasted_iota(jnp.int32, (block, experts), 1)
        p = p_ref[...]
        dp = jnp.zeros((block, experts), f32)
        weighted = jnp.zeros((block, count), f32)
        for k in range(2):
            hot = slot_lane == slot_ref[:, k : k + 1]
            weighted = weighted + jnp.where(hot, gate_ref[:, k : k + 1], 0.0)
            dgate = jnp.sum(jnp.where(hot, dgs_ref[...], 0.0), axis=-1, keepdims=True)
            dp = dp + jnp.where(lane == id_ref[:, k : k + 1], dgate, 0.0)
        dl = (p * (dp - jnp.sum(p * dp, axis=-1, keepdims=True))).astype(bf16)
        dm = dot(weighted.astype(bf16), dx_ref[...]) + dot(dl, wr_ref[...])
        dwr = dot_tn(dl, m_ref[...])
        unit, inverse = unit_norm(y_ref[...])
        dg3 = jnp.sum(dm * unit, axis=0, keepdims=True)
        dy = cot_ref[...].astype(f32) + norm_inward(dm, unit, inverse, g3_ref[...])
        dzl = dy.astype(bf16)
        dzl_ref[...] = dzl
        db = jnp.zeros((block, width), f32)
        for c in range(0, hidden, chunk):
            du = dot_nt(dzl, w2_ref[c : c + chunk, :]) * s_ref[:, c : c + chunk].astype(f32)
            du = du.astype(bf16)
            du_ref[:, c : c + chunk] = du
            db = db + dot_nt(du, w1_ref[:, c : c + chunk])
        unit, inverse = unit_norm(h_ref[...])
        dg2 = jnp.sum(db * unit, axis=0, keepdims=True)
        dh = dy + norm_inward(db, unit, inverse, g2_ref[...])
        dh_ref[...] = dh
        dhl_ref[...] = dh.astype(bf16)

        @pl.when(first)
        def _():
            dwr_ref[...] = dwr
            dg3_ref[...] = dg3
            dg2_ref[...] = dg2

        @pl.when(jnp.logical_not(first))
        def _():
            dwr_ref[...] += dwr
            dg3_ref[...] += dg3
            dg2_ref[...] += dg2

    def by_row(cols):
        return spec((block, cols), lambda i: (i, 0))

    def whole(shape):
        return spec(shape, lambda i: (0, 0))

    return pl.pallas_call(
        kernel,
        name="dense_backward",
        grid=(rows // block,),
        in_specs=[
            fixed((count, width)), fixed((1, count)), by_row(2), by_row(2), by_row(2),
            by_row(experts), by_row(width), by_row(width), by_row(width), by_row(hidden),
            by_row(width),
            fixed((width, hidden)), fixed((hidden, width)), fixed((experts, width)),
            fixed((1, width)), fixed((1, width)),
        ],
        out_specs=[
            by_row(width), by_row(hidden), by_row(width), by_row(width),
            whole((experts, width)), whole((1, width)), whole((1, width)),
        ],
        out_shape=[
            shaped((rows, width), bf16), shaped((rows, hidden), bf16),
            shaped((rows, width), f32), shaped((rows, width), bf16),
            shaped((experts, width), f32), shaped((1, width), f32), shaped((1, width), f32),
        ],
        compiler_params=params,
    )(
        dx_slots, dgate_slots, slots, gates, ids, probs, cotangent, middle, hidden_rows, slope,
        m_rows, up_low, down_low, router_t, gain_two, gain_three,
    )


def to_slots(rows_in, slot_rows, count):
    rows, width = rows_in.shape
    block = 288

    def kernel(r_ref, s_ref, o_ref):
        base = pl.program_id(0) * block
        line = base + lax.broadcasted_iota(jnp.int32, (block, rows), 0)
        hot = (line == s_ref[0:1, :]) | (line == s_ref[1:2, :])
        o_ref[...] = dot(hot.astype(bf16), r_ref[...]).astype(bf16)

    return pl.pallas_call(
        kernel,
        name="to_slots",
        grid=(count // block,),
        in_specs=[fixed((rows, width)), fixed((2, rows))],
        out_specs=spec((block, width), lambda i: (i, 0)),
        out_shape=shaped((count, width), bf16),
        compiler_params=params,
    )(rows_in, slot_rows)


def to_slots_gated(rows_in, slot_rows, gate_rows, count):
    rows, width = rows_in.shape
    block = 288

    def kernel(r_ref, s_ref, g_ref, o_ref, go_ref):
        base = pl.program_id(0) * block
        line = base + lax.broadcasted_iota(jnp.int32, (block, rows), 0)
        first, second = line == s_ref[0:1, :], line == s_ref[1:2, :]
        o_ref[...] = dot((first | second).astype(bf16), r_ref[...]).astype(bf16)
        gate = jnp.where(first, g_ref[0:1, :], 0.0) + jnp.where(second, g_ref[1:2, :], 0.0)
        go_ref[...] = jnp.sum(gate, axis=-1, keepdims=True)

    return pl.pallas_call(
        kernel,
        name="to_slots_gated",
        grid=(count // block,),
        in_specs=[fixed((rows, width)), fixed((2, rows)), fixed((2, rows))],
        out_specs=[spec((block, width), lambda i: (i, 0)), spec((block, 1), lambda i: (i, 0))],
        out_shape=[shaped((count, width), bf16), shaped((count, 1), f32)],
        compiler_params=params,
    )(rows_in, slot_rows, gate_rows)


def combine(y_slots, slots, gates, middle):
    rows, width = middle.shape
    count = y_slots.shape[0]
    block = 288

    def kernel(ys_ref, slot_ref, gate_ref, y_ref, o_ref):
        slot_lane = lax.broadcasted_iota(jnp.int32, (block, count), 1)
        weighted = jnp.zeros((block, count), f32)
        for k in range(2):
            hot = slot_lane == slot_ref[:, k : k + 1]
            weighted = weighted + jnp.where(hot, gate_ref[:, k : k + 1], 0.0)
        o_ref[...] = (y_ref[...] + dot(weighted.astype(bf16), ys_ref[...])).astype(bf16)

    def by_row(cols):
        return spec((block, cols), lambda i: (i, 0))

    return pl.pallas_call(
        kernel,
        name="combine",
        grid=(rows // block,),
        in_specs=[fixed((count, width)), by_row(2), by_row(2), by_row(width)],
        out_specs=by_row(width),
        out_shape=shaped((rows, width), bf16),
        compiler_params=params,
    )(y_slots, slots, gates, middle)


def expert_main(rows_in, widen_low, cot_wide):
    rows, width = rows_in.shape
    hidden = widen_low.shape[1]
    chunk = 512
    steps = hidden // chunk

    def kernel(x_ref, a_ref, u_ref, z_ref, v_ref, dx_ref, dg_ref, acc_ref):
        step = pl.program_id(0)
        z, slope = gelu_pair(dot(x_ref[...], a_ref[...]))
        z = z.astype(bf16)
        u = u_ref[...].astype(f32)
        v = (u * slope).astype(bf16)
        z_ref[...] = z
        v_ref[...] = v
        dg = jnp.sum(u * z.astype(f32), axis=-1, keepdims=True)
        dx = dot_nt(v, a_ref[...])

        @pl.when(step == 0)
        def _():
            acc_ref[...] = dx
            dg_ref[...] = dg

        @pl.when(step > 0)
        def _():
            acc_ref[...] += dx
            dg_ref[...] += dg

        @pl.when(step == steps - 1)
        def _():
            dx_ref[...] = acc_ref[...].astype(bf16)

    by_col = spec((rows, chunk), lambda i: (0, i))
    return pl.pallas_call(
        kernel,
        name="expert_main",
        grid=(steps,),
        in_specs=[fixed((rows, width)), spec((width, chunk), lambda i: (0, i)), by_col],
        out_specs=[
            by_col, by_col,
            spec((rows, width), lambda i: (0, 0)), spec((rows, 1), lambda i: (0, 0)),
        ],
        out_shape=[
            shaped((rows, hidden), bf16), shaped((rows, hidden), bf16),
            shaped((rows, width), bf16), shaped((rows, 1), f32),
        ],
        scratch_shapes=[pltpu.VMEM((rows, width), f32)],
        compiler_params=params,
    )(rows_in, widen_low, cot_wide)


def product_low(left, right, chunk=1024):
    rows, depth = left.shape
    cols = right.shape[1]

    def kernel(l_ref, r_ref, o_ref):
        o_ref[...] = dot(l_ref[...], r_ref[...]).astype(bf16)

    block = 384
    return pl.pallas_call(
        kernel,
        name="product_low",
        grid=(rows // block,),
        in_specs=[spec((block, depth), lambda i: (i, 0)), fixed((depth, cols))],
        out_specs=spec((block, cols), lambda i: (i, 0)),
        out_shape=shaped((rows, cols), bf16),
        compiler_params=params,
    )(left, right)


def product_wide(left, right_t, chunk=1024):
    rows, depth = left.shape
    cols = right_t.shape[0]

    def kernel(l_ref, r_ref, o_ref):
        o_ref[...] = dot_nt(l_ref[...], r_ref[...]).astype(bf16)

    return pl.pallas_call(
        kernel,
        name="product_wide",
        grid=(cols // chunk,),
        in_specs=[fixed((rows, depth)), spec((chunk, depth), lambda i: (i, 0))],
        out_specs=spec((rows, chunk), lambda i: (0, i)),
        out_shape=shaped((rows, cols), bf16),
        compiler_params=params,
    )(left, right_t)


def outer_by_right(left, right, chunk):
    rows, mine = left.shape
    cols = right.shape[1]

    def kernel(l_ref, r_ref, o_ref):
        o_ref[...] = dot_tn(l_ref[...], r_ref[...]).astype(bf16)

    return pl.pallas_call(
        kernel,
        name="outer_by_right",
        grid=(cols // chunk,),
        in_specs=[fixed((rows, mine)), spec((rows, chunk), lambda i: (0, i))],
        out_specs=spec((mine, chunk), lambda i: (0, i)),
        out_shape=shaped((mine, cols), bf16),
        compiler_params=params,
    )(left, right)


def outer_by_left(left, right, chunk):
    rows, mine = left.shape
    cols = right.shape[1]

    def kernel(l_ref, r_ref, o_ref):
        o_ref[...] = dot_tn(l_ref[...], r_ref[...]).astype(bf16)

    return pl.pallas_call(
        kernel,
        name="outer_by_left",
        grid=(mine // chunk,),
        in_specs=[spec((rows, chunk), lambda i: (0, i)), fixed((rows, cols))],
        out_specs=spec((chunk, cols), lambda i: (i, 0)),
        out_shape=shaped((mine, cols), bf16),
        compiler_params=params,
    )(left, right)


def body(
    tokens, qkv_weight, out_weight, up_weight, down_weight, router_weight,
    first_gain, second_gain, third_gain, widening, narrowing, expert_ids, priority, cotangent,
):
    rows, width = tokens.shape
    ranks = lax.axis_size("exp")
    experts = widening.shape[0] * ranks
    capacity = (rows + experts - 1) // experts
    count = experts * capacity

    def gather(array):
        return lax.all_gather(array, "exp", axis=0, tiled=True)

    small = jnp.concatenate(
        [router_weight, first_gain[:, None], second_gain[:, None], third_gain[:, None]], axis=1
    ).astype(bf16)
    qkv_low = gather(qkv_weight.astype(bf16))
    small = gather(small)
    out_low = gather(out_weight.astype(bf16))
    up_low = gather(up_weight.astype(bf16))
    down_low = gather(down_weight.astype(bf16))
    small_t = small.T
    router_t = small_t[:experts]
    gains = small_t[experts:].astype(f32)
    gain_one, gain_two, gain_three = gains[0:1], gains[1:2], gains[2:3]

    choice_hot = (expert_ids[:, :, None] == jnp.arange(experts, dtype=jnp.int32)).astype(f32)
    rank_row = priority[0]
    earlier = (rank_row[None, :] < rank_row[:, None]).astype(bf16)
    ahead = dot(earlier, choice_hot.reshape(rows, -1).astype(bf16)).reshape(choice_hot.shape)
    totals = jnp.sum(choice_hot, axis=0)
    prior = jnp.cumsum(totals, axis=0) - totals
    position = jnp.sum((ahead + prior[None]) * choice_hot, axis=-1).astype(jnp.int32)
    slots = jnp.where(position < capacity, expert_ids * capacity + position, -1)
    slot_rows = slots.T

    def exchange(array):
        return lax.all_to_all(
            array.reshape(experts, capacity, width), "exp", split_axis=0, concat_axis=0, tiled=True
        ).reshape(count, width)

    def exchange_small(column):
        everyone = lax.all_gather(column.reshape(1, experts, capacity), "exp", axis=0, tiled=True)
        return lax.dynamic_slice_in_dim(everyone, lax.axis_index("exp"), 1, 1).reshape(count)

    cot_here = exchange(to_slots(cotangent, slot_rows, count))
    widen_low = widening[0].astype(bf16)
    narrow_low = narrowing[0].astype(bf16)
    cot_wide = product_wide(cot_here, narrow_low)

    first_low, qkv, probs, attended = attention_forward(tokens, qkv_low, gain_one)
    hidden, second_low, activ, slope, middle, third_low, soft, gates = dense_forward(
        attended, tokens, expert_ids, out_low, up_low, down_low, router_t, gain_two, gain_three
    )
    sent, gate_slots = to_slots_gated(third_low, slot_rows, gates.T, count)
    arrived = exchange(sent)
    gate_here = exchange_small(gate_slots)[:, None]

    z_rows, v_rows, dx_rows, dgate_rows = expert_main(arrived, widen_low, cot_wide)
    dx_slots = exchange(dx_rows)
    dgate_slots = exchange_small(dgate_rows)[None, :]
    dy_rows = (cot_here.astype(f32) * gate_here).astype(bf16)
    narrow_grads = outer_by_left(z_rows, dy_rows, 1024)
    gated_rows = (arrived.astype(f32) * gate_here).astype(bf16)
    widen_grads = outer_by_right(gated_rows, v_rows, 1024)
    y_slots = exchange(product_low(z_rows, narrow_low))
    output = combine(y_slots, slots, gates, middle)

    dzl, du, dh, dhl, router_part, third_part, second_part = dense_backward(
        dx_slots, dgate_slots, slots, gates, expert_ids, soft, cotangent, middle, hidden, slope,
        third_low, up_low, down_low, router_t, gain_two, gain_three,
    )
    down_grads = outer_by_left(activ, dzl, 1024)
    up_grads = outer_by_right(second_low, du, 1024)
    out_grads = outer_by_right(attended, dhl, 768)
    dqkv, token_grads, first_part = attention_backward(
        dh, out_low, qkv, probs, attended, tokens, qkv_low, gain_one
    )
    qkv_grads = outer_by_right(first_low, dqkv, 1152 if False else 768)

    def reduce_dense(array):
        return lax.psum_scatter(array, "exp", scatter_dimension=0, tiled=True)

    small_part = jnp.concatenate([router_part, first_part, second_part, third_part], axis=0)
    small_sum = lax.psum(small_part.astype(bf16), ("exp", "rep")).astype(f32)
    mine = lax.dynamic_slice_in_dim(
        small_sum, lax.axis_index("exp") * router_weight.shape[0], router_weight.shape[0], 1
    )

    def over_rep(array):
        return lax.psum(array, "rep").astype(f32)

    narrow_out = over_rep(narrow_grads)[None]
    widen_out = over_rep(widen_grads)[None]
    down_out = over_rep(reduce_dense(down_grads))
    up_out = over_rep(reduce_dense(up_grads))
    out_out = over_rep(reduce_dense(out_grads))
    qkv_out = over_rep(reduce_dense(qkv_grads))
    return (
        output, token_grads, qkv_out, out_out, up_out, down_out,
        mine[:experts].T, mine[experts], mine[experts + 1], mine[experts + 2],
        widen_out, narrow_out,
    )


def solution(mesh):
    rows_spec, exp_spec = P(("rep", "exp"), None), P("exp", None)
    return jax.shard_map(
        body,
        mesh=mesh,
        in_specs=(
            rows_spec, exp_spec, exp_spec, exp_spec, exp_spec, exp_spec,
            P("exp"), P("exp"), P("exp"), P("exp", None, None), P("exp", None, None),
            rows_spec, rows_spec, rows_spec,
        ),
        out_specs=(
            rows_spec, rows_spec, exp_spec, exp_spec, exp_spec, exp_spec, exp_spec,
            P("exp"), P("exp"), P("exp"), P("exp", None, None), P("exp", None, None),
        ),
        check_vma=False,
    )
```

```python
import jax
import jax.numpy as jnp
from jax import lax
from jax.experimental import pallas as pl
from jax.experimental.pallas import tpu as pltpu
from jax.sharding import PartitionSpec as P

PATCHES = 576
HEAD_DIM = 64
EPSILON = 1e-6
LOG2E = 1.4426950408889634
ROOT_HALF = 0.7071067811865476
INV_ROOT_2PI = 0.3989422804014327
bf16 = jnp.bfloat16
f32 = jnp.float32
params = pltpu.CompilerParams(vmem_limit_bytes=58 << 20)


def dot(left, right):
    return jnp.dot(left, right, preferred_element_type=f32)


def dot_nt(left, right):
    return lax.dot_general(left, right, (((1,), (1,)), ((), ())), preferred_element_type=f32)


def dot_tn(left, right):
    return lax.dot_general(left, right, (((0,), (0,)), ((), ())), preferred_element_type=f32)


def unit_norm(values):
    centred = values - jnp.mean(values, axis=-1, keepdims=True)
    inverse = lax.rsqrt(jnp.mean(centred * centred, axis=-1, keepdims=True) + EPSILON)
    return centred * inverse, inverse


def norm_inward(upstream, unit, inverse, gain):
    scaled = upstream * gain
    return inverse * (
        scaled
        - jnp.mean(scaled, axis=-1, keepdims=True)
        - unit * jnp.mean(scaled * unit, axis=-1, keepdims=True)
    )


def gelu_pair(u):
    half = 0.5 + 0.5 * lax.erf(u * ROOT_HALF)
    density = jnp.exp2(u * u * (-0.5 * LOG2E)) * INV_ROOT_2PI
    return u * half, half + u * density


def cost(microseconds):
    return pl.CostEstimate(
        flops=int(microseconds * 8e+08), bytes_accessed=int(microseconds * 2e+06), transcendentals=0
    )


def spec(shape, index):
    return pl.BlockSpec(shape, index)


def fixed(shape):
    zeros = (0,) * len(shape)
    return pl.BlockSpec(shape, lambda *_: zeros, pipeline_mode=pl.Buffered(1))


def shaped(shape, dtype):
    return jax.ShapeDtypeStruct(shape, dtype)


any_space = pl.BlockSpec(memory_space=pl.ANY)
scalar_space = pl.BlockSpec(memory_space=pltpu.SMEM)


def attention_forward(rows_in, weight, small, first_pair, pairs, pairs_all, earlier):
    rows, width = rows_in.shape
    images, first = rows // PATCHES, earlier is None
    cols = 384 * pairs

    def kernel(*refs):
        if first:
            (core_ref, x_ref, hw_ref, kw_ref, qkv_ref, p_ref, o_ref, a_ref, st_ref,
             w_ref, sem, sm_ref, sem_small) = refs
        else:
            (core_ref, a_ref, hw_ref, kw_ref, _, _, _, qkv_ref, p_ref, o_ref, w_ref, sem) = refs
        image, pair = pl.program_id(0), pl.program_id(1)

        @pl.when((pair == 0) & (image == 0))
        def _():
            load_halves(core_ref[0], hw_ref, kw_ref, w_ref, sem, 384 * first_pair, cols)
            if first:
                load_halves(core_ref[0], hw_ref, kw_ref, sm_ref, sem_small, 3 * width, 128)
                st_ref[...] = sm_ref[...].astype(f32).T

        if first:
            @pl.when(pair == 0)
            def _():
                unit, _ = unit_norm(x_ref[...].astype(f32))
                a_ref[...] = (unit * st_ref[small : small + 1, :]).astype(bf16)

        qkv = dot(a_ref[...], w_ref[:, pl.ds(pl.multiple_of(pair * 384, 128), 384)]).astype(bf16)
        qkv_ref[...] = qkv
        q, k, v = qkv[:, :128], qkv[:, 128:256], qkv[:, 256:]
        q = (q.astype(f32) * HEAD_DIM ** (-0.5)).astype(bf16)
        low_lane = lax.broadcasted_iota(jnp.int32, (PATCHES, 128), 1) < HEAD_DIM
        v_t = v.T
        outs = []
        for h in range(2):
            k_head = jnp.where(low_lane == (h == 0), k, jnp.zeros_like(k))
            s = dot_nt(k_head, q)
            top = jnp.max(s, axis=0, keepdims=True)
            e = jnp.exp2((s - top) * LOG2E)
            total = jnp.sum(e, axis=0, keepdims=True)
            p = (e * (1.0 / total)).astype(bf16)
            p_ref[0, h] = p
            outs.append(dot(v_t[h * HEAD_DIM : (h + 1) * HEAD_DIM], p))
        o_ref[...] = jnp.concatenate(outs, axis=0).T.astype(bf16)

    groups = weight[1].shape[0]
    by_image = spec((PATCHES, width), lambda i, j: (i, 0))
    out_specs = [
        spec((PATCHES, 384), lambda i, j: (i, j + first_pair)),
        spec((1, 2, PATCHES, PATCHES), lambda i, j: (i, j + first_pair, 0, 0)),
        spec((PATCHES, 128), lambda i, j: (i, j + first_pair)),
    ]
    out_shape = [
        shaped((rows, 384 * pairs_all), bf16),
        shaped((images, 2 * pairs_all, PATCHES, PATCHES), bf16),
        shaped((rows, 128 * pairs_all), bf16),
    ]
    in_specs = [scalar_space, by_image, any_space, any_space]
    scratch = [pltpu.VMEM((width, cols), bf16), pltpu.SemaphoreType.DMA((2, groups))]
    if first:
        out_specs += [by_image, spec((128, width), lambda i, j: (0, 0))]
        out_shape += [shaped((rows, width), bf16), shaped((128, width), f32)]
        scratch += [pltpu.VMEM((width, 128), bf16), pltpu.SemaphoreType.DMA((2, groups))]
        operands, aliases = (weight[0], rows_in, *weight[1:]), {}
    else:
        in_specs += [any_space] * 3
        operands, aliases = (weight[0], rows_in, *weight[1:], *earlier), {4: 0, 5: 1, 6: 2}
    return pl.pallas_call(
        kernel,
        name="attention_forward",
        cost_estimate=cost(8 * images * pairs // 4),
        grid=(images, pairs),
        in_specs=in_specs,
        out_specs=out_specs,
        out_shape=out_shape,
        scratch_shapes=scratch,
        input_output_aliases=aliases,
        compiler_params=params,
    )(*operands)


def attention_backward(image, dh, out_weight, qkv, probs, attended, tokens, qkv_weight, gain):
    width = dh.shape[1]
    pairs = width // 128

    def kernel(
        core_ref, dh_ref, ho_ref, ko_ref, qkv_ref, p_ref, o_ref, x_ref, hw_ref, kw_ref, g_ref,
        dq_ref, dx_ref, dg_ref, do_ref, db_ref, wo_ref, w_ref, sem, sem_w,
    ):
        pair = pl.program_id(0)

        @pl.when(pair == 0)
        def _():
            load_halves(core_ref[0], ho_ref, ko_ref, wo_ref, sem, 0, width)
            load_halves(core_ref[0], hw_ref, kw_ref, w_ref, sem_w, 0, 3 * width)

        @pl.when(pair == 0)
        def _():
            do = dot_nt(dh_ref[...].astype(bf16), wo_ref[...]).astype(bf16)
            for j in range(pairs):
                do_ref[j] = do[:, j * 128 : (j + 1) * 128]

        q, k, v = qkv_ref[:, :128], qkv_ref[:, 128:256], qkv_ref[:, 256:]
        q = (q.astype(f32) * HEAD_DIM ** (-0.5)).astype(bf16)
        do = do_ref[pair]
        low_lane = lax.broadcasted_iota(jnp.int32, (PATCHES, 128), 1) < HEAD_DIM
        prod = do.astype(f32) * o_ref[...].astype(f32)
        prod_high = prod.astype(bf16)
        prod_low = (prod - prod_high.astype(f32)).astype(bf16)
        pick_row = lax.broadcasted_iota(jnp.int32, (16, 128), 0)
        pick_lane = lax.broadcasted_iota(jnp.int32, (16, 128), 1)
        pick = (pick_lane // HEAD_DIM == pick_row).astype(bf16)
        row_sums = dot_nt(pick, prod_high) + dot_nt(pick, prod_low)
        k_t = k.T
        dqs, dks, dvs = [], [], []
        for h in range(2):
            v_head = jnp.where(low_lane == (h == 0), v, jnp.zeros_like(v))
            dp = dot_nt(v_head, do)
            p = p_ref[0, h]
            ds = (p.astype(f32) * (dp - row_sums[h : h + 1])).astype(bf16)
            dvs.append(dot(p, do))
            dks.append(dot(ds, q))
            dqs.append(dot(k_t[h * HEAD_DIM : (h + 1) * HEAD_DIM], ds))
        dq = (jnp.concatenate(dqs, axis=0) * HEAD_DIM ** (-0.5)).T
        dqkv = jnp.concatenate(
            [dq, jnp.where(low_lane, dks[0], dks[1]), jnp.where(low_lane, dvs[0], dvs[1])], axis=1
        ).astype(bf16)
        dq_ref[...] = dqkv

        w_pair = w_ref[:, pl.ds(pl.multiple_of(pair * 384, 128), 384)]

        @pl.when(pair == 0)
        def _():
            db_ref[...] = dot_nt(dqkv, w_pair)

        @pl.when(pair > 0)
        def _():
            db_ref[...] += dot_nt(dqkv, w_pair)

        @pl.when(pair == pairs - 1)
        def _():
            upstream = db_ref[...]
            unit, inverse = unit_norm(x_ref[...].astype(f32))
            inward = norm_inward(upstream, unit, inverse, g_ref[...])
            dx_ref[...] = (dh_ref[...] + inward).astype(bf16)
            dg_ref[...] = jnp.sum(upstream * unit, axis=0, keepdims=True)

    by_image = spec((PATCHES, width), lambda j: (image, 0))
    out_image = spec((PATCHES, width), lambda j: (0, 0))
    return pl.pallas_call(
        kernel,
        name="attention_backward",
        cost_estimate=cost(21),
        grid=(pairs,),
        in_specs=[
            scalar_space, by_image, any_space, any_space,
            spec((PATCHES, 384), lambda j: (image, j)),
            spec((1, 2, PATCHES, PATCHES), lambda j: (image, j, 0, 0)),
            spec((PATCHES, 128), lambda j: (image, j)),
            by_image,
            any_space, any_space,
            fixed((1, width)),
        ],
        out_specs=[
            spec((PATCHES, 384), lambda j: (0, j)), out_image,
            spec((1, width), lambda j: (0, 0)),
        ],
        out_shape=[
            shaped((PATCHES, 3 * width), bf16), shaped((PATCHES, width), bf16),
            shaped((1, width), f32),
        ],
        scratch_shapes=[
            pltpu.VMEM((pairs, PATCHES, 128), bf16),
            pltpu.VMEM((PATCHES, width), f32),
            pltpu.VMEM((width, width), bf16),
            pltpu.VMEM((width, 3 * width), bf16),
            pltpu.SemaphoreType.DMA((2, out_weight[1].shape[0])),
            pltpu.SemaphoreType.DMA((2, out_weight[1].shape[0])),
        ],
        compiler_params=params,
    )(out_weight[0], dh, *out_weight[1:], qkv, probs, attended, tokens, *qkv_weight[1:], gain)


def load_halves(core, mine_ref, other_ref, whole_ref, sem, start, cols):
    groups, rows, _ = mine_ref.shape
    copies = []
    for z in range(groups):
        for side, ref in enumerate((mine_ref, other_ref)):
            place = core if side == 0 else 1 - core
            base = pl.multiple_of((2 * z + place) * rows, 16)
            copies.append(
                pltpu.make_async_copy(
                    ref.at[z, :, pl.ds(start, cols)],
                    whole_ref.at[pl.ds(base, rows), :],
                    sem.at[side, z],
                )
            )
    for copy in copies:
        copy.start()
    for copy in copies:
        copy.wait()


def assemble(place, parts, layout, total):
    groups, rows, _ = parts[0].shape

    def kernel(r_ref, own_ref, x_ref, y_ref, far_ref, o_ref):
        down, right = r_ref[0] // 2, r_ref[0] % 2

        def put(ref, row_half, col_half):
            at = pl.multiple_of(row_half * rows, 16)
            for start, wide, base, step in layout:
                to = pl.multiple_of(base + col_half * step, 128)
                o_ref[:, pl.ds(at, rows), pl.ds(to, wide)] = ref[:, :, start : start + wide]

        put(own_ref, down, right)
        put(x_ref, down, 1 - right)
        put(y_ref, 1 - down, right)
        put(far_ref, 1 - down, 1 - right)

    return pl.pallas_call(
        kernel,
        name="assemble",
        cost_estimate=cost(4),
        in_specs=[scalar_space] + [pl.BlockSpec(memory_space=pltpu.VMEM)] * 4,
        out_specs=pl.BlockSpec(memory_space=pltpu.VMEM),
        out_shape=shaped((groups, 2 * rows, total), bf16),
        compiler_params=params,
    )(place, *parts)


def by_rows(block, cols):
    return spec((block, cols), lambda i: (i, 0))


def whole(shape):
    return spec(shape, lambda i: (0,) * len(shape))


def dense_up(attended, tokens, weights, gain):
    rows, width = tokens.shape
    hidden = weights[1].shape[2] - width
    block, chunk = 288, 512

    def kernel(
        core_ref, o_ref, x_ref, hw_ref, kw_ref, g_ref, h_ref, b_ref, z_ref, s_ref, w_ref, sem
    ):
        @pl.when(pl.program_id(0) == 0)
        def _():
            load_halves(core_ref[0], hw_ref, kw_ref, w_ref, sem, 0, width + hidden)

        h = x_ref[...].astype(f32) + dot(o_ref[...], w_ref[:, :width])
        h_ref[...] = h
        b = (unit_norm(h)[0] * g_ref[...]).astype(bf16)
        b_ref[...] = b
        for c in range(0, hidden, chunk):
            z, slope = gelu_pair(dot(b, w_ref[:, width + c : width + c + chunk]))
            z_ref[:, c : c + chunk] = z.astype(bf16)
            s_ref[:, c : c + chunk] = slope.astype(bf16)

    return pl.pallas_call(
        kernel,
        name="dense_up",
        cost_estimate=cost(18),
        grid=(rows // block,),
        in_specs=[
            scalar_space, by_rows(block, width), by_rows(block, width), any_space, any_space,
            fixed((1, width)),
        ],
        out_specs=[
            by_rows(block, width), by_rows(block, width), by_rows(block, hidden),
            by_rows(block, hidden),
        ],
        out_shape=[
            shaped((rows, width), f32), shaped((rows, width), bf16),
            shaped((rows, hidden), bf16), shaped((rows, hidden), bf16),
        ],
        scratch_shapes=[
            pltpu.VMEM((width, width + hidden), bf16),
            pltpu.SemaphoreType.DMA((2, weights[1].shape[0])),
        ],
        compiler_params=params,
    )(weights[0], attended, tokens, *weights[1:], gain)


def dense_down(activ, hidden_rows, ids, weights, router_t, gain):
    rows, width = hidden_rows.shape
    hidden = activ.shape[1]
    experts = router_t.shape[0]
    block = 288

    def kernel(
        core_ref, z_ref, h_ref, id_ref, hw_ref, kw_ref, wr_ref, g_ref,
        y_ref, m_ref, gate_ref, w_ref, sem,
    ):
        @pl.when(pl.program_id(0) == 0)
        def _():
            load_halves(core_ref[0], hw_ref, kw_ref, w_ref, sem, 0, width)

        y = h_ref[...] + dot(z_ref[...], w_ref[...])
        y_ref[...] = y
        m = (unit_norm(y)[0] * g_ref[...]).astype(bf16)
        m_ref[...] = m
        logits = dot_nt(m, wr_ref[...].astype(bf16))
        e = jnp.exp(logits - jnp.max(logits, axis=-1, keepdims=True))
        p = e / jnp.sum(e, axis=-1, keepdims=True)
        lane = lax.broadcasted_iota(jnp.int32, (block, experts), 1)
        for k in range(2):
            hot = lane == id_ref[:, k : k + 1]
            gate_ref[:, k : k + 1] = jnp.sum(jnp.where(hot, p, 0.0), axis=-1, keepdims=True)

    return pl.pallas_call(
        kernel,
        name="dense_down",
        cost_estimate=cost(15),
        grid=(rows // block,),
        in_specs=[
            scalar_space, by_rows(block, hidden), by_rows(block, width), by_rows(block, 2),
            any_space, any_space, fixed((experts, width)), fixed((1, width)),
        ],
        out_specs=[by_rows(block, width), by_rows(block, width), by_rows(block, 2)],
        out_shape=[
            shaped((rows, width), f32), shaped((rows, width), bf16), shaped((rows, 2), f32),
        ],
        scratch_shapes=[
            pltpu.VMEM((hidden, width), bf16),
            pltpu.SemaphoreType.DMA((2, weights[1].shape[0])),
        ],
        compiler_params=params,
    )(weights[0], activ, hidden_rows, ids, *weights[1:], router_t, gain)


def gated_rows(slot_ref, gate_ref, slots_refs, block):
    total, base = None, 0
    for ref in slots_refs:
        count = ref.shape[0]
        lane = base + lax.broadcasted_iota(jnp.int32, (block, count), 1)
        weighted = jnp.zeros((block, count), f32)
        for k in range(2):
            hot = lane == slot_ref[:, k : k + 1]
            weighted = weighted + jnp.where(hot, gate_ref[:, k : k + 1], 0.0)
        part = dot(weighted.astype(bf16), ref[...])
        total = part if total is None else total + part
        base += count
    return total


def norm_three_backward(dx_slots, slots, gates, cotangent, middle, gain):
    rows, width = cotangent.shape
    block = 288

    def kernel(da_ref, db_ref, slot_ref, gate_ref, cot_ref, y_ref, g_ref, dy_ref, dzl_ref, dg_ref):
        dm = gated_rows(slot_ref, gate_ref, (da_ref, db_ref), block)
        unit, inverse = unit_norm(y_ref[...])
        part = jnp.sum(dm * unit, axis=0, keepdims=True)
        dy = cot_ref[...].astype(f32) + norm_inward(dm, unit, inverse, g_ref[...])
        dy_ref[...] = dy
        dzl_ref[...] = dy.astype(bf16)
        first = pl.program_id(0) == 0

        @pl.when(first)
        def _():
            dg_ref[...] = part

        @pl.when(jnp.logical_not(first))
        def _():
            dg_ref[...] += part

    return pl.pallas_call(
        kernel,
        name="norm_three_backward",
        cost_estimate=cost(10),
        grid=(rows // block,),
        in_specs=[
            fixed(dx_slots[0].shape), fixed(dx_slots[1].shape), by_rows(block, 2),
            by_rows(block, 2), by_rows(block, width), by_rows(block, width), fixed((1, width)),
        ],
        out_specs=[by_rows(block, width), by_rows(block, width), whole((1, width))],
        out_shape=[shaped((rows, width), f32), shaped((rows, width), bf16), shaped((1, width), f32)],
        compiler_params=params,
    )(*dx_slots, slots, gates, cotangent, middle, gain)


def dense_backward(dzl, dy, slope, hidden_rows, up_weight, down_weight, gain):
    rows, width = dy.shape
    hidden = slope.shape[1]
    block, chunk = 288, 512

    def kernel(
        core_ref, dzl_ref, dy_ref, s_ref, h_ref, hu_ref, ku_ref, hd_ref, kd_ref, g_ref,
        du_ref, dh_ref, dhl_ref, dg_ref, w1_ref, w2_ref, sem,
    ):
        first = pl.program_id(0) == 0

        @pl.when(first)
        def _():
            load_halves(core_ref[0], hd_ref, kd_ref, w2_ref, sem, 0, width)
            load_halves(core_ref[0], hu_ref, ku_ref, w1_ref, sem, width, hidden)

        dzl = dzl_ref[...]
        db = jnp.zeros((block, width), f32)
        for c in range(0, hidden, chunk):
            du = dot_nt(dzl, w2_ref[c : c + chunk, :]) * s_ref[:, c : c + chunk].astype(f32)
            du = du.astype(bf16)
            du_ref[:, c : c + chunk] = du
            db = db + dot_nt(du, w1_ref[:, c : c + chunk])
        unit, inverse = unit_norm(h_ref[...])
        part = jnp.sum(db * unit, axis=0, keepdims=True)
        dh = dy_ref[...] + norm_inward(db, unit, inverse, g_ref[...])
        dh_ref[...] = dh
        dhl_ref[...] = dh.astype(bf16)

        @pl.when(first)
        def _():
            dg_ref[...] = part

        @pl.when(jnp.logical_not(first))
        def _():
            dg_ref[...] += part

    return pl.pallas_call(
        kernel,
        name="dense_backward",
        cost_estimate=cost(24),
        grid=(rows // block,),
        in_specs=[
            scalar_space, by_rows(block, width), by_rows(block, width), by_rows(block, hidden),
            by_rows(block, width), any_space, any_space, any_space, any_space, fixed((1, width)),
        ],
        out_specs=[
            by_rows(block, hidden), by_rows(block, width), by_rows(block, width),
            whole((1, width)),
        ],
        out_shape=[
            shaped((rows, hidden), bf16), shaped((rows, width), f32), shaped((rows, width), bf16),
            shaped((1, width), f32),
        ],
        scratch_shapes=[
            pltpu.VMEM((width, hidden), bf16), pltpu.VMEM((hidden, width), bf16),
            pltpu.SemaphoreType.DMA((2, up_weight[1].shape[0])),
        ],
        compiler_params=params,
    )(up_weight[0], dzl, dy, slope, hidden_rows, *up_weight[1:], *down_weight[1:], gain)


def combine(y_slots, slots, gates, middle):
    rows, width = middle.shape
    block = 288

    def kernel(ya_ref, slot_ref, gate_ref, y_ref, o_ref):
        o_ref[...] = (
            y_ref[...] + gated_rows(slot_ref, gate_ref, (ya_ref,), block)
        ).astype(bf16)

    return pl.pallas_call(
        kernel,
        name="combine",
        cost_estimate=cost(8),
        grid=(rows // block,),
        in_specs=[
            fixed(y_slots.shape), by_rows(block, 2), by_rows(block, 2), by_rows(block, width),
        ],
        out_specs=by_rows(block, width),
        out_shape=shaped((rows, width), bf16),
        compiler_params=params,
    )(y_slots, slots, gates, middle)


def expert_main(me, rows_in, widen_low, cot_wide, router_t):
    rows, width = rows_in.shape
    hidden = widen_low.shape[1]
    experts = router_t.shape[0]
    chunk = 512
    steps = hidden // chunk

    def kernel(
        me_ref, x_ref, a_ref, u_ref, wr_ref,
        z_ref, v_ref, dx_ref, gate_ref, dwr_ref, acc_ref, dg_ref,
    ):
        step = pl.program_id(0)
        x = x_ref[...]
        z, slope = gelu_pair(dot(x, a_ref[...]))
        z = z.astype(bf16)
        u = u_ref[...].astype(f32)
        v = (u * slope).astype(bf16)
        z_ref[...] = z
        v_ref[...] = v
        dg = jnp.sum(u * z.astype(f32), axis=-1, keepdims=True)
        dx = dot_nt(v, a_ref[...])

        @pl.when(step == 0)
        def _():
            acc_ref[...] = dx
            dg_ref[...] = dg

        @pl.when(step > 0)
        def _():
            acc_ref[...] += dx
            dg_ref[...] += dg

        @pl.when(step == steps - 1)
        def _():
            wr = wr_ref[...].astype(bf16)
            logits = dot_nt(x, wr)
            e = jnp.exp(logits - jnp.max(logits, axis=-1, keepdims=True))
            p = e / jnp.sum(e, axis=-1, keepdims=True)
            own = lax.broadcasted_iota(jnp.int32, (rows, experts), 1) == me_ref[0]
            gate = jnp.sum(jnp.where(own, p, 0.0), axis=-1, keepdims=True)
            gate_ref[...] = gate
            spread = dg_ref[...] * (own.astype(f32) - p)
            dx_ref[...] = (acc_ref[...] + dot(spread.astype(bf16), wr)).astype(bf16)
            dwr_ref[...] = dot_tn((gate * spread).astype(bf16), x)

    by_col = spec((rows, chunk), lambda i: (0, i))
    return pl.pallas_call(
        kernel,
        name="expert_main",
        cost_estimate=cost(15),
        grid=(steps,),
        in_specs=[
            scalar_space, fixed((rows, width)), spec((width, chunk), lambda i: (0, i)), by_col,
            fixed((experts, width)),
        ],
        out_specs=[by_col, by_col, whole((rows, width)), whole((rows, 1)), whole((experts, width))],
        out_shape=[
            shaped((rows, hidden), bf16), shaped((rows, hidden), bf16),
            shaped((rows, width), bf16), shaped((rows, 1), f32), shaped((experts, width), f32),
        ],
        scratch_shapes=[pltpu.VMEM((rows, width), f32), pltpu.VMEM((rows, 1), f32)],
        compiler_params=params,
    )(me, rows_in, widen_low, cot_wide, router_t)


def narrow_outer(activs, cots, gates):
    rows, width = cots[0].shape
    hidden = activs[0].shape[1]
    chunk = 1024

    def kernel(za_ref, zb_ref, ca_ref, cb_ref, ga_ref, gb_ref, o_ref, da_ref, db_ref):
        @pl.when(pl.program_id(0) == 0)
        def _():
            da_ref[...] = (ca_ref[...].astype(f32) * ga_ref[...]).astype(bf16)
            db_ref[...] = (cb_ref[...].astype(f32) * gb_ref[...]).astype(bf16)

        o_ref[...] = (
            dot_tn(za_ref[...], da_ref[...]) + dot_tn(zb_ref[...], db_ref[...])
        ).astype(bf16)

    by_col = spec((rows, chunk), lambda i: (0, i))
    return pl.pallas_call(
        kernel,
        name="narrow_outer",
        cost_estimate=cost(12),
        grid=(hidden // chunk,),
        in_specs=[by_col, by_col] + [fixed((rows, width))] * 2 + [fixed((rows, 1))] * 2,
        out_specs=spec((chunk, width), lambda i: (i, 0)),
        out_shape=shaped((hidden, width), bf16),
        scratch_shapes=[pltpu.VMEM((rows, width), bf16)] * 2,
        compiler_params=params,
    )(*activs, *cots, *gates)


def widen_outer(rows_in, slopes, gates):
    rows, width = rows_in[0].shape
    hidden = slopes[0].shape[1]
    chunk = 1024

    def kernel(xa_ref, xb_ref, va_ref, vb_ref, ga_ref, gb_ref, o_ref, da_ref, db_ref):
        @pl.when(pl.program_id(0) == 0)
        def _():
            da_ref[...] = (xa_ref[...].astype(f32) * ga_ref[...]).astype(bf16)
            db_ref[...] = (xb_ref[...].astype(f32) * gb_ref[...]).astype(bf16)

        o_ref[...] = (
            dot_tn(da_ref[...], va_ref[...]) + dot_tn(db_ref[...], vb_ref[...])
        ).astype(bf16)

    by_col = spec((rows, chunk), lambda i: (0, i))
    return pl.pallas_call(
        kernel,
        name="widen_outer",
        cost_estimate=cost(12),
        grid=(hidden // chunk,),
        in_specs=[fixed((rows, width))] * 2 + [by_col, by_col] + [fixed((rows, 1))] * 2,
        out_specs=spec((width, chunk), lambda i: (0, i)),
        out_shape=shaped((width, hidden), bf16),
        scratch_shapes=[pltpu.VMEM((rows, width), bf16)] * 2,
        compiler_params=params,
    )(*rows_in, *slopes, *gates)


def narrow_product(activs, narrow_low):
    rows, hidden = activs[0].shape
    width = narrow_low.shape[1]

    def kernel(za_ref, zb_ref, w_ref, o_ref):
        @pl.when(pl.program_id(0) == 0)
        def _():
            o_ref[...] = dot(za_ref[...], w_ref[...]).astype(bf16)

        @pl.when(pl.program_id(0) == 1)
        def _():
            o_ref[...] = dot(zb_ref[...], w_ref[...]).astype(bf16)

    return pl.pallas_call(
        kernel,
        name="narrow_product",
        cost_estimate=cost(11),
        grid=(2,),
        in_specs=[fixed((rows, hidden)), fixed((rows, hidden)), fixed((hidden, width))],
        out_specs=by_rows(rows, width),
        out_shape=shaped((2 * rows, width), bf16),
        compiler_params=params,
    )(*activs, narrow_low)


def outer_pair(left, rights, small_parts, chunk):
    half, cols = rights[0].shape
    mine = left.shape[1]
    blocks = cols // chunk
    routers, firsts, second, third = small_parts
    experts = routers[0].shape[0]

    def kernel(l_ref, a_ref, b_ref, ra_ref, rb_ref, fa_ref, fb_ref, s_ref, t_ref, o_ref, rows_ref):
        step = pl.program_id(0)

        @pl.when(step < blocks)
        def _():
            o_ref[...] = (
                dot_tn(l_ref[:half], a_ref[...]) + dot_tn(l_ref[half:], b_ref[...])
            ).astype(bf16)

        @pl.when(step == blocks)
        def _():
            rows_ref[...] = jnp.zeros_like(rows_ref)
            rows_ref[:experts] = ra_ref[...] + rb_ref[...]
            rows_ref[experts : experts + 1] = fa_ref[...] + fb_ref[...]
            rows_ref[experts + 1 : experts + 2] = s_ref[...]
            rows_ref[experts + 2 : experts + 3] = t_ref[...]
            o_ref[:, :128] = rows_ref[...].T.astype(bf16)

    by_col = spec((half, chunk), lambda i: (0, jnp.minimum(i, blocks - 1)))
    return pl.pallas_call(
        kernel,
        name="outer_pair",
        cost_estimate=cost(10),
        grid=(blocks + 1,),
        in_specs=[fixed((2 * half, mine)), by_col, by_col]
        + [fixed((experts, mine))] * 2 + [fixed((1, mine))] * 4,
        out_specs=spec((mine, chunk), lambda i: (0, i)),
        out_shape=shaped((mine, cols + 128), bf16),
        scratch_shapes=[pltpu.VMEM((128, mine), f32)],
        compiler_params=params,
    )(left, *rights, *routers, *firsts, second, third)


def place_quarters(place, pieces):
    rows, cols = pieces[0].shape

    def kernel(place_ref, *refs):
        out_ref = refs[4]
        for k in range(4):

            @pl.when(pl.program_id(0) == k)
            def _():
                out_ref[...] = refs[k][...].astype(f32)

    return pl.pallas_call(
        kernel,
        name="place_quarters",
        cost_estimate=cost(rows * cols // 120000),
        grid_spec=pltpu.PrefetchScalarGridSpec(
            num_scalar_prefetch=1,
            grid=(4,),
            in_specs=[pl.BlockSpec((rows, cols), lambda i, p: (0, 0))] * 4,
            out_specs=pl.BlockSpec((rows, cols), lambda i, p: (p[i], 0)),
        ),
        out_shape=shaped((4 * rows, cols), f32),
        compiler_params=params,
    )(place, *pieces)


def to_slots(rows_in, slot_rows, count):
    rows, width = rows_in.shape
    block = 288

    def kernel(r_ref, s_ref, o_ref):
        base = pl.program_id(0) * block
        line = base + lax.broadcasted_iota(jnp.int32, (block, rows), 0)
        hot = (line == s_ref[0:1, :]) | (line == s_ref[1:2, :])
        o_ref[...] = dot(hot.astype(bf16), r_ref[...]).astype(bf16)

    return pl.pallas_call(
        kernel,
        name="to_slots",
        cost_estimate=cost(4),
        grid=(count // block,),
        in_specs=[fixed((rows, width)), fixed((2, rows))],
        out_specs=spec((block, width), lambda i: (i, 0)),
        out_shape=shaped((count, width), bf16),
        compiler_params=params,
    )(rows_in, slot_rows)


def product_wide(left, right_t, chunk=1024):
    rows, depth = left.shape
    cols = right_t.shape[0]

    def kernel(l_ref, r_ref, o_ref):
        o_ref[...] = dot_nt(l_ref[...], r_ref[...]).astype(bf16)

    return pl.pallas_call(
        kernel,
        name="product_wide",
        cost_estimate=cost(7),
        grid=(cols // chunk,),
        in_specs=[fixed((rows, depth)), spec((chunk, depth), lambda i: (i, 0))],
        out_specs=spec((rows, chunk), lambda i: (0, i)),
        out_shape=shaped((rows, cols), bf16),
        compiler_params=params,
    )(left, right_t)


def outer_by_right(left, right, chunk):
    rows, mine = left.shape
    cols = right.shape[1]

    def kernel(l_ref, r_ref, o_ref):
        o_ref[...] = dot_tn(l_ref[...], r_ref[...]).astype(bf16)

    return pl.pallas_call(
        kernel,
        name="outer_by_right",
        cost_estimate=cost(10),
        grid=(cols // chunk,),
        in_specs=[fixed((rows, mine)), spec((rows, chunk), lambda i: (0, i))],
        out_specs=spec((mine, chunk), lambda i: (0, i)),
        out_shape=shaped((mine, cols), bf16),
        compiler_params=params,
    )(left, right)


def outer_by_left(left, right, chunk):
    rows, mine = left.shape
    cols = right.shape[1]

    def kernel(l_ref, r_ref, o_ref):
        o_ref[...] = dot_tn(l_ref[...], r_ref[...]).astype(bf16)

    return pl.pallas_call(
        kernel,
        name="outer_by_left",
        cost_estimate=cost(10),
        grid=(mine // chunk,),
        in_specs=[spec((rows, chunk), lambda i: (0, i)), fixed((rows, cols))],
        out_specs=spec((chunk, cols), lambda i: (i, 0)),
        out_shape=shaped((mine, cols), bf16),
        compiler_params=params,
    )(left, right)


def plane_neighbours(array, by):
    return lax.ppermute(array, "rep", [(i, i ^ by) for i in range(4)])


def after(value, *others):
    return lax.optimization_barrier((value, *others))[0]


def add_low(left, right):
    return (left.astype(f32) + right.astype(f32)).astype(bf16)


class PlaneSum:
    def __init__(self, array, first):
        self.first, self.second = first, 3 - first
        rep = lax.axis_index("rep")
        self.near, self.far = lax.rem(rep // first, 2), lax.rem(rep // self.second, 2)
        self.kept, self.got = self.exchange_half(array, self.near, first)

    def exchange_half(self, whole, bit, by):
        halves = whole.reshape(2, whole.shape[0] // 2, whole.shape[1])
        kept = lax.dynamic_index_in_dim(halves, bit, 0, False)
        sent = lax.dynamic_index_in_dim(halves, 1 - bit, 0, False)
        return kept, plane_neighbours(sent, by)

    def fold(self):
        half = add_low(self.kept, self.got)
        self.kept, self.got = self.exchange_half(half, self.far, self.second)
        return half

    def spread(self):
        self.own = add_low(self.kept, self.got)
        self.beside = plane_neighbours(self.own, self.second)
        return self.own

    def cross(self):
        self.across = [plane_neighbours(p, self.first) for p in (self.own, self.beside)]
        return self.beside, self.across[0]

    def finish(self):
        across = self.across
        low, high = 2 * self.near + self.far, 2 * (1 - self.near) + self.far
        flip = 1 - 2 * self.far
        place = jnp.stack([low, low + flip, high, high + flip]).astype(jnp.int32)
        return place_quarters(place, (self.own, self.beside, *across))


class PlainSum:
    def __init__(self, array, first):
        self.total = lax.psum(array, "rep").astype(f32)

    def fold(self):
        return self.total

    spread = cross = finish = fold


def plane_sum_small(array):
    here = array.astype(f32) + plane_neighbours(array, 1).astype(f32)
    there = plane_neighbours(array, 2).astype(f32) + plane_neighbours(array, 3).astype(f32)
    return here + there


def plane_piece(shards, tail=None):
    rep = lax.axis_index("rep")
    pieces = []
    for shard in shards:
        rows, cols = shard.shape[0] // 2, shard.shape[1] // 2
        pieces.append(
            lax.dynamic_slice(shard, ((rep // 2) * rows, (rep % 2) * cols), (rows, cols))
        )
    if tail is not None:
        rows = tail.shape[0] // 2
        pieces.append(lax.dynamic_slice(tail, ((rep // 2) * rows, 0), (rows, tail.shape[1])))
    return jnp.concatenate(pieces, axis=1).astype(bf16)


def gather_line(piece):
    groups = lax.axis_size("exp") // 2
    lines = [[2 * z + c for z in range(groups)] for c in range(2)]
    return lax.all_to_all(
        jnp.broadcast_to(piece[None], (groups,) + piece.shape),
        "exp", split_axis=0, concat_axis=0, axis_index_groups=lines,
    )


def gather_plane(own):
    return own, *[plane_neighbours(own, by) for by in (1, 2, 3)]


def gather_cores(parts, layout, total):
    ranks = lax.axis_size("exp")
    mine = assemble(lax.axis_index("rep").reshape(1), parts, layout, total)
    other = lax.ppermute(mine, "exp", [(i, i ^ 1) for i in range(ranks)])
    return lax.rem(lax.axis_index("exp"), 2).reshape(1), mine, other


def gather_plain(shards):
    whole_rows = [lax.all_gather(s.astype(bf16), "exp", axis=0, tiled=True) for s in shards]
    joined = jnp.concatenate(whole_rows, axis=1)
    halves = joined.reshape(4, 2, joined.shape[0] // 8, joined.shape[1])
    return jnp.zeros((1,), jnp.int32), halves[:, 0], halves[:, 1]


def body(
    tokens, qkv_weight, out_weight, up_weight, down_weight, router_weight,
    first_gain, second_gain, third_gain, widening, narrowing, expert_ids, priority, cotangent,
):
    rows, width = tokens.shape
    hidden_width = up_weight.shape[1]
    ranks, reps = lax.axis_size("exp"), lax.axis_size("rep")
    experts = widening.shape[0] * ranks
    capacity = (rows + experts - 1) // experts
    half = capacity // 2
    count = experts * capacity
    pairs = width // 128
    me = lax.axis_index("exp").reshape(1)

    def reduce_dense(array):
        return lax.psum_scatter(array, "exp", scatter_dimension=0, tiled=True)

    plane = ranks == 8 and reps == 4

    over_rep = PlaneSum if plane else PlainSum

    choice_hot = (expert_ids[:, :, None] == jnp.arange(experts, dtype=jnp.int32)).astype(f32)
    rank_row = priority[0]
    earlier = (rank_row[None, :] < rank_row[:, None]).astype(bf16)
    ahead = dot(earlier, choice_hot.reshape(rows, -1).astype(bf16)).reshape(choice_hot.shape)
    totals = jnp.sum(choice_hot, axis=0)
    prior = jnp.cumsum(totals, axis=0) - totals
    position = jnp.sum((ahead + prior[None]) * choice_hot, axis=-1).astype(jnp.int32)
    kept = position < capacity
    slots = jnp.where(kept, expert_ids * capacity + position, -1)
    later = position >= half
    split_slots = expert_ids * half + position + jnp.where(later, experts * half - half, 0)
    split_slots = jnp.where(kept, split_slots, -1)
    slot_rows = split_slots.T

    def exchange(array, amount):
        return lax.all_to_all(
            array.reshape(experts, amount, width), "exp", split_axis=0, concat_axis=0, tiled=True
        ).reshape(experts * amount, width)

    def both_halves(rows_in):
        return [to_slots(rows_in, slot_rows - j * (count // 2), count // 2) for j in range(2)]

    narrow_low = narrowing[0].astype(bf16)
    sent_cots = both_halves(cotangent)
    small = jnp.concatenate(
        [router_weight, first_gain[:, None], second_gain[:, None], third_gain[:, None]], axis=1
    )
    small = jnp.pad(small, ((0, 0), (0, 128 - experts - 3)))
    by_pair = qkv_weight.reshape(-1, 3, pairs, 128).swapaxes(1, 2).reshape(-1, 3 * width)
    wide, deep = width // 2, hidden_width // 2
    if plane:
        own = gather_line(plane_piece((by_pair,), small))
        pieces = gather_plane(after(own, narrow_low))
        piece, piece_down = plane_piece((out_weight, up_weight)), plane_piece((down_weight,))
        tall = piece.shape[0]
        piece = piece.reshape(tall, -1, wide).swapaxes(0, 1).reshape(-1, wide)
        own_both = gather_line(after(jnp.concatenate([piece, piece_down], axis=0), own))
        own_next = own_both[:, : piece.shape[0]].reshape(ranks // 2, -1, tall, wide)
        own_next = own_next.swapaxes(1, 2).reshape(ranks // 2, tall, -1)
        own_down = own_both[:, piece.shape[0] :]
        qkv_w = gather_cores(
            after(pieces, own_both, sent_cots),
            ((0, 3 * wide, 0, 3 * wide), (3 * wide, 128, 3 * width, 0)), 3 * width + 128,
        )
        pieces = gather_plane(after(own_next, pieces))
        pieces_down = gather_plane(after(own_down, pieces))
    else:
        qkv_w = gather_plain((by_pair, small))
        out_up = gather_plain((out_weight, up_weight))
        down = gather_plain((down_weight,))

    if plane:
        sent_cots = after(sent_cots, own_down)
    cots = [exchange(c, half) for c in sent_cots]

    split = 2 * pairs // 3
    qkv, probs, attended, first_low, small_t = attention_forward(
        tokens, qkv_w, experts, 0, split, pairs, None
    )
    if plane:
        out_up = gather_cores(
            after(pieces, small_t), ((0, wide, 0, wide), (wide, deep, width, deep)),
            width + hidden_width,
        )
    gain_one = small_t[experts : experts + 1]
    gain_two = small_t[experts + 1 : experts + 2]
    gain_three = small_t[experts + 2 : experts + 3]
    router_t = small_t[:experts]
    qkv, probs, attended = attention_forward(
        first_low, qkv_w, experts, split, pairs - split, pairs, (qkv, probs, attended)
    )
    if plane:
        down = gather_cores(after(pieces_down, attended), ((0, wide, 0, wide),), width)
    hidden, second_low, activ, slope = dense_up(after(attended, cots[0]), tokens, out_up, gain_two)
    middle, third_low, gates = dense_down(activ, hidden, expert_ids, down, router_t, gain_three)

    sent_rows = both_halves(after(third_low, cots[1]))
    cot_wide = [product_wide(c, narrow_low) for c in after(cots, sent_rows[0])]
    widen_low = after(widening[0], sent_rows[0]).astype(bf16)
    arrived = [exchange(x, half) for x in sent_rows]
    mains = []
    for j in range(2):
        ready = after(arrived[j], cot_wide, widen_low, *[m[2] for m in mains])
        mains.append(expert_main(me, ready, widen_low, cot_wide[j], router_t))
    z_rows, v_rows, dx_rows, slot_gates, router_parts = zip(*mains)
    dx_slots = [exchange(dx_rows[0], half)]
    dx_slots.append(exchange(after(dx_rows[1], dx_slots[0]), half))
    narrow_grads = narrow_outer(z_rows, cots, slot_gates)
    narrow_sum = lax.psum(narrow_grads, "rep")
    y_rows = narrow_product(z_rows, narrow_low)
    y_sent = y_rows.reshape(2, experts, half, width).swapaxes(0, 1)
    y_slots = exchange(after(y_sent, dx_slots), capacity)

    dy, dzl, third_part = norm_three_backward(
        after(dx_slots, narrow_grads, y_rows), split_slots, gates, cotangent, middle, gain_three
    )
    down_grads = outer_by_left(activ, dzl, 1024)
    down_shard = reduce_dense(down_grads)
    widen_grads = widen_outer(after(arrived, down_grads), v_rows, slot_gates)
    order = list(range(reps))
    widen_sum = lax.psum(widen_grads, "rep", axis_index_groups=[order[:2] + order[:1:-1]])
    du, dh, dhl, second_part = dense_backward(
        after(dzl, widen_grads), dy, slope, hidden, out_up, down, gain_two
    )
    up_grads = outer_by_right(after(second_low, y_slots), du, 1024)
    up_shard = reduce_dense(up_grads)
    out_grads = outer_by_right(after(attended, up_grads), dhl, 768)
    out_shard = reduce_dense(out_grads)
    dh = after(dh, out_grads)
    halves = []
    for image in range(2):
        halves.append(attention_backward(
            image, dh, out_up, qkv, probs, attended, tokens, qkv_w, gain_one
        ))
        dh = after(dh, halves[0], narrow_sum, down_shard)
    dqkv, token_grads, first_parts = zip(*halves)
    token_grads = jnp.concatenate(token_grads, axis=0)
    qkv_grads = outer_pair(
        first_low, dqkv, (router_parts, first_parts, second_part, third_part), 384
    )
    qkv_shard = reduce_dense(qkv_grads)
    output = combine(after(y_slots, qkv_grads), slots, gates, middle)

    joined = jnp.concatenate(
        [down_shard, up_shard.reshape(-1, width), out_shard], axis=0
    )
    joined = over_rep(after(joined, qkv_grads), 1)
    joined.fold()
    joined.spread()
    joined.cross()
    joined = joined.finish()
    down_sum, up_sum, out_sum = jnp.split(
        joined, [down_weight.shape[0], joined.shape[0] - out_weight.shape[0]], axis=0
    )
    up_sum = up_sum.reshape(up_weight.shape)
    qkv_shard = after(qkv_shard, widen_sum, output, joined)
    qkv_sum = plane_sum_small(qkv_shard) if plane else over_rep(qkv_shard, 1).finish()
    small_sum = qkv_sum[:, 3 * width :]
    qkv_sum = qkv_sum[:, : 3 * width].reshape(-1, pairs, 3, 128).swapaxes(1, 2)
    qkv_sum = qkv_sum.reshape(-1, 3 * width)
    return (
        output, token_grads,
        qkv_sum, out_sum, up_sum, down_sum,
        small_sum[:, :experts], small_sum[:, experts], small_sum[:, experts + 1],
        small_sum[:, experts + 2],
        after(widen_sum, joined).astype(f32)[None], narrow_sum.astype(f32)[None],
    )


def solution(mesh):
    rows_spec, exp_spec = P(("rep", "exp"), None), P("exp", None)
    return jax.shard_map(
        body,
        mesh=mesh,
        in_specs=(
            rows_spec, exp_spec, exp_spec, exp_spec, exp_spec, exp_spec,
            P("exp"), P("exp"), P("exp"), P("exp", None, None), P("exp", None, None),
            rows_spec, rows_spec, rows_spec,
        ),
        out_specs=(
            rows_spec, rows_spec, exp_spec, exp_spec, exp_spec, exp_spec, exp_spec,
            P("exp"), P("exp"), P("exp"), P("exp", None, None), P("exp", None, None),
        ),
        check_vma=False,
    )
```

```python
import jax
import jax.numpy as jnp
from jax import lax
from jax.experimental import pallas as pl
from jax.experimental.pallas import tpu as pltpu
from jax.sharding import PartitionSpec as P

PATCHES = 576
HEAD_DIM = 64
EPSILON = 1e-6
LOG2E = 1.4426950408889634
ROOT_HALF = 0.7071067811865476
INV_ROOT_2PI = 0.3989422804014327
bf16 = jnp.bfloat16
f32 = jnp.float32
params = pltpu.CompilerParams(vmem_limit_bytes=58 << 20)


def dot(left, right):
    return jnp.dot(left, right, preferred_element_type=f32)


def dot_nt(left, right):
    return lax.dot_general(left, right, (((1,), (1,)), ((), ())), preferred_element_type=f32)


def dot_tn(left, right):
    return lax.dot_general(left, right, (((0,), (0,)), ((), ())), preferred_element_type=f32)


def unit_norm(values):
    centred = values - jnp.mean(values, axis=-1, keepdims=True)
    inverse = lax.rsqrt(jnp.mean(centred * centred, axis=-1, keepdims=True) + EPSILON)
    return centred * inverse, inverse


def norm_inward(upstream, unit, inverse, gain):
    scaled = upstream * gain
    return inverse * (
        scaled
        - jnp.mean(scaled, axis=-1, keepdims=True)
        - unit * jnp.mean(scaled * unit, axis=-1, keepdims=True)
    )


def gelu_pair(u):
    half = 0.5 + 0.5 * lax.erf(u * ROOT_HALF)
    density = jnp.exp2(u * u * (-0.5 * LOG2E)) * INV_ROOT_2PI
    return u * half, half + u * density


def cost(microseconds):
    return pl.CostEstimate(
        flops=int(microseconds * 8e+08), bytes_accessed=int(microseconds * 2e+06), transcendentals=0
    )


def spec(shape, index):
    return pl.BlockSpec(shape, index)


def fixed(shape):
    zeros = (0,) * len(shape)
    return pl.BlockSpec(shape, lambda *_: zeros, pipeline_mode=pl.Buffered(1))


def shaped(shape, dtype):
    return jax.ShapeDtypeStruct(shape, dtype)


any_space = pl.BlockSpec(memory_space=pl.ANY)
scalar_space = pl.BlockSpec(memory_space=pltpu.SMEM)


def attention_forward(rows_in, weight, small, first_pair, pairs, pairs_all, earlier):
    rows, width = rows_in.shape
    images, first = rows // PATCHES, earlier is None
    cols = 384 * pairs

    def kernel(*refs):
        if first:
            (core_ref, x_ref, hw_ref, kw_ref, qkv_ref, p_ref, o_ref, a_ref, st_ref,
             w_ref, sem, sm_ref, sem_small) = refs
        else:
            (core_ref, a_ref, hw_ref, kw_ref, _, _, _, qkv_ref, p_ref, o_ref, w_ref, sem) = refs
        image, pair = pl.program_id(0), pl.program_id(1)

        @pl.when((pair == 0) & (image == 0))
        def _():
            load_halves(core_ref[0], hw_ref, kw_ref, w_ref, sem, 384 * first_pair, cols)
            if first:
                load_halves(core_ref[0], hw_ref, kw_ref, sm_ref, sem_small, 3 * width, 128)
                st_ref[...] = sm_ref[...].astype(f32).T

        if first:
            @pl.when(pair == 0)
            def _():
                unit, _ = unit_norm(x_ref[...].astype(f32))
                a_ref[...] = (unit * st_ref[small : small + 1, :]).astype(bf16)

        qkv = dot(a_ref[...], w_ref[:, pl.ds(pl.multiple_of(pair * 384, 128), 384)]).astype(bf16)
        qkv_ref[...] = qkv
        q, k, v = qkv[:, :128], qkv[:, 128:256], qkv[:, 256:]
        q = (q.astype(f32) * HEAD_DIM ** (-0.5)).astype(bf16)
        low_lane = lax.broadcasted_iota(jnp.int32, (PATCHES, 128), 1) < HEAD_DIM
        v_t = v.T
        outs = []
        for h in range(2):
            k_head = jnp.where(low_lane == (h == 0), k, jnp.zeros_like(k))
            s = dot_nt(k_head, q)
            top = jnp.max(s, axis=0, keepdims=True)
            e = jnp.exp2((s - top) * LOG2E)
            total = jnp.sum(e, axis=0, keepdims=True)
            p = (e * (1.0 / total)).astype(bf16)
            p_ref[0, h] = p
            outs.append(dot(v_t[h * HEAD_DIM : (h + 1) * HEAD_DIM], p))
        o_ref[...] = jnp.concatenate(outs, axis=0).T.astype(bf16)

    groups = weight[1].shape[0]
    by_image = spec((PATCHES, width), lambda i, j: (i, 0))
    out_specs = [
        spec((PATCHES, 384), lambda i, j: (i, j + first_pair)),
        spec((1, 2, PATCHES, PATCHES), lambda i, j: (i, j + first_pair, 0, 0)),
        spec((PATCHES, 128), lambda i, j: (i, j + first_pair)),
    ]
    out_shape = [
        shaped((rows, 384 * pairs_all), bf16),
        shaped((images, 2 * pairs_all, PATCHES, PATCHES), bf16),
        shaped((rows, 128 * pairs_all), bf16),
    ]
    in_specs = [scalar_space, by_image, any_space, any_space]
    scratch = [pltpu.VMEM((width, cols), bf16), pltpu.SemaphoreType.DMA((2, groups))]
    if first:
        out_specs += [by_image, spec((128, width), lambda i, j: (0, 0))]
        out_shape += [shaped((rows, width), bf16), shaped((128, width), f32)]
        scratch += [pltpu.VMEM((width, 128), bf16), pltpu.SemaphoreType.DMA((2, groups))]
        operands, aliases = (weight[0], rows_in, *weight[1:]), {}
    else:
        in_specs += [any_space] * 3
        operands, aliases = (weight[0], rows_in, *weight[1:], *earlier), {4: 0, 5: 1, 6: 2}
    return pl.pallas_call(
        kernel,
        name="attention_forward",
        cost_estimate=cost(8 * images * pairs // 4),
        grid=(images, pairs),
        in_specs=in_specs,
        out_specs=out_specs,
        out_shape=out_shape,
        scratch_shapes=scratch,
        input_output_aliases=aliases,
        compiler_params=params,
    )(*operands)


def attention_backward(image, dh, out_weight, qkv, probs, attended, tokens, qkv_weight, gain):
    width = dh.shape[1]
    pairs = width // 128

    def kernel(
        core_ref, dh_ref, ho_ref, ko_ref, qkv_ref, p_ref, o_ref, x_ref, hw_ref, kw_ref, g_ref,
        dq_ref, dx_ref, dg_ref, do_ref, db_ref, wo_ref, w_ref, sem, sem_w,
    ):
        pair = pl.program_id(0)

        @pl.when(pair == 0)
        def _():
            load_halves(core_ref[0], ho_ref, ko_ref, wo_ref, sem, 0, width)
            load_halves(core_ref[0], hw_ref, kw_ref, w_ref, sem_w, 0, 3 * width)

        @pl.when(pair == 0)
        def _():
            do = dot_nt(dh_ref[...], wo_ref[...]).astype(bf16)
            for j in range(pairs):
                do_ref[j] = do[:, j * 128 : (j + 1) * 128]

        q, k, v = qkv_ref[:, :128], qkv_ref[:, 128:256], qkv_ref[:, 256:]
        q = (q.astype(f32) * HEAD_DIM ** (-0.5)).astype(bf16)
        do = do_ref[pair]
        low_lane = lax.broadcasted_iota(jnp.int32, (PATCHES, 128), 1) < HEAD_DIM
        prod = do.astype(f32) * o_ref[...].astype(f32)
        prod_high = prod.astype(bf16)
        prod_low = (prod - prod_high.astype(f32)).astype(bf16)
        pick_row = lax.broadcasted_iota(jnp.int32, (16, 128), 0)
        pick_lane = lax.broadcasted_iota(jnp.int32, (16, 128), 1)
        pick = (pick_lane // HEAD_DIM == pick_row).astype(bf16)
        row_sums = dot_nt(pick, prod_high) + dot_nt(pick, prod_low)
        k_t = k.T
        dqs, dks, dvs = [], [], []
        for h in range(2):
            v_head = jnp.where(low_lane == (h == 0), v, jnp.zeros_like(v))
            dp = dot_nt(v_head, do)
            p = p_ref[0, h]
            ds = (p.astype(f32) * (dp - row_sums[h : h + 1])).astype(bf16)
            dvs.append(dot(p, do))
            dks.append(dot(ds, q))
            dqs.append(dot(k_t[h * HEAD_DIM : (h + 1) * HEAD_DIM], ds))
        dq = (jnp.concatenate(dqs, axis=0) * HEAD_DIM ** (-0.5)).T
        dqkv = jnp.concatenate(
            [dq, jnp.where(low_lane, dks[0], dks[1]), jnp.where(low_lane, dvs[0], dvs[1])], axis=1
        ).astype(bf16)
        dq_ref[...] = dqkv

        w_pair = w_ref[:, pl.ds(pl.multiple_of(pair * 384, 128), 384)]

        @pl.when(pair == 0)
        def _():
            db_ref[...] = dot_nt(dqkv, w_pair)

        @pl.when(pair > 0)
        def _():
            db_ref[...] += dot_nt(dqkv, w_pair)

        @pl.when(pair == pairs - 1)
        def _():
            upstream = db_ref[...]
            unit, inverse = unit_norm(x_ref[...].astype(f32))
            inward = norm_inward(upstream, unit, inverse, g_ref[gain[1] : gain[1] + 1, :])
            dx_ref[...] = (dh_ref[...].astype(f32) + inward).astype(bf16)
            dg_ref[...] = jnp.sum(upstream * unit, axis=0, keepdims=True)

    by_image = spec((PATCHES, width), lambda j: (image, 0))
    out_image = spec((PATCHES, width), lambda j: (0, 0))
    return pl.pallas_call(
        kernel,
        name="attention_backward",
        cost_estimate=cost(1000),
        grid=(pairs,),
        in_specs=[
            scalar_space, by_image, any_space, any_space,
            spec((PATCHES, 384), lambda j: (image, j)),
            spec((1, 2, PATCHES, PATCHES), lambda j: (image, j, 0, 0)),
            spec((PATCHES, 128), lambda j: (image, j)),
            by_image,
            any_space, any_space,
            fixed(gain[0].shape),
        ],
        out_specs=[
            spec((PATCHES, 384), lambda j: (0, j)), out_image,
            spec((1, width), lambda j: (0, 0)),
        ],
        out_shape=[
            shaped((PATCHES, 3 * width), bf16), shaped((PATCHES, width), bf16),
            shaped((1, width), f32),
        ],
        scratch_shapes=[
            pltpu.VMEM((pairs, PATCHES, 128), bf16),
            pltpu.VMEM((PATCHES, width), f32),
            pltpu.VMEM((width, width), bf16),
            pltpu.VMEM((width, 3 * width), bf16),
            pltpu.SemaphoreType.DMA((2, out_weight[1].shape[0])),
            pltpu.SemaphoreType.DMA((2, out_weight[1].shape[0])),
        ],
        compiler_params=params,
    )(out_weight[0], dh, *out_weight[1:], qkv, probs, attended, tokens, *qkv_weight[1:], gain[0])


def load_halves(core, mine_ref, other_ref, whole_ref, sem, start, cols):
    groups, rows, _ = mine_ref.shape
    copies = []
    for z in range(groups):
        for side, ref in enumerate((mine_ref, other_ref)):
            place = core if side == 0 else 1 - core
            base = pl.multiple_of((2 * z + place) * rows, 16)
            copies.append(
                pltpu.make_async_copy(
                    ref.at[z, :, pl.ds(start, cols)],
                    whole_ref.at[pl.ds(base, rows), :],
                    sem.at[side, z],
                )
            )
    for copy in copies:
        copy.start()
    for copy in copies:
        copy.wait()


def assemble(place, parts, layout, total):
    groups, rows, _ = parts[0].shape

    def kernel(r_ref, own_ref, x_ref, y_ref, far_ref, o_ref):
        down, right = r_ref[0] // 2, r_ref[0] % 2

        def put(ref, row_half, col_half):
            at = pl.multiple_of(row_half * rows, 16)
            for start, wide, base, step in layout:
                to = pl.multiple_of(base + col_half * step, 128)
                o_ref[:, pl.ds(at, rows), pl.ds(to, wide)] = ref[:, :, start : start + wide]

        put(own_ref, down, right)
        put(x_ref, down, 1 - right)
        put(y_ref, 1 - down, right)
        put(far_ref, 1 - down, 1 - right)

    return pl.pallas_call(
        kernel,
        name="assemble",
        cost_estimate=cost(4),
        in_specs=[scalar_space] + [pl.BlockSpec(memory_space=pltpu.VMEM)] * 4,
        out_specs=pl.BlockSpec(memory_space=pltpu.VMEM),
        out_shape=shaped((groups, 2 * rows, total), bf16),
        compiler_params=params,
    )(place, *parts)


def by_rows(block, cols):
    return spec((block, cols), lambda i: (i, 0))


def whole(shape):
    return spec(shape, lambda i: (0,) * len(shape))


def dense_up(attended, tokens, weights, gain, extra):
    rows, width = tokens.shape
    hidden = weights[1].shape[2] - width
    block, chunk = 288, 512
    tall, wide = extra.shape
    tall = tall * block // rows

    def kernel(
        core_ref, o_ref, x_ref, hw_ref, kw_ref, g_ref, e_ref,
        h_ref, b_ref, z_ref, s_ref, low_ref, w_ref, sem,
    ):
        @pl.when(pl.program_id(0) == 0)
        def _():
            load_halves(core_ref[0], hw_ref, kw_ref, w_ref, sem, 0, width + hidden)

        low_ref[...] = e_ref[...].astype(bf16)
        h = x_ref[...].astype(f32) + dot(o_ref[...], w_ref[:, :width])
        h = h.astype(bf16)
        h_ref[...] = h
        h = h.astype(f32)
        b = (unit_norm(h)[0] * g_ref[gain[1] : gain[1] + 1, :]).astype(bf16)
        b_ref[...] = b
        ahead = dot(b, w_ref[:, width : width + chunk])
        for c in range(0, hidden, chunk):
            u = ahead
            if c + chunk < hidden:
                ahead = dot(b, w_ref[:, width + c + chunk : width + c + 2 * chunk])
            z, slope = gelu_pair(u)
            z_ref[:, c : c + chunk] = z.astype(bf16)
            s_ref[:, c : c + chunk] = slope.astype(bf16)

    return pl.pallas_call(
        kernel,
        name="dense_up",
        cost_estimate=cost(18),
        grid=(rows // block,),
        in_specs=[
            scalar_space, by_rows(block, width), by_rows(block, width), any_space, any_space,
            fixed(gain[0].shape), by_rows(tall, wide),
        ],
        out_specs=[
            by_rows(block, width), by_rows(block, width), by_rows(block, hidden),
            by_rows(block, hidden), by_rows(tall, wide),
        ],
        out_shape=[
            shaped((rows, width), bf16), shaped((rows, width), bf16),
            shaped((rows, hidden), bf16), shaped((rows, hidden), bf16),
            shaped(extra.shape, bf16),
        ],
        scratch_shapes=[
            pltpu.VMEM((width, width + hidden), bf16),
            pltpu.SemaphoreType.DMA((2, weights[1].shape[0])),
        ],
        compiler_params=params,
    )(weights[0], attended, tokens, *weights[1:], gain[0], extra)


def dense_down(activ, hidden_rows, ids, weights, experts, gain):
    rows, width = hidden_rows.shape
    hidden = activ.shape[1]
    block = 288

    def kernel(
        core_ref, z_ref, h_ref, id_ref, hw_ref, kw_ref, g_ref,
        y_ref, m_ref, gate_ref, w_ref, sem,
    ):
        @pl.when(pl.program_id(0) == 0)
        def _():
            load_halves(core_ref[0], hw_ref, kw_ref, w_ref, sem, 0, width)

        y = h_ref[...].astype(f32) + dot(z_ref[...], w_ref[...])
        y_ref[...] = y.astype(bf16)
        m = (unit_norm(y)[0] * g_ref[gain[1] : gain[1] + 1, :]).astype(bf16)
        m_ref[...] = m
        logits = dot_nt(g_ref[:experts, :].astype(bf16), m)
        e = jnp.exp(logits - jnp.max(logits, axis=0, keepdims=True))
        p = e / jnp.sum(e, axis=0, keepdims=True)
        line = lax.broadcasted_iota(jnp.int32, (experts, block), 0)
        for k in range(2):
            hot = line == id_ref[0, k : k + 1, :]
            gate_ref[0, k : k + 1, :] = jnp.sum(jnp.where(hot, p, 0.0), axis=0, keepdims=True)

    return pl.pallas_call(
        kernel,
        name="dense_down",
        cost_estimate=cost(15),
        grid=(rows // block,),
        in_specs=[
            scalar_space, by_rows(block, hidden), by_rows(block, width),
            spec((1, 2, block), lambda i: (i, 0, 0)),
            any_space, any_space, fixed(gain[0].shape),
        ],
        out_specs=[
            by_rows(block, width), by_rows(block, width),
            spec((1, 2, block), lambda i: (i, 0, 0)),
        ],
        out_shape=[
            shaped((rows, width), bf16), shaped((rows, width), bf16),
            shaped((rows // block, 2, block), f32),
        ],
        scratch_shapes=[
            pltpu.VMEM((hidden, width), bf16),
            pltpu.SemaphoreType.DMA((2, weights[1].shape[0])),
        ],
        compiler_params=params,
    )(weights[0], activ, hidden_rows, ids, *weights[1:], gain[0])


def gated_rows(slot_ref, gate_ref, slots_refs, block):
    total, base = None, 0
    for ref in slots_refs:
        count = ref.shape[0]
        lane = base + lax.broadcasted_iota(jnp.int32, (block, count), 1)
        weighted = jnp.zeros((block, count), f32)
        for k in range(2):
            hot = lane == slot_ref[:, k : k + 1]
            weighted = weighted + jnp.where(hot, gate_ref[:, k : k + 1], 0.0)
        part = dot(weighted.astype(bf16), ref[...])
        total = part if total is None else total + part
        base += count
    return total


def norm_three_backward(dx_slots, slots, gates, cotangent, middle, gain):
    rows, width = cotangent.shape
    block = 288

    def kernel(da_ref, db_ref, slot_ref, gate_ref, cot_ref, y_ref, g_ref, dzl_ref, dg_ref):
        dm = gated_rows(slot_ref, gate_ref, (da_ref, db_ref), block)
        unit, inverse = unit_norm(y_ref[...].astype(f32))
        part = jnp.sum(dm * unit, axis=0, keepdims=True)
        dy = cot_ref[...].astype(f32) + norm_inward(dm, unit, inverse, g_ref[gain[1] : gain[1] + 1, :])
        dzl_ref[...] = dy.astype(bf16)
        first = pl.program_id(0) == 0

        @pl.when(first)
        def _():
            dg_ref[...] = part

        @pl.when(jnp.logical_not(first))
        def _():
            dg_ref[...] += part

    return pl.pallas_call(
        kernel,
        name="norm_three_backward",
        cost_estimate=cost(10),
        grid=(rows // block,),
        in_specs=[
            fixed(dx_slots[0].shape), fixed(dx_slots[1].shape), by_rows(block, 2),
            by_rows(block, 2), by_rows(block, width), by_rows(block, width), fixed(gain[0].shape),
        ],
        out_specs=[by_rows(block, width), whole((1, width))],
        out_shape=[shaped((rows, width), bf16), shaped((1, width), f32)],
        compiler_params=params,
    )(*dx_slots, slots, gates, cotangent, middle, gain[0])


def dense_backward(dzl, slope, hidden_rows, up_weight, down_weight, gain):
    rows, width = dzl.shape
    hidden = slope.shape[1]
    block, chunk = 288, 512

    def kernel(
        core_ref, dzl_ref, s_ref, h_ref, hu_ref, ku_ref, hd_ref, kd_ref, g_ref,
        du_ref, dhl_ref, dg_ref, w1_ref, w2_ref, sem,
    ):
        first = pl.program_id(0) == 0

        @pl.when(first)
        def _():
            load_halves(core_ref[0], hd_ref, kd_ref, w2_ref, sem, 0, width)
            load_halves(core_ref[0], hu_ref, ku_ref, w1_ref, sem, width, hidden)

        dzl = dzl_ref[...]
        db = jnp.zeros((block, width), f32)
        ahead = dot_nt(dzl, w2_ref[:chunk, :])
        for c in range(0, hidden, chunk):
            dz = ahead
            if c + chunk < hidden:
                ahead = dot_nt(dzl, w2_ref[c + chunk : c + 2 * chunk, :])
            du = (dz * s_ref[:, c : c + chunk].astype(f32)).astype(bf16)
            du_ref[:, c : c + chunk] = du
            db = db + dot_nt(du, w1_ref[:, c : c + chunk])
        unit, inverse = unit_norm(h_ref[...].astype(f32))
        part = jnp.sum(db * unit, axis=0, keepdims=True)
        dh = dzl.astype(f32) + norm_inward(db, unit, inverse, g_ref[gain[1] : gain[1] + 1, :])
        dhl_ref[...] = dh.astype(bf16)

        @pl.when(first)
        def _():
            dg_ref[...] = part

        @pl.when(jnp.logical_not(first))
        def _():
            dg_ref[...] += part

    return pl.pallas_call(
        kernel,
        name="dense_backward",
        cost_estimate=cost(24),
        grid=(rows // block,),
        in_specs=[
            scalar_space, by_rows(block, width), by_rows(block, hidden),
            by_rows(block, width), any_space, any_space, any_space, any_space, fixed(gain[0].shape),
        ],
        out_specs=[
            by_rows(block, hidden), by_rows(block, width), whole((1, width)),
        ],
        out_shape=[
            shaped((rows, hidden), bf16), shaped((rows, width), bf16), shaped((1, width), f32),
        ],
        scratch_shapes=[
            pltpu.VMEM((width, hidden), bf16), pltpu.VMEM((hidden, width), bf16),
            pltpu.SemaphoreType.DMA((2, up_weight[1].shape[0])),
        ],
        compiler_params=params,
    )(up_weight[0], dzl, slope, hidden_rows, *up_weight[1:], *down_weight[1:], gain[0])


def combine(y_slots, slots, gates, middle):
    rows, width = middle.shape
    block = 288

    def kernel(ya_ref, slot_ref, gate_ref, y_ref, o_ref):
        o_ref[...] = (
            y_ref[...].astype(f32) + gated_rows(slot_ref, gate_ref, (ya_ref,), block)
        ).astype(bf16)

    return pl.pallas_call(
        kernel,
        name="combine",
        cost_estimate=cost(8),
        grid=(rows // block,),
        in_specs=[
            fixed(y_slots.shape), by_rows(block, 2), by_rows(block, 2), by_rows(block, width),
        ],
        out_specs=by_rows(block, width),
        out_shape=shaped((rows, width), bf16),
        compiler_params=params,
    )(y_slots, slots, gates, middle)


def expert_main(me, rows_in, widen_low, cot_wide, small_t, experts):
    rows, width = rows_in.shape
    hidden = widen_low.shape[1]
    chunk, part = 1024, 512
    steps = hidden // chunk

    def kernel(
        me_ref, x_ref, a_ref, u_ref, wr_ref,
        z_ref, v_ref, dx_ref, gate_ref, dwr_ref, acc_ref, dg_ref,
    ):
        step = pl.program_id(0)

        @pl.when(step == 0)
        def _():
            acc_ref[...] = jnp.zeros_like(acc_ref)
            dg_ref[...] = jnp.zeros_like(dg_ref)

        x = x_ref[...]
        ahead = dot(x, a_ref[:, :part])
        sums = jnp.zeros((rows, 128), f32)
        for c in range(0, chunk, part):
            cols = slice(c, c + part)
            r = ahead
            if c + part < chunk:
                ahead = dot(x, a_ref[:, c + part : c + 2 * part])
            z, slope = gelu_pair(r)
            u = u_ref[:, cols].astype(f32)
            v = (u * slope).astype(bf16)
            z_ref[:, cols] = z.astype(bf16)
            v_ref[:, cols] = v
            dg = u * z
            sums = sums + sum(dg[:, q : q + 128] for q in range(0, part, 128))
            acc_ref[...] += dot_nt(v, a_ref[:, cols])
        dg_ref[...] += sums

        @pl.when(step == steps - 1)
        def _():
            wr = wr_ref[:experts, :].astype(bf16)
            logits = dot_nt(wr, x)
            e = jnp.exp(logits - jnp.max(logits, axis=0, keepdims=True))
            p = e / jnp.sum(e, axis=0, keepdims=True)
            own = lax.broadcasted_iota(jnp.int32, (experts, rows), 0) == me_ref[0]
            gate = jnp.sum(jnp.where(own, p, 0.0), axis=0, keepdims=True)
            gate_ref[...] = jnp.broadcast_to(gate, (128, rows)).T[:, :1]
            dgate = jnp.sum(dg_ref[...].T, axis=0, keepdims=True)
            spread = dgate * (own.astype(f32) - p)
            dx_ref[...] = (acc_ref[...] + dot_tn(spread.astype(bf16), wr)).astype(bf16)
            dwr_ref[...] = dot((gate * spread).astype(bf16), x)

    by_col = spec((rows, chunk), lambda i: (0, i))
    return pl.pallas_call(
        kernel,
        name="expert_main",
        cost_estimate=cost(15),
        grid=(steps,),
        in_specs=[
            scalar_space, fixed((rows, width)), spec((width, chunk), lambda i: (0, i)), by_col,
            fixed(small_t.shape),
        ],
        out_specs=[by_col, by_col, whole((rows, width)), whole((rows, 1)), whole((experts, width))],
        out_shape=[
            shaped((rows, hidden), bf16), shaped((rows, hidden), bf16),
            shaped((rows, width), bf16), shaped((rows, 1), f32), shaped((experts, width), f32),
        ],
        scratch_shapes=[pltpu.VMEM((rows, width), f32), pltpu.VMEM((rows, 128), f32)],
        compiler_params=params,
    )(me, rows_in, widen_low, cot_wide, small_t)


def narrow_outer(activs, cots, gates):
    rows, width = cots[0].shape
    hidden = activs[0].shape[1]
    chunk = 1024

    def kernel(za_ref, zb_ref, ca_ref, cb_ref, ga_ref, gb_ref, o_ref, da_ref, db_ref):
        @pl.when(pl.program_id(0) == 0)
        def _():
            da_ref[...] = (ca_ref[...].astype(f32) * ga_ref[...]).astype(bf16)
            db_ref[...] = (cb_ref[...].astype(f32) * gb_ref[...]).astype(bf16)

        o_ref[...] = (
            dot_tn(za_ref[...], da_ref[...]) + dot_tn(zb_ref[...], db_ref[...])
        ).astype(bf16)

    by_col = spec((rows, chunk), lambda i: (0, i))
    return pl.pallas_call(
        kernel,
        name="narrow_outer",
        cost_estimate=cost(12),
        grid=(hidden // chunk,),
        in_specs=[by_col, by_col] + [fixed((rows, width))] * 2 + [fixed((rows, 1))] * 2,
        out_specs=spec((chunk, width), lambda i: (i, 0)),
        out_shape=shaped((hidden, width), bf16),
        scratch_shapes=[pltpu.VMEM((rows, width), bf16)] * 2,
        compiler_params=params,
    )(*activs, *cots, *gates)


def widen_outer(rows_in, slopes, gates):
    rows, width = rows_in[0].shape
    hidden = slopes[0].shape[1]
    chunk = 1024

    def kernel(xa_ref, xb_ref, va_ref, vb_ref, ga_ref, gb_ref, o_ref, da_ref, db_ref):
        @pl.when(pl.program_id(0) == 0)
        def _():
            da_ref[...] = (xa_ref[...].astype(f32) * ga_ref[...]).astype(bf16)
            db_ref[...] = (xb_ref[...].astype(f32) * gb_ref[...]).astype(bf16)

        o_ref[...] = (
            dot_tn(da_ref[...], va_ref[...]) + dot_tn(db_ref[...], vb_ref[...])
        ).astype(bf16)

    by_col = spec((rows, chunk), lambda i: (0, i))
    return pl.pallas_call(
        kernel,
        name="widen_outer",
        cost_estimate=cost(12),
        grid=(hidden // chunk,),
        in_specs=[fixed((rows, width))] * 2 + [by_col, by_col] + [fixed((rows, 1))] * 2,
        out_specs=spec((width, chunk), lambda i: (0, i)),
        out_shape=shaped((width, hidden), bf16),
        scratch_shapes=[pltpu.VMEM((rows, width), bf16)] * 2,
        compiler_params=params,
    )(*rows_in, *slopes, *gates)


def narrow_product(activ, narrow_low):
    rows, hidden = activ.shape
    width = narrow_low.shape[1]
    block = rows // 2

    def kernel(z_ref, w_ref, o_ref):
        o_ref[...] = dot(z_ref[...], w_ref[...]).astype(bf16)

    return pl.pallas_call(
        kernel,
        name="narrow_product",
        cost_estimate=cost(6),
        grid=(2,),
        in_specs=[by_rows(block, hidden), fixed((hidden, width))],
        out_specs=by_rows(block, width),
        out_shape=shaped((rows, width), bf16),
        compiler_params=params,
    )(activ, narrow_low)


def outer_pair(left, rights, small_parts, chunk):
    half, cols = rights[0].shape
    mine = left.shape[1]
    blocks = cols // chunk
    routers, firsts, second, third = small_parts
    experts = routers[0].shape[0]

    def kernel(l_ref, a_ref, b_ref, ra_ref, rb_ref, fa_ref, fb_ref, s_ref, t_ref, o_ref, rows_ref):
        step = pl.program_id(0)

        @pl.when(step < blocks)
        def _():
            o_ref[...] = (
                dot_tn(l_ref[:half], a_ref[...]) + dot_tn(l_ref[half:], b_ref[...])
            ).astype(bf16)

        @pl.when(step == blocks)
        def _():
            rows_ref[...] = jnp.zeros_like(rows_ref)
            rows_ref[:experts] = ra_ref[...] + rb_ref[...]
            rows_ref[experts : experts + 1] = fa_ref[...] + fb_ref[...]
            rows_ref[experts + 1 : experts + 2] = s_ref[...]
            rows_ref[experts + 2 : experts + 3] = t_ref[...]
            o_ref[:, :128] = rows_ref[...].T.astype(bf16)

    by_col = spec((half, chunk), lambda i: (0, jnp.minimum(i, blocks - 1)))
    return pl.pallas_call(
        kernel,
        name="outer_pair",
        cost_estimate=cost(10),
        grid=(blocks + 1,),
        in_specs=[fixed((2 * half, mine)), by_col, by_col]
        + [fixed((experts, mine))] * 2 + [fixed((1, mine))] * 4,
        out_specs=spec((mine, chunk), lambda i: (0, i)),
        out_shape=shaped((mine, cols + 128), bf16),
        scratch_shapes=[pltpu.VMEM((128, mine), f32)],
        compiler_params=params,
    )(left, *rights, *routers, *firsts, second, third)


def place_pieces(place, pieces):
    rows, cols = pieces[0].shape
    amount = len(pieces)

    def kernel(place_ref, *refs):
        for k in range(amount):

            @pl.when(pl.program_id(0) == k)
            def _():
                refs[amount][...] = refs[k][...].astype(f32)

    return pl.pallas_call(
        kernel,
        name="place_pieces",
        cost_estimate=cost(amount * rows * cols // 480000),
        grid_spec=pltpu.PrefetchScalarGridSpec(
            num_scalar_prefetch=1,
            grid=(amount,),
            in_specs=[pl.BlockSpec((rows, cols), lambda i, p: (0, 0))] * amount,
            out_specs=pl.BlockSpec((rows, cols), lambda i, p: (p[i], 0)),
        ),
        out_shape=shaped((amount * rows, cols), f32),
        compiler_params=params,
    )(place, *pieces)


def to_slots_cast(rows_in, slot_rows, count, weight):
    rows, width = rows_in.shape
    block = 288
    steps = count // block
    tall, wide = weight.shape

    def kernel(r_ref, s_ref, w_ref, o_ref, low_ref):
        base = pl.program_id(0) * block
        line = base + lax.broadcasted_iota(jnp.int32, (block, rows), 0)
        hot = (line == s_ref[0:1, :]) | (line == s_ref[1:2, :])
        o_ref[...] = dot(hot.astype(bf16), r_ref[...]).astype(bf16)
        low_ref[...] = w_ref[...].astype(bf16)

    return pl.pallas_call(
        kernel,
        name="to_slots_cast",
        cost_estimate=cost(20),
        grid=(steps,),
        in_specs=[fixed((rows, width)), fixed((2, rows)), by_rows(tall // steps, wide)],
        out_specs=[by_rows(block, width), by_rows(tall // steps, wide)],
        out_shape=[shaped((count, width), bf16), shaped((tall, wide), bf16)],
        compiler_params=params,
    )(rows_in, slot_rows, weight)


def to_slots(rows_in, slot_rows, count):
    rows, width = rows_in.shape
    block = 288

    def kernel(r_ref, s_ref, o_ref):
        base = pl.program_id(0) * block
        line = base + lax.broadcasted_iota(jnp.int32, (block, rows), 0)
        hot = (line == s_ref[0:1, :]) | (line == s_ref[1:2, :])
        o_ref[...] = dot(hot.astype(bf16), r_ref[...]).astype(bf16)

    return pl.pallas_call(
        kernel,
        name="to_slots",
        cost_estimate=cost(4),
        grid=(count // block,),
        in_specs=[fixed((rows, width)), fixed((2, rows))],
        out_specs=spec((block, width), lambda i: (i, 0)),
        out_shape=shaped((count, width), bf16),
        compiler_params=params,
    )(rows_in, slot_rows)


def product_wide(left, right_t, chunk=1024):
    rows, depth = left.shape
    cols = right_t.shape[0]

    def kernel(l_ref, r_ref, o_ref):
        o_ref[...] = dot_nt(l_ref[...], r_ref[...]).astype(bf16)

    return pl.pallas_call(
        kernel,
        name="product_wide",
        cost_estimate=cost(7),
        grid=(cols // chunk,),
        in_specs=[fixed((rows, depth)), spec((chunk, depth), lambda i: (i, 0))],
        out_specs=spec((rows, chunk), lambda i: (0, i)),
        out_shape=shaped((rows, cols), bf16),
        compiler_params=params,
    )(left, right_t)


def outer_by_right(left, right, chunk):
    rows, mine = left.shape
    cols = right.shape[1]

    def kernel(l_ref, r_ref, o_ref):
        o_ref[...] = dot_tn(l_ref[...], r_ref[...]).astype(bf16)

    return pl.pallas_call(
        kernel,
        name="outer_by_right",
        cost_estimate=cost(10),
        grid=(cols // chunk,),
        in_specs=[fixed((rows, mine)), spec((rows, chunk), lambda i: (0, i))],
        out_specs=spec((mine, chunk), lambda i: (0, i)),
        out_shape=shaped((mine, cols), bf16),
        compiler_params=params,
    )(left, right)


def outer_by_left(left, right, chunk):
    rows, mine = left.shape
    cols = right.shape[1]

    def kernel(l_ref, r_ref, o_ref):
        o_ref[...] = dot_tn(l_ref[...], r_ref[...]).astype(bf16)

    return pl.pallas_call(
        kernel,
        name="outer_by_left",
        cost_estimate=cost(10),
        grid=(mine // chunk,),
        in_specs=[spec((rows, chunk), lambda i: (0, i)), fixed((rows, cols))],
        out_specs=spec((chunk, cols), lambda i: (i, 0)),
        out_shape=shaped((mine, cols), bf16),
        compiler_params=params,
    )(left, right)


def plane_neighbours(array, by):
    return lax.ppermute(array, "rep", [(i, i ^ by) for i in range(4)])


def after(value, *others):
    return lax.optimization_barrier((value, *others))[0]


def add_low(left, right):
    return (left.astype(f32) + right.astype(f32)).astype(bf16)


class PlaneSum:
    def __init__(self, array, first):
        self.first, self.second = first, 3 - first
        rep = lax.axis_index("rep")
        self.near, self.far = lax.rem(rep // first, 2), lax.rem(rep // self.second, 2)
        self.kept, self.got = self.exchange_half(array, self.near, first)

    def exchange_half(self, whole, bit, by):
        halves = whole.reshape(2, whole.shape[0] // 2, whole.shape[1])
        kept = lax.dynamic_index_in_dim(halves, bit, 0, False)
        sent = lax.dynamic_index_in_dim(halves, 1 - bit, 0, False)
        return kept, plane_neighbours(sent, by)

    def fold(self, *before):
        self.kept, self.got = after((self.kept, self.got), *before)
        half = add_low(self.kept, self.got)
        self.kept, self.got = self.exchange_half(half, self.far, self.second)
        return half

    def spread(self, *before):
        self.kept, self.got = after((self.kept, self.got), *before)
        self.own = add_low(self.kept, self.got)
        self.beside = plane_neighbours(self.own, self.second)
        return self.own

    def cross(self, *before):
        self.beside = after(self.beside, *before)
        self.across = [plane_neighbours(p, self.first) for p in (self.own, self.beside)]
        return self.beside

    def pieces(self):
        low, high = 2 * self.near + self.far, 2 * (1 - self.near) + self.far
        flip = 1 - 2 * self.far
        return [low, low + flip, high, high + flip], [self.own, self.beside, *self.across]


class PlanePair:
    def __init__(self, array):
        half = array.shape[0] // 2
        self.parts = [PlaneSum(array[:half], 1), PlaneSum(array[half:], 2)]

    def fold(self, *before):
        return [p.fold(*before) for p in self.parts]

    def spread(self, *before):
        return [p.spread(*before) for p in self.parts]

    def cross(self, *before):
        return [p.cross(*before) for p in self.parts]

    def finish(self, *before):
        places, pieces = [], []
        for base, part in zip((0, 4), self.parts):
            where, what = part.pieces()
            places += [base + w for w in where]
            pieces += what
        pieces = after(pieces, *before)
        return place_pieces(jnp.stack(places).astype(jnp.int32), pieces)


class PlainSum:
    def __init__(self, array):
        self.total = lax.psum(array, "rep").astype(f32)

    def fold(self, *before):
        return self.total

    spread = cross = finish = fold


def plane_sum_small(array):
    parts = jnp.split(array, 2, axis=0)
    firsts = [add_low(p, plane_neighbours(p, by)) for p, by in zip(parts, (1, 2))]
    lasts = [
        p.astype(f32) + plane_neighbours(p, by).astype(f32) for p, by in zip(firsts, (2, 1))
    ]
    return jnp.concatenate(lasts, axis=0)


def plane_piece(shards, tail=None):
    rep = lax.axis_index("rep")
    pieces = []
    for shard in shards:
        rows, cols = shard.shape[0] // 2, shard.shape[1] // 2
        pieces.append(
            lax.dynamic_slice(shard, ((rep // 2) * rows, (rep % 2) * cols), (rows, cols))
        )
    if tail is not None:
        rows = tail.shape[0] // 2
        pieces.append(lax.dynamic_slice(tail, ((rep // 2) * rows, 0), (rows, tail.shape[1])))
    return jnp.concatenate(pieces, axis=1).astype(bf16)


def gather_line(piece):
    groups = lax.axis_size("exp") // 2
    lines = [[2 * z + c for z in range(groups)] for c in range(2)]
    return lax.all_to_all(
        jnp.broadcast_to(piece[None], (groups,) + piece.shape),
        "exp", split_axis=0, concat_axis=0, axis_index_groups=lines,
    )


def gather_plane(own):
    return own, *[plane_neighbours(own, by) for by in (1, 2, 3)]


def gather_cores(parts, layout, total):
    ranks = lax.axis_size("exp")
    mine = assemble(lax.axis_index("rep").reshape(1), parts, layout, total)
    other = lax.ppermute(mine, "exp", [(i, i ^ 1) for i in range(ranks)])
    return lax.rem(lax.axis_index("exp"), 2).reshape(1), mine, other


def gather_plain(shards):
    whole_rows = [lax.all_gather(s.astype(bf16), "exp", axis=0, tiled=True) for s in shards]
    joined = jnp.concatenate(whole_rows, axis=1)
    halves = joined.reshape(4, 2, joined.shape[0] // 8, joined.shape[1])
    return jnp.zeros((1,), jnp.int32), halves[:, 0], halves[:, 1]


def body(
    tokens, qkv_weight, out_weight, up_weight, down_weight, router_weight,
    first_gain, second_gain, third_gain, widening, narrowing, expert_ids, priority, cotangent,
):
    rows, width = tokens.shape
    hidden_width = up_weight.shape[1]
    ranks, reps = lax.axis_size("exp"), lax.axis_size("rep")
    experts = widening.shape[0] * ranks
    capacity = (rows + experts - 1) // experts
    half = capacity // 2
    count = experts * capacity
    pairs = width // 128
    me = lax.axis_index("exp").reshape(1)

    def reduce_dense(array):
        return lax.psum_scatter(array, "exp", scatter_dimension=0, tiled=True)

    plane = ranks == 8 and reps == 4

    over_rep = PlanePair if plane else PlainSum

    choice_hot = (expert_ids[:, :, None] == jnp.arange(experts, dtype=jnp.int32)).astype(f32)
    rank_row = priority[0]
    earlier = (rank_row[None, :] < rank_row[:, None]).astype(bf16)
    ahead = dot(earlier, choice_hot.reshape(rows, -1).astype(bf16)).reshape(choice_hot.shape)
    totals = jnp.sum(choice_hot, axis=0)
    prior = jnp.cumsum(totals, axis=0) - totals
    position = jnp.sum((ahead + prior[None]) * choice_hot, axis=-1).astype(jnp.int32)
    kept = position < capacity
    slots = jnp.where(kept, expert_ids * capacity + position, -1)
    later = position >= half
    split_slots = expert_ids * half + position + jnp.where(later, experts * half - half, 0)
    split_slots = jnp.where(kept, split_slots, -1)
    slot_rows = split_slots.T
    ids_rows = expert_ids.reshape(rows // 288, 288, 2).swapaxes(1, 2)
    whole_rows = slots.T

    def exchange(array, amount):
        return lax.all_to_all(
            array.reshape(experts, amount, width), "exp", split_axis=0, concat_axis=0, tiled=True
        ).reshape(experts * amount, width)

    def both_halves(rows_in):
        return [to_slots(rows_in, slot_rows - j * (count // 2), count // 2) for j in range(2)]

    small = jnp.concatenate(
        [router_weight, first_gain[:, None], second_gain[:, None], third_gain[:, None]], axis=1
    )
    small = jnp.pad(small, ((0, 0), (0, 128 - experts - 3)))
    by_pair = qkv_weight.reshape(-1, 3, pairs, 128).swapaxes(1, 2).reshape(-1, 3 * width)
    wide, deep = width // 2, hidden_width // 2
    if plane:
        own = gather_line(plane_piece((by_pair,), small))
        pieces = gather_plane(own)
        sent_cots, narrow_low = to_slots_cast(
            after(cotangent, own, slot_rows, ids_rows, slots, split_slots),
            whole_rows, count, narrowing[0],
        )
        piece, piece_down = plane_piece((out_weight, up_weight)), plane_piece((down_weight,))
        tall = piece.shape[0]
        piece = piece.reshape(tall, -1, wide).swapaxes(0, 1).reshape(-1, wide)
        own_both = gather_line(after(jnp.concatenate([piece, piece_down], axis=0), own))
        own_next = own_both[:, : piece.shape[0]].reshape(ranks // 2, -1, tall, wide)
        own_next = own_next.swapaxes(1, 2).reshape(ranks // 2, tall, -1)
        own_down = own_both[:, piece.shape[0] :]
        qkv_w = gather_cores(
            after(pieces, own_both, sent_cots),
            ((0, 3 * wide, 0, 3 * wide), (3 * wide, 128, 3 * width, 0)), 3 * width + 128,
        )
        pieces = gather_plane(after(own_next, pieces))
        pieces_down = gather_plane(after(own_down, pieces))
    else:
        sent_cots, narrow_low = to_slots_cast(cotangent, whole_rows, count, narrowing[0])
        qkv_w = gather_plain((by_pair, small))
        out_up = gather_plain((out_weight, up_weight))
        down = gather_plain((down_weight,))

    split = pairs - 1
    qkv, probs, attended, first_low, small_t = attention_forward(
        tokens, qkv_w, experts, 0, split, pairs, None
    )
    if plane:
        out_up = gather_cores(
            after(pieces, small_t), ((0, wide, 0, wide), (wide, deep, width, deep)),
            width + hidden_width,
        )
    cots = exchange(after(sent_cots, small_t), capacity)
    gain_one, gain_two, gain_three = [(small_t, experts + k) for k in range(3)]
    qkv, probs, attended = attention_forward(
        first_low, qkv_w, experts, split, pairs - split, pairs, (qkv, probs, attended)
    )
    hidden, second_low, activ, slope, widen_low = dense_up(
        attended, tokens, out_up, gain_two, widening[0]
    )
    if plane:
        down = gather_cores(after(pieces_down, hidden), ((0, wide, 0, wide),), width)
    middle, third_low, gate_rows = dense_down(
        after(activ, cots), hidden, ids_rows, down, experts, gain_three
    )
    gates = gate_rows.swapaxes(1, 2).reshape(rows, 2)

    sent_rows = both_halves(third_low)
    cots = after(cots, third_low).reshape(experts, 2, half, width)
    cots = [cots[:, j].reshape(-1, width) for j in range(2)]
    cot_wide = [product_wide(c, narrow_low) for c in cots]
    sent_rows[1] = after(sent_rows[1], cot_wide)
    arrived = [exchange(x, half) for x in sent_rows]
    mains, y_rows = [], []
    for j in range(2):
        ready = after(arrived[j], y_rows, *[m[2] for m in mains])
        mains.append(expert_main(me, ready, widen_low, cot_wide[j], small_t, experts))
        if j == 0:
            y_rows.append(narrow_product(after(mains[j][0], mains[j][2]), narrow_low))
    z_rows, v_rows, dx_rows, slot_gates, router_parts = zip(*mains)
    dx_slots = [exchange(after(dx_rows[0], y_rows), half)]
    dx_slots.append(exchange(after(dx_rows[1], dx_slots[0]), half))
    y_rows.append(narrow_product(after(z_rows[1], dx_slots[0]), narrow_low))
    narrow_grads = narrow_outer(z_rows, after(cots, y_rows), slot_gates)
    narrow_sum = lax.psum(narrow_grads, "rep")
    widen_grads = widen_outer(after(arrived, narrow_grads), v_rows, slot_gates)
    y_sent = jnp.stack([y.reshape(experts, half, width) for y in y_rows], axis=1)

    y_slots = exchange(after(y_sent, dx_slots), capacity)

    dzl, third_part = norm_three_backward(
        after(dx_slots, widen_grads), split_slots, gates, cotangent, middle, gain_three
    )
    down_grads = outer_by_left(after(activ, y_slots), dzl, 1024)
    down_shard = reduce_dense(down_grads)
    widen_sum = over_rep(after(widen_grads, down_grads))
    du, dh, second_part = dense_backward(
        after(dzl, down_grads), slope, hidden, out_up, down, gain_two
    )
    widen_step = widen_sum.fold(du)
    up_grads = outer_by_right(after(second_low, widen_step), du, 1024)
    up_shard = reduce_dense(up_grads)
    out_grads = outer_by_right(after(attended, up_grads), dh, 768)
    out_shard = reduce_dense(out_grads)
    dh = after(dh, out_grads)
    halves = []
    for image in range(2):
        halves.append(attention_backward(
            image, dh, out_up, qkv, probs, attended, tokens, qkv_w, gain_one
        ))
        if image == 0:
            widen_step = widen_sum.spread(halves[0])
            dh = after(dh, halves[0], narrow_sum, down_shard, widen_step)
    dqkv, token_grads, first_parts = zip(*halves)
    widen_sum.cross(dqkv, up_shard)
    token_grads = jnp.concatenate(token_grads, axis=0)
    qkv_grads = outer_pair(
        first_low, dqkv, (router_parts, first_parts, second_part, third_part), 384
    )
    qkv_shard = reduce_dense(qkv_grads)
    widen_out = widen_sum.finish(qkv_grads)
    output = combine(after(y_slots, qkv_grads), slots, gates, middle)

    down_sum, up_sum = [
        lax.psum(s, "rep").astype(f32) for s in after((down_shard, up_shard), narrow_sum)
    ]
    narrow_out = after(narrow_sum, qkv_grads).astype(f32)
    small_total = plane_sum_small if plane else (lambda s: over_rep(s).finish())
    out_sum = small_total(after(out_shard, qkv_grads))
    qkv_shard = after(qkv_shard, widen_out, output, narrow_out, down_sum, up_sum, out_sum)
    qkv_sum = small_total(qkv_shard)
    small_sum = qkv_sum[:, 3 * width :]
    qkv_sum = qkv_sum[:, : 3 * width].reshape(-1, pairs, 3, 128).swapaxes(1, 2)
    qkv_sum = qkv_sum.reshape(-1, 3 * width)
    return (
        output, token_grads,
        qkv_sum, out_sum, up_sum, down_sum,
        small_sum[:, :experts], small_sum[:, experts], small_sum[:, experts + 1],
        small_sum[:, experts + 2],
        widen_out[None], narrow_out[None],
    )


def solution(mesh):
    rows_spec, exp_spec = P(("rep", "exp"), None), P("exp", None)
    return jax.shard_map(
        body,
        mesh=mesh,
        in_specs=(
            rows_spec, exp_spec, exp_spec, exp_spec, exp_spec, exp_spec,
            P("exp"), P("exp"), P("exp"), P("exp", None, None), P("exp", None, None),
            rows_spec, rows_spec, rows_spec,
        ),
        out_specs=(
            rows_spec, rows_spec, exp_spec, exp_spec, exp_spec, exp_spec, exp_spec,
            P("exp"), P("exp"), P("exp"), P("exp", None, None), P("exp", None, None),
        ),
        check_vma=False,
    )
```

```python
import jax
import jax.numpy as jnp
from jax import lax
from jax.experimental import pallas as pl
from jax.experimental.pallas import tpu as pltpu
from jax.sharding import PartitionSpec as P

PATCHES = 576
HEAD_DIM = 64
EPSILON = 1e-6
LOG2E = 1.4426950408889634
ROOT_HALF = 0.7071067811865476
INV_ROOT_2PI = 0.3989422804014327
bf16 = jnp.bfloat16
f32 = jnp.float32
params = pltpu.CompilerParams(vmem_limit_bytes=58 << 20)


def dot(left, right):
    return jnp.dot(left, right, preferred_element_type=f32)


def dot_nt(left, right):
    return lax.dot_general(left, right, (((1,), (1,)), ((), ())), preferred_element_type=f32)


def dot_tn(left, right):
    return lax.dot_general(left, right, (((0,), (0,)), ((), ())), preferred_element_type=f32)


def unit_norm(values):
    centred = values - jnp.mean(values, axis=-1, keepdims=True)
    inverse = lax.rsqrt(jnp.mean(centred * centred, axis=-1, keepdims=True) + EPSILON)
    return centred * inverse, inverse


def norm_inward(upstream, unit, inverse, gain):
    scaled = upstream * gain
    return inverse * (
        scaled
        - jnp.mean(scaled, axis=-1, keepdims=True)
        - unit * jnp.mean(scaled * unit, axis=-1, keepdims=True)
    )


def gelu_pair(u):
    half = 0.5 + 0.5 * lax.erf(u * ROOT_HALF)
    density = jnp.exp2(u * u * (-0.5 * LOG2E)) * INV_ROOT_2PI
    return u * half, half + u * density


def cost(microseconds):
    return pl.CostEstimate(
        flops=int(microseconds * 8e+08), bytes_accessed=int(microseconds * 2e+06), transcendentals=0
    )


def spec(shape, index):
    return pl.BlockSpec(shape, index)


def fixed(shape):
    zeros = (0,) * len(shape)
    return pl.BlockSpec(shape, lambda *_: zeros, pipeline_mode=pl.Buffered(1))


def shaped(shape, dtype):
    return jax.ShapeDtypeStruct(shape, dtype)


any_space = pl.BlockSpec(memory_space=pl.ANY)
scalar_space = pl.BlockSpec(memory_space=pltpu.SMEM)


def attention_forward(rows_in, weight, small, first_pair, pairs, pairs_all, earlier):
    rows, width = rows_in.shape
    images, first = rows // PATCHES, earlier is None
    cols = 384 * pairs

    def kernel(*refs):
        if first:
            (core_ref, x_ref, hw_ref, kw_ref, qkv_ref, p_ref, o_ref, a_ref, st_ref,
             w_ref, sem, sm_ref, sem_small) = refs
        else:
            (core_ref, a_ref, hw_ref, kw_ref, _, _, _, qkv_ref, p_ref, o_ref, w_ref, sem) = refs
        image, pair = pl.program_id(0), pl.program_id(1)

        @pl.when((pair == 0) & (image == 0))
        def _():
            load_halves(core_ref[0], hw_ref, kw_ref, w_ref, sem, 384 * first_pair, cols)
            if first:
                load_halves(core_ref[0], hw_ref, kw_ref, sm_ref, sem_small, 3 * width, 128)
                st_ref[...] = sm_ref[...].astype(f32).T

        if first:
            @pl.when(pair == 0)
            def _():
                unit, _ = unit_norm(x_ref[...].astype(f32))
                a_ref[...] = (unit * st_ref[small : small + 1, :]).astype(bf16)

        qkv = dot(a_ref[...], w_ref[:, pl.ds(pl.multiple_of(pair * 384, 128), 384)]).astype(bf16)
        qkv_ref[...] = qkv
        q, k, v = qkv[:, :128], qkv[:, 128:256], qkv[:, 256:]
        q = (q.astype(f32) * HEAD_DIM ** (-0.5)).astype(bf16)
        low_lane = lax.broadcasted_iota(jnp.int32, (PATCHES, 128), 1) < HEAD_DIM
        v_t = v.T
        outs = []
        for h in range(2):
            k_head = jnp.where(low_lane == (h == 0), k, jnp.zeros_like(k))
            s = dot_nt(k_head, q)
            top = jnp.max(s, axis=0, keepdims=True)
            e = jnp.exp2((s - top) * LOG2E)
            total = jnp.sum(e, axis=0, keepdims=True)
            p = (e * (1.0 / total)).astype(bf16)
            p_ref[0, h] = p
            outs.append(dot(v_t[h * HEAD_DIM : (h + 1) * HEAD_DIM], p))
        o_ref[...] = jnp.concatenate(outs, axis=0).T.astype(bf16)

    groups = weight[1].shape[0]
    by_image = spec((PATCHES, width), lambda i, j: (i, 0))
    out_specs = [
        spec((PATCHES, 384), lambda i, j: (i, j + first_pair)),
        spec((1, 2, PATCHES, PATCHES), lambda i, j: (i, j + first_pair, 0, 0)),
        spec((PATCHES, 128), lambda i, j: (i, j + first_pair)),
    ]
    out_shape = [
        shaped((rows, 384 * pairs_all), bf16),
        shaped((images, 2 * pairs_all, PATCHES, PATCHES), bf16),
        shaped((rows, 128 * pairs_all), bf16),
    ]
    in_specs = [scalar_space, by_image, any_space, any_space]
    scratch = [pltpu.VMEM((width, cols), bf16), pltpu.SemaphoreType.DMA((2, groups))]
    if first:
        out_specs += [by_image, spec((128, width), lambda i, j: (0, 0))]
        out_shape += [shaped((rows, width), bf16), shaped((128, width), f32)]
        scratch += [pltpu.VMEM((width, 128), bf16), pltpu.SemaphoreType.DMA((2, groups))]
        operands, aliases = (weight[0], rows_in, *weight[1:]), {}
    else:
        in_specs += [any_space] * 3
        operands, aliases = (weight[0], rows_in, *weight[1:], *earlier), {4: 0, 5: 1, 6: 2}
    return pl.pallas_call(
        kernel,
        name="attention_forward",
        cost_estimate=cost(8 * images * pairs // 4),
        grid=(images, pairs),
        in_specs=in_specs,
        out_specs=out_specs,
        out_shape=out_shape,
        scratch_shapes=scratch,
        input_output_aliases=aliases,
        compiler_params=params,
    )(*operands)


def attention_backward(image, dh, out_weight, qkv, probs, attended, tokens, qkv_weight, gain):
    width = dh.shape[1]
    pairs = width // 128

    def kernel(
        core_ref, dh_ref, ho_ref, ko_ref, qkv_ref, p_ref, o_ref, x_ref, hw_ref, kw_ref, g_ref,
        dq_ref, dx_ref, dg_ref, do_ref, db_ref, wo_ref, w_ref, sem, sem_w,
    ):
        pair = pl.program_id(0)

        @pl.when(pair == 0)
        def _():
            load_halves(core_ref[0], ho_ref, ko_ref, wo_ref, sem, 0, width)
            load_halves(core_ref[0], hw_ref, kw_ref, w_ref, sem_w, 0, 3 * width)

        @pl.when(pair == 0)
        def _():
            do = dot_nt(dh_ref[...], wo_ref[...]).astype(bf16)
            for j in range(pairs):
                do_ref[j] = do[:, j * 128 : (j + 1) * 128]

        q, k, v = qkv_ref[:, :128], qkv_ref[:, 128:256], qkv_ref[:, 256:]
        q = (q.astype(f32) * HEAD_DIM ** (-0.5)).astype(bf16)
        do = do_ref[pair]
        low_lane = lax.broadcasted_iota(jnp.int32, (PATCHES, 128), 1) < HEAD_DIM
        prod = do.astype(f32) * o_ref[...].astype(f32)
        prod_high = prod.astype(bf16)
        prod_low = (prod - prod_high.astype(f32)).astype(bf16)
        pick_row = lax.broadcasted_iota(jnp.int32, (16, 128), 0)
        pick_lane = lax.broadcasted_iota(jnp.int32, (16, 128), 1)
        pick = (pick_lane // HEAD_DIM == pick_row).astype(bf16)
        row_sums = dot_nt(pick, prod_high) + dot_nt(pick, prod_low)
        k_t = k.T
        dqs, dks, dvs = [], [], []
        for h in range(2):
            v_head = jnp.where(low_lane == (h == 0), v, jnp.zeros_like(v))
            dp = dot_nt(v_head, do)
            p = p_ref[0, h]
            ds = (p.astype(f32) * (dp - row_sums[h : h + 1])).astype(bf16)
            dvs.append(dot(p, do))
            dks.append(dot(ds, q))
            dqs.append(dot(k_t[h * HEAD_DIM : (h + 1) * HEAD_DIM], ds))
        dq = (jnp.concatenate(dqs, axis=0) * HEAD_DIM ** (-0.5)).T
        dqkv = jnp.concatenate(
            [dq, jnp.where(low_lane, dks[0], dks[1]), jnp.where(low_lane, dvs[0], dvs[1])], axis=1
        ).astype(bf16)
        dq_ref[...] = dqkv

        w_pair = w_ref[:, pl.ds(pl.multiple_of(pair * 384, 128), 384)]

        @pl.when(pair == 0)
        def _():
            db_ref[...] = dot_nt(dqkv, w_pair)

        @pl.when(pair > 0)
        def _():
            db_ref[...] += dot_nt(dqkv, w_pair)

        @pl.when(pair == pairs - 1)
        def _():
            upstream = db_ref[...]
            unit, inverse = unit_norm(x_ref[...].astype(f32))
            inward = norm_inward(upstream, unit, inverse, g_ref[gain[1] : gain[1] + 1, :])
            dx_ref[...] = (dh_ref[...].astype(f32) + inward).astype(bf16)
            dg_ref[...] = jnp.sum(upstream * unit, axis=0, keepdims=True)

    by_image = spec((PATCHES, width), lambda j: (image, 0))
    out_image = spec((PATCHES, width), lambda j: (0, 0))
    return pl.pallas_call(
        kernel,
        name="attention_backward",
        cost_estimate=cost(1000),
        grid=(pairs,),
        in_specs=[
            scalar_space, by_image, any_space, any_space,
            spec((PATCHES, 384), lambda j: (image, j)),
            spec((1, 2, PATCHES, PATCHES), lambda j: (image, j, 0, 0)),
            spec((PATCHES, 128), lambda j: (image, j)),
            by_image,
            any_space, any_space,
            fixed(gain[0].shape),
        ],
        out_specs=[
            spec((PATCHES, 384), lambda j: (0, j)), out_image,
            spec((1, width), lambda j: (0, 0)),
        ],
        out_shape=[
            shaped((PATCHES, 3 * width), bf16), shaped((PATCHES, width), bf16),
            shaped((1, width), f32),
        ],
        scratch_shapes=[
            pltpu.VMEM((pairs, PATCHES, 128), bf16),
            pltpu.VMEM((PATCHES, width), f32),
            pltpu.VMEM((width, width), bf16),
            pltpu.VMEM((width, 3 * width), bf16),
            pltpu.SemaphoreType.DMA((2, out_weight[1].shape[0])),
            pltpu.SemaphoreType.DMA((2, out_weight[1].shape[0])),
        ],
        compiler_params=params,
    )(out_weight[0], dh, *out_weight[1:], qkv, probs, attended, tokens, *qkv_weight[1:], gain[0])


def load_halves(core, mine_ref, other_ref, whole_ref, sem, start, cols):
    groups, rows, _ = mine_ref.shape
    copies = []
    for z in range(groups):
        for side, ref in enumerate((mine_ref, other_ref)):
            place = core if side == 0 else 1 - core
            base = pl.multiple_of((2 * z + place) * rows, 16)
            copies.append(
                pltpu.make_async_copy(
                    ref.at[z, :, pl.ds(start, cols)],
                    whole_ref.at[pl.ds(base, rows), :],
                    sem.at[side, z],
                )
            )
    for copy in copies:
        copy.start()
    for copy in copies:
        copy.wait()


def assemble(place, parts, layout, total):
    groups, rows, _ = parts[0].shape

    def kernel(r_ref, own_ref, x_ref, y_ref, far_ref, o_ref):
        down, right = r_ref[0] // 2, r_ref[0] % 2

        def put(ref, row_half, col_half):
            at = pl.multiple_of(row_half * rows, 16)
            for start, wide, base, step in layout:
                to = pl.multiple_of(base + col_half * step, 128)
                o_ref[:, pl.ds(at, rows), pl.ds(to, wide)] = ref[:, :, start : start + wide]

        put(own_ref, down, right)
        put(x_ref, down, 1 - right)
        put(y_ref, 1 - down, right)
        put(far_ref, 1 - down, 1 - right)

    return pl.pallas_call(
        kernel,
        name="assemble",
        cost_estimate=cost(4),
        in_specs=[scalar_space] + [pl.BlockSpec(memory_space=pltpu.VMEM)] * 4,
        out_specs=pl.BlockSpec(memory_space=pltpu.VMEM),
        out_shape=shaped((groups, 2 * rows, total), bf16),
        compiler_params=params,
    )(place, *parts)


def by_rows(block, cols):
    return spec((block, cols), lambda i: (i, 0))


def whole(shape):
    return spec(shape, lambda i: (0,) * len(shape))


def dense_up(attended, tokens, weights, gain, extra):
    rows, width = tokens.shape
    hidden = weights[1].shape[2] - width
    block, chunk = 288, 512
    tall, wide = extra.shape
    tall = tall * block // rows

    def kernel(
        core_ref, o_ref, x_ref, hw_ref, kw_ref, g_ref, e_ref,
        h_ref, b_ref, z_ref, s_ref, low_ref, w_ref, sem,
    ):
        @pl.when(pl.program_id(0) == 0)
        def _():
            load_halves(core_ref[0], hw_ref, kw_ref, w_ref, sem, 0, width + hidden)

        low_ref[...] = e_ref[...].astype(bf16)
        h = x_ref[...].astype(f32) + dot(o_ref[...], w_ref[:, :width])
        h = h.astype(bf16)
        h_ref[...] = h
        h = h.astype(f32)
        b = (unit_norm(h)[0] * g_ref[gain[1] : gain[1] + 1, :]).astype(bf16)
        b_ref[...] = b
        ahead = dot(b, w_ref[:, width : width + chunk])
        for c in range(0, hidden, chunk):
            u = ahead
            if c + chunk < hidden:
                ahead = dot(b, w_ref[:, width + c + chunk : width + c + 2 * chunk])
            z, slope = gelu_pair(u)
            z_ref[:, c : c + chunk] = z.astype(bf16)
            s_ref[:, c : c + chunk] = slope.astype(bf16)

    return pl.pallas_call(
        kernel,
        name="dense_up",
        cost_estimate=cost(18),
        grid=(rows // block,),
        in_specs=[
            scalar_space, by_rows(block, width), by_rows(block, width), any_space, any_space,
            fixed(gain[0].shape), by_rows(tall, wide),
        ],
        out_specs=[
            by_rows(block, width), by_rows(block, width), by_rows(block, hidden),
            by_rows(block, hidden), by_rows(tall, wide),
        ],
        out_shape=[
            shaped((rows, width), bf16), shaped((rows, width), bf16),
            shaped((rows, hidden), bf16), shaped((rows, hidden), bf16),
            shaped(extra.shape, bf16),
        ],
        scratch_shapes=[
            pltpu.VMEM((width, width + hidden), bf16),
            pltpu.SemaphoreType.DMA((2, weights[1].shape[0])),
        ],
        compiler_params=params,
    )(weights[0], attended, tokens, *weights[1:], gain[0], extra)


def dense_down(activ, hidden_rows, ids, weights, experts, gain):
    rows, width = hidden_rows.shape
    hidden = activ.shape[1]
    block = 288

    def kernel(
        core_ref, z_ref, h_ref, id_ref, hw_ref, kw_ref, g_ref,
        y_ref, m_ref, gate_ref, w_ref, sem,
    ):
        @pl.when(pl.program_id(0) == 0)
        def _():
            load_halves(core_ref[0], hw_ref, kw_ref, w_ref, sem, 0, width)

        y = h_ref[...].astype(f32) + dot(z_ref[...], w_ref[...])
        y_ref[...] = y.astype(bf16)
        m = (unit_norm(y)[0] * g_ref[gain[1] : gain[1] + 1, :]).astype(bf16)
        m_ref[...] = m
        logits = dot_nt(g_ref[:experts, :].astype(bf16), m)
        e = jnp.exp(logits - jnp.max(logits, axis=0, keepdims=True))
        p = e / jnp.sum(e, axis=0, keepdims=True)
        line = lax.broadcasted_iota(jnp.int32, (experts, block), 0)
        for k in range(2):
            hot = line == id_ref[0, k : k + 1, :]
            gate_ref[0, k : k + 1, :] = jnp.sum(jnp.where(hot, p, 0.0), axis=0, keepdims=True)

    return pl.pallas_call(
        kernel,
        name="dense_down",
        cost_estimate=cost(15),
        grid=(rows // block,),
        in_specs=[
            scalar_space, by_rows(block, hidden), by_rows(block, width),
            spec((1, 2, block), lambda i: (i, 0, 0)),
            any_space, any_space, fixed(gain[0].shape),
        ],
        out_specs=[
            by_rows(block, width), by_rows(block, width),
            spec((1, 2, block), lambda i: (i, 0, 0)),
        ],
        out_shape=[
            shaped((rows, width), bf16), shaped((rows, width), bf16),
            shaped((rows // block, 2, block), f32),
        ],
        scratch_shapes=[
            pltpu.VMEM((hidden, width), bf16),
            pltpu.SemaphoreType.DMA((2, weights[1].shape[0])),
        ],
        compiler_params=params,
    )(weights[0], activ, hidden_rows, ids, *weights[1:], gain[0])


def gated_rows(slot_ref, gate_ref, slots_refs, block):
    total, base = None, 0
    for ref in slots_refs:
        count = ref.shape[0]
        lane = base + lax.broadcasted_iota(jnp.int32, (block, count), 1)
        weighted = jnp.zeros((block, count), f32)
        for k in range(2):
            hot = lane == slot_ref[:, k : k + 1]
            weighted = weighted + jnp.where(hot, gate_ref[:, k : k + 1], 0.0)
        part = dot(weighted.astype(bf16), ref[...])
        total = part if total is None else total + part
        base += count
    return total


def norm_three_backward(dx_slots, slots, gates, cotangent, middle, gain):
    rows, width = cotangent.shape
    block = 288

    def kernel(da_ref, db_ref, slot_ref, gate_ref, cot_ref, y_ref, g_ref, dzl_ref, dg_ref):
        dm = gated_rows(slot_ref, gate_ref, (da_ref, db_ref), block)
        unit, inverse = unit_norm(y_ref[...].astype(f32))
        part = jnp.sum(dm * unit, axis=0, keepdims=True)
        dy = cot_ref[...].astype(f32) + norm_inward(dm, unit, inverse, g_ref[gain[1] : gain[1] + 1, :])
        dzl_ref[...] = dy.astype(bf16)
        first = pl.program_id(0) == 0

        @pl.when(first)
        def _():
            dg_ref[...] = part

        @pl.when(jnp.logical_not(first))
        def _():
            dg_ref[...] += part

    return pl.pallas_call(
        kernel,
        name="norm_three_backward",
        cost_estimate=cost(10),
        grid=(rows // block,),
        in_specs=[
            fixed(dx_slots[0].shape), fixed(dx_slots[1].shape), by_rows(block, 2),
            by_rows(block, 2), by_rows(block, width), by_rows(block, width), fixed(gain[0].shape),
        ],
        out_specs=[by_rows(block, width), whole((1, width))],
        out_shape=[shaped((rows, width), bf16), shaped((1, width), f32)],
        compiler_params=params,
    )(*dx_slots, slots, gates, cotangent, middle, gain[0])


def dense_backward(dzl, slope, hidden_rows, up_weight, down_weight, gain):
    rows, width = dzl.shape
    hidden = slope.shape[1]
    block, chunk = 288, 512

    def kernel(
        core_ref, dzl_ref, s_ref, h_ref, hu_ref, ku_ref, hd_ref, kd_ref, g_ref,
        du_ref, dhl_ref, dg_ref, w1_ref, w2_ref, sem,
    ):
        first = pl.program_id(0) == 0

        @pl.when(first)
        def _():
            load_halves(core_ref[0], hd_ref, kd_ref, w2_ref, sem, 0, width)
            load_halves(core_ref[0], hu_ref, ku_ref, w1_ref, sem, width, hidden)

        dzl = dzl_ref[...]
        db = jnp.zeros((block, width), f32)
        ahead = dot_nt(dzl, w2_ref[:chunk, :])
        for c in range(0, hidden, chunk):
            dz = ahead
            if c + chunk < hidden:
                ahead = dot_nt(dzl, w2_ref[c + chunk : c + 2 * chunk, :])
            du = (dz * s_ref[:, c : c + chunk].astype(f32)).astype(bf16)
            du_ref[:, c : c + chunk] = du
            db = db + dot_nt(du, w1_ref[:, c : c + chunk])
        unit, inverse = unit_norm(h_ref[...].astype(f32))
        part = jnp.sum(db * unit, axis=0, keepdims=True)
        dh = dzl.astype(f32) + norm_inward(db, unit, inverse, g_ref[gain[1] : gain[1] + 1, :])
        dhl_ref[...] = dh.astype(bf16)

        @pl.when(first)
        def _():
            dg_ref[...] = part

        @pl.when(jnp.logical_not(first))
        def _():
            dg_ref[...] += part

    return pl.pallas_call(
        kernel,
        name="dense_backward",
        cost_estimate=cost(24),
        grid=(rows // block,),
        in_specs=[
            scalar_space, by_rows(block, width), by_rows(block, hidden),
            by_rows(block, width), any_space, any_space, any_space, any_space, fixed(gain[0].shape),
        ],
        out_specs=[
            by_rows(block, hidden), by_rows(block, width), whole((1, width)),
        ],
        out_shape=[
            shaped((rows, hidden), bf16), shaped((rows, width), bf16), shaped((1, width), f32),
        ],
        scratch_shapes=[
            pltpu.VMEM((width, hidden), bf16), pltpu.VMEM((hidden, width), bf16),
            pltpu.SemaphoreType.DMA((2, up_weight[1].shape[0])),
        ],
        compiler_params=params,
    )(up_weight[0], dzl, slope, hidden_rows, *up_weight[1:], *down_weight[1:], gain[0])


def combine(y_slots, slots, gates, middle):
    rows, width = middle.shape
    block = 288

    def kernel(ya_ref, slot_ref, gate_ref, y_ref, o_ref):
        o_ref[...] = (
            y_ref[...].astype(f32) + gated_rows(slot_ref, gate_ref, (ya_ref,), block)
        ).astype(bf16)

    return pl.pallas_call(
        kernel,
        name="combine",
        cost_estimate=cost(8),
        grid=(rows // block,),
        in_specs=[
            fixed(y_slots.shape), by_rows(block, 2), by_rows(block, 2), by_rows(block, width),
        ],
        out_specs=by_rows(block, width),
        out_shape=shaped((rows, width), bf16),
        compiler_params=params,
    )(y_slots, slots, gates, middle)


def expert_main(me, rows_in, widen_low, cot_wide, small_t, experts):
    rows, width = rows_in.shape
    hidden = widen_low.shape[1]
    chunk, part = 1024, 512
    steps = hidden // chunk

    def kernel(
        me_ref, x_ref, a_ref, u_ref, wr_ref,
        z_ref, v_ref, dx_ref, gate_ref, dwr_ref, acc_ref, dg_ref,
    ):
        step = pl.program_id(0)

        @pl.when(step == 0)
        def _():
            acc_ref[...] = jnp.zeros_like(acc_ref)
            dg_ref[...] = jnp.zeros_like(dg_ref)

        x = x_ref[...]
        ahead = dot(x, a_ref[:, :part])
        sums = jnp.zeros((rows, 128), f32)
        for c in range(0, chunk, part):
            cols = slice(c, c + part)
            r = ahead
            if c + part < chunk:
                ahead = dot(x, a_ref[:, c + part : c + 2 * part])
            z, slope = gelu_pair(r)
            u = u_ref[:, cols].astype(f32)
            v = (u * slope).astype(bf16)
            z_ref[:, cols] = z.astype(bf16)
            v_ref[:, cols] = v
            dg = u * z
            sums = sums + sum(dg[:, q : q + 128] for q in range(0, part, 128))
            acc_ref[...] += dot_nt(v, a_ref[:, cols])
        dg_ref[...] += sums

        @pl.when(step == steps - 1)
        def _():
            wr = wr_ref[:experts, :].astype(bf16)
            logits = dot_nt(wr, x)
            e = jnp.exp(logits - jnp.max(logits, axis=0, keepdims=True))
            p = e / jnp.sum(e, axis=0, keepdims=True)
            own = lax.broadcasted_iota(jnp.int32, (experts, rows), 0) == me_ref[0]
            gate = jnp.sum(jnp.where(own, p, 0.0), axis=0, keepdims=True)
            gate_ref[...] = jnp.broadcast_to(gate, (128, rows)).T[:, :1]
            dgate = jnp.sum(dg_ref[...].T, axis=0, keepdims=True)
            spread = dgate * (own.astype(f32) - p)
            dx_ref[...] = (acc_ref[...] + dot_tn(spread.astype(bf16), wr)).astype(bf16)
            dwr_ref[...] = dot((gate * spread).astype(bf16), x)

    by_col = spec((rows, chunk), lambda i: (0, i))
    return pl.pallas_call(
        kernel,
        name="expert_main",
        cost_estimate=cost(15),
        grid=(steps,),
        in_specs=[
            scalar_space, fixed((rows, width)), spec((width, chunk), lambda i: (0, i)), by_col,
            fixed(small_t.shape),
        ],
        out_specs=[by_col, by_col, whole((rows, width)), whole((rows, 1)), whole((experts, width))],
        out_shape=[
            shaped((rows, hidden), bf16), shaped((rows, hidden), bf16),
            shaped((rows, width), bf16), shaped((rows, 1), f32), shaped((experts, width), f32),
        ],
        scratch_shapes=[pltpu.VMEM((rows, width), f32), pltpu.VMEM((rows, 128), f32)],
        compiler_params=params,
    )(me, rows_in, widen_low, cot_wide, small_t)


def narrow_outer(activs, cots, gates):
    rows, width = cots[0].shape
    hidden = activs[0].shape[1]
    chunk = 1024

    def kernel(za_ref, zb_ref, ca_ref, cb_ref, ga_ref, gb_ref, o_ref, da_ref, db_ref):
        @pl.when(pl.program_id(0) == 0)
        def _():
            da_ref[...] = (ca_ref[...].astype(f32) * ga_ref[...]).astype(bf16)
            db_ref[...] = (cb_ref[...].astype(f32) * gb_ref[...]).astype(bf16)

        o_ref[...] = (
            dot_tn(za_ref[...], da_ref[...]) + dot_tn(zb_ref[...], db_ref[...])
        ).astype(bf16)

    by_col = spec((rows, chunk), lambda i: (0, i))
    return pl.pallas_call(
        kernel,
        name="narrow_outer",
        cost_estimate=cost(12),
        grid=(hidden // chunk,),
        in_specs=[by_col, by_col] + [fixed((rows, width))] * 2 + [fixed((rows, 1))] * 2,
        out_specs=spec((chunk, width), lambda i: (i, 0)),
        out_shape=shaped((hidden, width), bf16),
        scratch_shapes=[pltpu.VMEM((rows, width), bf16)] * 2,
        compiler_params=params,
    )(*activs, *cots, *gates)


def widen_outer(rows_in, slopes, gates):
    rows, width = rows_in[0].shape
    hidden = slopes[0].shape[1]
    chunk = 1024

    def kernel(xa_ref, xb_ref, va_ref, vb_ref, ga_ref, gb_ref, o_ref, da_ref, db_ref):
        @pl.when(pl.program_id(0) == 0)
        def _():
            da_ref[...] = (xa_ref[...].astype(f32) * ga_ref[...]).astype(bf16)
            db_ref[...] = (xb_ref[...].astype(f32) * gb_ref[...]).astype(bf16)

        o_ref[...] = (
            dot_tn(da_ref[...], va_ref[...]) + dot_tn(db_ref[...], vb_ref[...])
        ).astype(bf16)

    by_col = spec((rows, chunk), lambda i: (0, i))
    return pl.pallas_call(
        kernel,
        name="widen_outer",
        cost_estimate=cost(12),
        grid=(hidden // chunk,),
        in_specs=[fixed((rows, width))] * 2 + [by_col, by_col] + [fixed((rows, 1))] * 2,
        out_specs=spec((width, chunk), lambda i: (0, i)),
        out_shape=shaped((width, hidden), bf16),
        scratch_shapes=[pltpu.VMEM((rows, width), bf16)] * 2,
        compiler_params=params,
    )(*rows_in, *slopes, *gates)


def narrow_product(activ, narrow_low):
    rows, hidden = activ.shape
    width = narrow_low.shape[1]
    block = rows // 2

    def kernel(z_ref, w_ref, o_ref):
        o_ref[...] = dot(z_ref[...], w_ref[...]).astype(bf16)

    return pl.pallas_call(
        kernel,
        name="narrow_product",
        cost_estimate=cost(6),
        grid=(2,),
        in_specs=[by_rows(block, hidden), fixed((hidden, width))],
        out_specs=by_rows(block, width),
        out_shape=shaped((rows, width), bf16),
        compiler_params=params,
    )(activ, narrow_low)


def outer_pair(left, rights, small_parts, chunk):
    half, cols = rights[0].shape
    mine = left.shape[1]
    blocks = cols // chunk
    routers, firsts, second, third = small_parts
    experts = routers[0].shape[0]

    def kernel(l_ref, a_ref, b_ref, ra_ref, rb_ref, fa_ref, fb_ref, s_ref, t_ref, o_ref, rows_ref):
        step = pl.program_id(0)

        @pl.when(step < blocks)
        def _():
            o_ref[...] = (
                dot_tn(l_ref[:half], a_ref[...]) + dot_tn(l_ref[half:], b_ref[...])
            ).astype(bf16)

        @pl.when(step == blocks)
        def _():
            rows_ref[...] = jnp.zeros_like(rows_ref)
            rows_ref[:experts] = ra_ref[...] + rb_ref[...]
            rows_ref[experts : experts + 1] = fa_ref[...] + fb_ref[...]
            rows_ref[experts + 1 : experts + 2] = s_ref[...]
            rows_ref[experts + 2 : experts + 3] = t_ref[...]
            o_ref[:, :128] = rows_ref[...].T.astype(bf16)

    by_col = spec((half, chunk), lambda i: (0, jnp.minimum(i, blocks - 1)))
    return pl.pallas_call(
        kernel,
        name="outer_pair",
        cost_estimate=cost(10),
        grid=(blocks + 1,),
        in_specs=[fixed((2 * half, mine)), by_col, by_col]
        + [fixed((experts, mine))] * 2 + [fixed((1, mine))] * 4,
        out_specs=spec((mine, chunk), lambda i: (0, i)),
        out_shape=shaped((mine, cols + 128), bf16),
        scratch_shapes=[pltpu.VMEM((128, mine), f32)],
        compiler_params=params,
    )(left, *rights, *routers, *firsts, second, third)


def place_pieces(place, pieces, earlier):
    rows, cols = pieces[0].shape
    amount = len(pieces)

    def kernel(place_ref, *refs):
        for k in range(amount):

            @pl.when(pl.program_id(0) == k)
            def _():
                refs[amount + 1][...] = refs[k][...].astype(f32)

    return pl.pallas_call(
        kernel,
        name="place_pieces",
        cost_estimate=cost(5),
        grid_spec=pltpu.PrefetchScalarGridSpec(
            num_scalar_prefetch=1,
            grid=(amount,),
            in_specs=[pl.BlockSpec((rows, cols), lambda i, p: (0, 0))] * amount + [any_space],
            out_specs=pl.BlockSpec((rows, cols), lambda i, p: (p[i], 0)),
        ),
        out_shape=shaped(earlier.shape, f32),
        input_output_aliases={amount + 1: 0},
        compiler_params=params,
    )(place, *pieces, earlier)


def cast_first(array, total):
    rows, cols = array.shape
    block = rows // 4

    def kernel(a_ref, o_ref):
        o_ref[...] = a_ref[...].astype(f32)

    return pl.pallas_call(
        kernel,
        name="cast_first",
        cost_estimate=cost(3),
        grid=(4,),
        in_specs=[by_rows(block, cols)],
        out_specs=by_rows(block, cols),
        out_shape=shaped((total, cols), f32),
        compiler_params=params,
    )(array)


def to_slots_cast(rows_in, slot_rows, count, weight):
    rows, width = rows_in.shape
    block = 288
    steps = count // block
    tall, wide = weight.shape

    def kernel(r_ref, s_ref, w_ref, o_ref, low_ref):
        base = pl.program_id(0) * block
        line = base + lax.broadcasted_iota(jnp.int32, (block, rows), 0)
        hot = (line == s_ref[0:1, :]) | (line == s_ref[1:2, :])
        o_ref[...] = dot(hot.astype(bf16), r_ref[...]).astype(bf16)
        low_ref[...] = w_ref[...].astype(bf16)

    return pl.pallas_call(
        kernel,
        name="to_slots_cast",
        cost_estimate=cost(20),
        grid=(steps,),
        in_specs=[fixed((rows, width)), fixed((2, rows)), by_rows(tall // steps, wide)],
        out_specs=[by_rows(block, width), by_rows(tall // steps, wide)],
        out_shape=[shaped((count, width), bf16), shaped((tall, wide), bf16)],
        compiler_params=params,
    )(rows_in, slot_rows, weight)


def outer_two(left, right, left_last, right_last):
    rows, mine = left.shape
    chunk = right_last.shape[1]
    blocks = right.shape[1] // chunk

    def kernel(l_ref, r_ref, ll_ref, rl_ref, o_ref):
        step = pl.program_id(0)

        @pl.when(step < blocks)
        def _():
            o_ref[...] = dot_tn(l_ref[...], r_ref[...]).astype(bf16)

        @pl.when(step == blocks)
        def _():
            o_ref[...] = dot_tn(ll_ref[...], rl_ref[...]).astype(bf16)

    return pl.pallas_call(
        kernel,
        name="outer_two",
        cost_estimate=cost(15),
        grid=(blocks + 1,),
        in_specs=[
            fixed((rows, mine)),
            spec((rows, chunk), lambda i: (0, jnp.minimum(i, blocks - 1))),
            fixed((rows, mine)), fixed((rows, chunk)),
        ],
        out_specs=spec((mine, chunk), lambda i: (0, i)),
        out_shape=shaped((mine, chunk * (blocks + 1)), bf16),
        compiler_params=params,
    )(left, right, left_last, right_last)


def to_slots(rows_in, slot_rows, count):
    rows, width = rows_in.shape
    block = 288

    def kernel(r_ref, s_ref, o_ref):
        base = pl.program_id(0) * block
        line = base + lax.broadcasted_iota(jnp.int32, (block, rows), 0)
        hot = (line == s_ref[0:1, :]) | (line == s_ref[1:2, :])
        o_ref[...] = dot(hot.astype(bf16), r_ref[...]).astype(bf16)

    return pl.pallas_call(
        kernel,
        name="to_slots",
        cost_estimate=cost(4),
        grid=(count // block,),
        in_specs=[fixed((rows, width)), fixed((2, rows))],
        out_specs=spec((block, width), lambda i: (i, 0)),
        out_shape=shaped((count, width), bf16),
        compiler_params=params,
    )(rows_in, slot_rows)


def product_wide(left, right_t, chunk=1024):
    rows, depth = left.shape
    cols = right_t.shape[0]

    def kernel(l_ref, r_ref, o_ref):
        o_ref[...] = dot_nt(l_ref[...], r_ref[...]).astype(bf16)

    return pl.pallas_call(
        kernel,
        name="product_wide",
        cost_estimate=cost(7),
        grid=(cols // chunk,),
        in_specs=[fixed((rows, depth)), spec((chunk, depth), lambda i: (i, 0))],
        out_specs=spec((rows, chunk), lambda i: (0, i)),
        out_shape=shaped((rows, cols), bf16),
        compiler_params=params,
    )(left, right_t)


def outer_by_right(left, right, chunk):
    rows, mine = left.shape
    cols = right.shape[1]

    def kernel(l_ref, r_ref, o_ref):
        o_ref[...] = dot_tn(l_ref[...], r_ref[...]).astype(bf16)

    return pl.pallas_call(
        kernel,
        name="outer_by_right",
        cost_estimate=cost(10),
        grid=(cols // chunk,),
        in_specs=[fixed((rows, mine)), spec((rows, chunk), lambda i: (0, i))],
        out_specs=spec((mine, chunk), lambda i: (0, i)),
        out_shape=shaped((mine, cols), bf16),
        compiler_params=params,
    )(left, right)


def outer_by_left(left, right, chunk):
    rows, mine = left.shape
    cols = right.shape[1]

    def kernel(l_ref, r_ref, o_ref):
        o_ref[...] = dot_tn(l_ref[...], r_ref[...]).astype(bf16)

    return pl.pallas_call(
        kernel,
        name="outer_by_left",
        cost_estimate=cost(10),
        grid=(mine // chunk,),
        in_specs=[spec((rows, chunk), lambda i: (0, i)), fixed((rows, cols))],
        out_specs=spec((chunk, cols), lambda i: (i, 0)),
        out_shape=shaped((mine, cols), bf16),
        compiler_params=params,
    )(left, right)


def plane_neighbours(array, by):
    return lax.ppermute(array, "rep", [(i, i ^ by) for i in range(4)])


def after(value, *others):
    return lax.optimization_barrier((value, *others))[0]


def add_low(left, right):
    return (left.astype(f32) + right.astype(f32)).astype(bf16)


class PlaneSum:
    def __init__(self, array, first):
        self.first, self.second = first, 3 - first
        rep = lax.axis_index("rep")
        self.near, self.far = lax.rem(rep // first, 2), lax.rem(rep // self.second, 2)
        self.kept, self.got = self.exchange_half(array, self.near, first)

    def exchange_half(self, whole, bit, by):
        halves = whole.reshape(2, whole.shape[0] // 2, whole.shape[1])
        kept = lax.dynamic_index_in_dim(halves, bit, 0, False)
        sent = lax.dynamic_index_in_dim(halves, 1 - bit, 0, False)
        return kept, plane_neighbours(sent, by)

    def fold(self, *before):
        self.kept, self.got = after((self.kept, self.got), *before)
        half = add_low(self.kept, self.got)
        self.kept, self.got = self.exchange_half(half, self.far, self.second)
        return half

    def spread(self, *before):
        self.kept, self.got = after((self.kept, self.got), *before)
        self.own = add_low(self.kept, self.got)
        self.beside = plane_neighbours(self.own, self.second)
        return self.own

    def cross(self, *before):
        self.beside = after(self.beside, *before)
        self.across = [plane_neighbours(p, self.first) for p in (self.own, self.beside)]
        return self.beside

    def pieces(self):
        low, high = 2 * self.near + self.far, 2 * (1 - self.near) + self.far
        flip = 1 - 2 * self.far
        return [low, low + flip, high, high + flip], [self.own, self.beside, *self.across]


class PlanePair:
    def __init__(self, array):
        half = array.shape[0] // 2
        self.parts = [PlaneSum(array[:half], 1), PlaneSum(array[half:], 2)]

    def fold(self, *before):
        return [p.fold(*before) for p in self.parts]

    def spread(self, *before):
        return [p.spread(*before) for p in self.parts]

    def cross(self, *before):
        return [p.cross(*before) for p in self.parts]

    def finish(self, earlier, *before):
        places, pieces = [], []
        base = earlier.shape[0] // self.parts[0].own.shape[0] - 8
        for start, part in zip((base, base + 4), self.parts):
            where, what = part.pieces()
            places += [start + w for w in where]
            pieces += what
        pieces = after(pieces, *before)
        return place_pieces(jnp.stack(places).astype(jnp.int32), pieces, earlier)


def plane_sum_small(array):
    parts = jnp.split(array, 2, axis=0)
    firsts = [add_low(p, plane_neighbours(p, by)) for p, by in zip(parts, (1, 2))]
    lasts = [
        p.astype(f32) + plane_neighbours(p, by).astype(f32) for p, by in zip(firsts, (2, 1))
    ]
    return jnp.concatenate(lasts, axis=0)


def plane_piece(shards, tail=None):
    rep = lax.axis_index("rep")
    pieces = []
    for shard in shards:
        rows, cols = shard.shape[0] // 2, shard.shape[1] // 2
        pieces.append(
            lax.dynamic_slice(shard, ((rep // 2) * rows, (rep % 2) * cols), (rows, cols))
        )
    if tail is not None:
        rows = tail.shape[0] // 2
        pieces.append(lax.dynamic_slice(tail, ((rep // 2) * rows, 0), (rows, tail.shape[1])))
    return jnp.concatenate(pieces, axis=1).astype(bf16)


def gather_line(piece):
    groups = lax.axis_size("exp") // 2
    lines = [[2 * z + c for z in range(groups)] for c in range(2)]
    return lax.all_to_all(
        jnp.broadcast_to(piece[None], (groups,) + piece.shape),
        "exp", split_axis=0, concat_axis=0, axis_index_groups=lines,
    )


def gather_plane(own):
    return own, *[plane_neighbours(own, by) for by in (1, 2, 3)]


def gather_cores(parts, layout, total):
    ranks = lax.axis_size("exp")
    mine = assemble(lax.axis_index("rep").reshape(1), parts, layout, total)
    other = lax.ppermute(mine, "exp", [(i, i ^ 1) for i in range(ranks)])
    return lax.rem(lax.axis_index("exp"), 2).reshape(1), mine, other


def gather_plain(shards):
    whole_rows = [lax.all_gather(s.astype(bf16), "exp", axis=0, tiled=True) for s in shards]
    joined = jnp.concatenate(whole_rows, axis=1)
    halves = joined.reshape(4, 2, joined.shape[0] // 8, joined.shape[1])
    return jnp.zeros((1,), jnp.int32), halves[:, 0], halves[:, 1]


def body(
    tokens, qkv_weight, out_weight, up_weight, down_weight, router_weight,
    first_gain, second_gain, third_gain, widening, narrowing, expert_ids, priority, cotangent,
):
    rows, width = tokens.shape
    hidden_width = up_weight.shape[1]
    ranks, reps = lax.axis_size("exp"), lax.axis_size("rep")
    experts = widening.shape[0] * ranks
    capacity = (rows + experts - 1) // experts
    half = capacity // 2
    count = experts * capacity
    pairs = width // 128
    me = lax.axis_index("exp").reshape(1)

    def reduce_dense(array):
        return lax.psum_scatter(array, "exp", scatter_dimension=0, tiled=True)

    plane = ranks == 8 and reps == 4

    choice_hot = (expert_ids[:, :, None] == jnp.arange(experts, dtype=jnp.int32)).astype(f32)
    rank_row = priority[0]
    earlier = (rank_row[None, :] < rank_row[:, None]).astype(bf16)
    ahead = dot(earlier, choice_hot.reshape(rows, -1).astype(bf16)).reshape(choice_hot.shape)
    totals = jnp.sum(choice_hot, axis=0)
    prior = jnp.cumsum(totals, axis=0) - totals
    position = jnp.sum((ahead + prior[None]) * choice_hot, axis=-1).astype(jnp.int32)
    kept = position < capacity
    slots = jnp.where(kept, expert_ids * capacity + position, -1)
    later = position >= half
    split_slots = expert_ids * half + position + jnp.where(later, experts * half - half, 0)
    split_slots = jnp.where(kept, split_slots, -1)
    slot_rows = split_slots.T
    ids_rows = expert_ids.reshape(rows // 288, 288, 2).swapaxes(1, 2)
    whole_rows = slots.T

    def exchange(array, amount):
        return lax.all_to_all(
            array.reshape(experts, amount, width), "exp", split_axis=0, concat_axis=0, tiled=True
        ).reshape(experts * amount, width)

    def both_halves(rows_in):
        return [to_slots(rows_in, slot_rows - j * (count // 2), count // 2) for j in range(2)]

    small = jnp.concatenate(
        [router_weight, first_gain[:, None], second_gain[:, None], third_gain[:, None]], axis=1
    )
    small = jnp.pad(small, ((0, 0), (0, 128 - experts - 3)))
    by_pair = qkv_weight.reshape(-1, 3, pairs, 128).swapaxes(1, 2).reshape(-1, 3 * width)
    wide, deep = width // 2, hidden_width // 2
    if plane:
        own = gather_line(plane_piece((by_pair,), small))
        pieces = gather_plane(own)
        sent_cots, narrow_low = to_slots_cast(
            after(cotangent, own, slot_rows, ids_rows, slots, split_slots),
            whole_rows, count, narrowing[0],
        )
        piece, piece_down = plane_piece((out_weight, up_weight)), plane_piece((down_weight,))
        tall = piece.shape[0]
        piece = piece.reshape(tall, -1, wide).swapaxes(0, 1).reshape(-1, wide)
        own_both = gather_line(after(jnp.concatenate([piece, piece_down], axis=0), own))
        own_next = own_both[:, : piece.shape[0]].reshape(ranks // 2, -1, tall, wide)
        own_next = own_next.swapaxes(1, 2).reshape(ranks // 2, tall, -1)
        own_down = own_both[:, piece.shape[0] :]
        qkv_w = gather_cores(
            after(pieces, own_both, sent_cots),
            ((0, 3 * wide, 0, 3 * wide), (3 * wide, 128, 3 * width, 0)), 3 * width + 128,
        )
        pieces = gather_plane(after(own_next, pieces))
        pieces_down = gather_plane(after(own_down, pieces))
    else:
        sent_cots, narrow_low = to_slots_cast(cotangent, whole_rows, count, narrowing[0])
        qkv_w = gather_plain((by_pair, small))
        out_up = gather_plain((out_weight, up_weight))
        down = gather_plain((down_weight,))

    split = pairs - 1
    qkv, probs, attended, first_low, small_t = attention_forward(
        tokens, qkv_w, experts, 0, split, pairs, None
    )
    if plane:
        out_up = gather_cores(
            after(pieces, small_t), ((0, wide, 0, wide), (wide, deep, width, deep)),
            width + hidden_width,
        )
    cots = exchange(after(sent_cots, small_t), capacity)
    gain_one, gain_two, gain_three = [(small_t, experts + k) for k in range(3)]
    qkv, probs, attended = attention_forward(
        first_low, qkv_w, experts, split, pairs - split, pairs, (qkv, probs, attended)
    )
    hidden, second_low, activ, slope, widen_low = dense_up(
        attended, tokens, out_up, gain_two, widening[0]
    )
    if plane:
        down = gather_cores(after(pieces_down, hidden), ((0, wide, 0, wide),), width)
    middle, third_low, gate_rows = dense_down(
        after(activ, cots), hidden, ids_rows, down, experts, gain_three
    )
    gates = gate_rows.swapaxes(1, 2).reshape(rows, 2)

    sent_rows = both_halves(third_low)
    cots = after(cots, third_low).reshape(experts, 2, half, width)
    cots = [cots[:, j].reshape(-1, width) for j in range(2)]
    cot_wide = [product_wide(c, narrow_low) for c in cots]
    sent_rows[1] = after(sent_rows[1], cot_wide)
    arrived = [exchange(x, half) for x in sent_rows]
    mains, y_rows = [], []
    for j in range(2):
        ready = after(arrived[j], y_rows, *[m[2] for m in mains])
        mains.append(expert_main(me, ready, widen_low, cot_wide[j], small_t, experts))
        if j == 0:
            y_rows.append(narrow_product(after(mains[j][0], mains[j][2]), narrow_low))
    z_rows, v_rows, dx_rows, slot_gates, router_parts = zip(*mains)
    dx_slots = [exchange(after(dx_rows[0], y_rows), half)]
    dx_slots.append(exchange(after(dx_rows[1], dx_slots[0]), half))
    y_rows.append(narrow_product(after(z_rows[1], dx_slots[0]), narrow_low))
    narrow_grads = narrow_outer(z_rows, after(cots, y_rows), slot_gates)
    widen_grads = widen_outer(after(arrived, narrow_grads), v_rows, slot_gates)
    narrow_sum = lax.psum(narrow_grads, "rep")
    y_sent = jnp.stack([y.reshape(experts, half, width) for y in y_rows], axis=1)

    y_slots = exchange(after(y_sent, dx_slots), capacity)

    dzl, third_part = norm_three_backward(
        after(dx_slots, widen_grads), split_slots, gates, cotangent, middle, gain_three
    )
    du, dh, second_part = dense_backward(
        dzl, slope, hidden, out_up, down, gain_two
    )
    down_grads = outer_by_left(after(activ, y_slots, du), dzl, 1024)
    down_shard = reduce_dense(down_grads)
    up_out_grads = outer_two(after(second_low, down_grads), du, attended, dh)
    up_out_shard = reduce_dense(up_out_grads)
    dh = after(dh, up_out_grads)
    halves = []
    for image in range(2):
        halves.append(attention_backward(
            image, dh, out_up, qkv, probs, attended, tokens, qkv_w, gain_one
        ))
        if image == 0:
            cut = width // 2
            order = list(range(reps))
            widen_top = lax.psum(
                widen_grads[:cut], "rep", axis_index_groups=[order[:2] + order[:1:-1]]
            )
            widen_rest = after(widen_grads, halves[0], narrow_sum)[cut:]
            widen_rest = (PlanePair if plane else lambda s: lax.psum(s, "rep"))(widen_rest)
            dh = after(dh, halves[0], narrow_sum, down_shard)
    dqkv, token_grads, first_parts = zip(*halves)
    widen_step = widen_rest.fold(dqkv) if plane else widen_rest
    token_grads = jnp.concatenate(token_grads, axis=0)
    qkv_grads = outer_pair(
        after(first_low, widen_step), dqkv, (router_parts, first_parts, second_part, third_part), 384
    )
    qkv_shard = reduce_dense(qkv_grads)
    if plane:
        widen_step = widen_rest.spread(qkv_grads)
        widen_rest.cross()
    output = combine(after(y_slots, qkv_grads, widen_step), slots, gates, middle)

    small_total = plane_sum_small if plane else (lambda s: lax.psum(s, "rep").astype(f32))
    down_sum = small_total(after(down_shard, dqkv))
    beside = [p.beside for p in widen_rest.parts] if plane else widen_rest
    up_out_sum = small_total(after(up_out_shard, qkv_grads, beside))
    up_sum, out_sum = up_out_sum[:, :hidden_width], up_out_sum[:, hidden_width:]
    narrow_out = after(narrow_sum, qkv_grads, output).astype(f32)
    qkv_shard = after(qkv_shard, output, narrow_out, down_sum, up_out_sum, widen_top)
    if plane:
        widen_top = after(widen_top, qkv_shard, [p.across for p in widen_rest.parts])
        widen_out = widen_rest.finish(cast_first(widen_top, width))
    else:
        widen_out = jnp.concatenate([widen_top, widen_rest], axis=0).astype(f32)
    qkv_sum = small_total(qkv_shard)
    small_sum = qkv_sum[:, 3 * width :]
    qkv_sum = qkv_sum[:, : 3 * width].reshape(-1, pairs, 3, 128).swapaxes(1, 2)
    qkv_sum = qkv_sum.reshape(-1, 3 * width)
    return (
        output, token_grads,
        qkv_sum, out_sum, up_sum, down_sum,
        small_sum[:, :experts], small_sum[:, experts], small_sum[:, experts + 1],
        small_sum[:, experts + 2],
        widen_out[None], narrow_out[None],
    )


def solution(mesh):
    rows_spec, exp_spec = P(("rep", "exp"), None), P("exp", None)
    return jax.shard_map(
        body,
        mesh=mesh,
        in_specs=(
            rows_spec, exp_spec, exp_spec, exp_spec, exp_spec, exp_spec,
            P("exp"), P("exp"), P("exp"), P("exp", None, None), P("exp", None, None),
            rows_spec, rows_spec, rows_spec,
        ),
        out_specs=(
            rows_spec, rows_spec, exp_spec, exp_spec, exp_spec, exp_spec, exp_spec,
            P("exp"), P("exp"), P("exp"), P("exp", None, None), P("exp", None, None),
        ),
        check_vma=False,
    )
```

```python
import jax
import jax.numpy as jnp
from jax import lax
from jax.experimental import pallas as pl
from jax.experimental.pallas import tpu as pltpu
from jax.sharding import PartitionSpec as P

PATCHES = 576
HEAD_DIM = 64
EPSILON = 1e-6
LOG2E = 1.4426950408889634
ROOT_HALF = 0.7071067811865476
INV_ROOT_2PI = 0.3989422804014327
bf16 = jnp.bfloat16
f32 = jnp.float32
params = pltpu.CompilerParams(vmem_limit_bytes=58 << 20)


def dot(left, right):
    return jnp.dot(left, right, preferred_element_type=f32)


def dot_nt(left, right):
    return lax.dot_general(left, right, (((1,), (1,)), ((), ())), preferred_element_type=f32)


def dot_tn(left, right):
    return lax.dot_general(left, right, (((0,), (0,)), ((), ())), preferred_element_type=f32)


def unit_norm(values):
    centred = values - jnp.mean(values, axis=-1, keepdims=True)
    inverse = lax.rsqrt(jnp.mean(centred * centred, axis=-1, keepdims=True) + EPSILON)
    return centred * inverse, inverse


def norm_inward(upstream, unit, inverse, gain):
    scaled = upstream * gain
    return inverse * (
        scaled
        - jnp.mean(scaled, axis=-1, keepdims=True)
        - unit * jnp.mean(scaled * unit, axis=-1, keepdims=True)
    )


def gelu_pair(u):
    half = 0.5 + 0.5 * lax.erf(u * ROOT_HALF)
    density = jnp.exp2(u * u * (-0.5 * LOG2E)) * INV_ROOT_2PI
    return u * half, half + u * density


def cost(microseconds):
    return pl.CostEstimate(
        flops=int(microseconds * 8e+08), bytes_accessed=int(microseconds * 2e+06), transcendentals=0
    )


def spec(shape, index):
    return pl.BlockSpec(shape, index)


def fixed(shape):
    zeros = (0,) * len(shape)
    return pl.BlockSpec(shape, lambda *_: zeros, pipeline_mode=pl.Buffered(1))


def shaped(shape, dtype):
    return jax.ShapeDtypeStruct(shape, dtype)


any_space = pl.BlockSpec(memory_space=pl.ANY)
scalar_space = pl.BlockSpec(memory_space=pltpu.SMEM)


def attention_forward(rows_in, weight, small, first_pair, pairs, pairs_all, earlier):
    rows, width = rows_in.shape
    images, first = rows // PATCHES, earlier is None
    cols = 384 * pairs

    def kernel(*refs):
        if first:
            (core_ref, x_ref, hw_ref, kw_ref, qkv_ref, p_ref, o_ref, a_ref, st_ref,
             w_ref, sem, sm_ref, sem_small) = refs
        else:
            (core_ref, a_ref, hw_ref, kw_ref, _, _, _, qkv_ref, p_ref, o_ref, w_ref, sem) = refs
        image, pair = pl.program_id(0), pl.program_id(1)

        @pl.when((pair == 0) & (image == 0))
        def _():
            load_halves(core_ref[0], hw_ref, kw_ref, w_ref, sem, 384 * first_pair, cols)
            if first:
                load_halves(core_ref[0], hw_ref, kw_ref, sm_ref, sem_small, 3 * width, 128)
                st_ref[...] = sm_ref[...].astype(f32).T

        if first:
            @pl.when(pair == 0)
            def _():
                unit, _ = unit_norm(x_ref[...].astype(f32))
                a_ref[...] = (unit * st_ref[small : small + 1, :]).astype(bf16)

        qkv = dot(a_ref[...], w_ref[:, pl.ds(pl.multiple_of(pair * 384, 128), 384)]).astype(bf16)
        qkv_ref[...] = qkv
        q, k, v = qkv[:, :128], qkv[:, 128:256], qkv[:, 256:]
        q = (q.astype(f32) * HEAD_DIM ** (-0.5)).astype(bf16)
        low_lane = lax.broadcasted_iota(jnp.int32, (PATCHES, 128), 1) < HEAD_DIM
        v_t = v.T
        outs = []
        for h in range(2):
            k_head = jnp.where(low_lane == (h == 0), k, jnp.zeros_like(k))
            s = dot_nt(k_head, q)
            top = jnp.max(s, axis=0, keepdims=True)
            e = jnp.exp2((s - top) * LOG2E)
            total = jnp.sum(e, axis=0, keepdims=True)
            p = (e * (1.0 / total)).astype(bf16)
            p_ref[0, h] = p
            outs.append(dot(v_t[h * HEAD_DIM : (h + 1) * HEAD_DIM], p))
        o_ref[...] = jnp.concatenate(outs, axis=0).T.astype(bf16)

    groups = weight[1].shape[0]
    by_image = spec((PATCHES, width), lambda i, j: (i, 0))
    out_specs = [
        spec((PATCHES, 384), lambda i, j: (i, j + first_pair)),
        spec((1, 2, PATCHES, PATCHES), lambda i, j: (i, j + first_pair, 0, 0)),
        spec((PATCHES, 128), lambda i, j: (i, j + first_pair)),
    ]
    out_shape = [
        shaped((rows, 384 * pairs_all), bf16),
        shaped((images, 2 * pairs_all, PATCHES, PATCHES), bf16),
        shaped((rows, 128 * pairs_all), bf16),
    ]
    in_specs = [scalar_space, by_image, any_space, any_space]
    scratch = [pltpu.VMEM((width, cols), bf16), pltpu.SemaphoreType.DMA((2, groups))]
    if first:
        out_specs += [by_image, spec((128, width), lambda i, j: (0, 0))]
        out_shape += [shaped((rows, width), bf16), shaped((128, width), f32)]
        scratch += [pltpu.VMEM((width, 128), bf16), pltpu.SemaphoreType.DMA((2, groups))]
        operands, aliases = (weight[0], rows_in, *weight[1:]), {}
    else:
        in_specs += [any_space] * 3
        operands, aliases = (weight[0], rows_in, *weight[1:], *earlier), {4: 0, 5: 1, 6: 2}
    return pl.pallas_call(
        kernel,
        name="attention_forward",
        cost_estimate=cost(8 * images * pairs // 4),
        grid=(images, pairs),
        in_specs=in_specs,
        out_specs=out_specs,
        out_shape=out_shape,
        scratch_shapes=scratch,
        input_output_aliases=aliases,
        compiler_params=params,
    )(*operands)


def attention_backward(image, dh, out_weight, qkv, probs, attended, tokens, qkv_weight, gain):
    width = dh.shape[1]
    pairs = width // 128

    def kernel(
        core_ref, dh_ref, ho_ref, ko_ref, qkv_ref, p_ref, o_ref, x_ref, hw_ref, kw_ref, g_ref,
        dq_ref, dx_ref, dg_ref, do_ref, db_ref, wo_ref, w_ref, sem, sem_w,
    ):
        pair = pl.program_id(0)

        @pl.when(pair == 0)
        def _():
            load_halves(core_ref[0], ho_ref, ko_ref, wo_ref, sem, 0, width)
            load_halves(core_ref[0], hw_ref, kw_ref, w_ref, sem_w, 0, 3 * width)

        @pl.when(pair == 0)
        def _():
            do = dot_nt(dh_ref[...], wo_ref[...]).astype(bf16)
            for j in range(pairs):
                do_ref[j] = do[:, j * 128 : (j + 1) * 128]

        q, k, v = qkv_ref[:, :128], qkv_ref[:, 128:256], qkv_ref[:, 256:]
        q = (q.astype(f32) * HEAD_DIM ** (-0.5)).astype(bf16)
        do = do_ref[pair]
        low_lane = lax.broadcasted_iota(jnp.int32, (PATCHES, 128), 1) < HEAD_DIM
        prod = do.astype(f32) * o_ref[...].astype(f32)
        prod_high = prod.astype(bf16)
        prod_low = (prod - prod_high.astype(f32)).astype(bf16)
        pick_row = lax.broadcasted_iota(jnp.int32, (16, 128), 0)
        pick_lane = lax.broadcasted_iota(jnp.int32, (16, 128), 1)
        pick = (pick_lane // HEAD_DIM == pick_row).astype(bf16)
        row_sums = dot_nt(pick, prod_high) + dot_nt(pick, prod_low)
        k_t = k.T
        dqs, dks, dvs = [], [], []
        for h in range(2):
            v_head = jnp.where(low_lane == (h == 0), v, jnp.zeros_like(v))
            dp = dot_nt(v_head, do)
            p = p_ref[0, h]
            ds = (p.astype(f32) * (dp - row_sums[h : h + 1])).astype(bf16)
            dvs.append(dot(p, do))
            dks.append(dot(ds, q))
            dqs.append(dot(k_t[h * HEAD_DIM : (h + 1) * HEAD_DIM], ds))
        dq = (jnp.concatenate(dqs, axis=0) * HEAD_DIM ** (-0.5)).T
        dqkv = jnp.concatenate(
            [dq, jnp.where(low_lane, dks[0], dks[1]), jnp.where(low_lane, dvs[0], dvs[1])], axis=1
        ).astype(bf16)
        dq_ref[...] = dqkv

        w_pair = w_ref[:, pl.ds(pl.multiple_of(pair * 384, 128), 384)]

        @pl.when(pair == 0)
        def _():
            db_ref[...] = dot_nt(dqkv, w_pair)

        @pl.when(pair > 0)
        def _():
            db_ref[...] += dot_nt(dqkv, w_pair)

        @pl.when(pair == pairs - 1)
        def _():
            upstream = db_ref[...]
            unit, inverse = unit_norm(x_ref[...].astype(f32))
            inward = norm_inward(upstream, unit, inverse, g_ref[gain[1] : gain[1] + 1, :])
            dx_ref[...] = (dh_ref[...].astype(f32) + inward).astype(bf16)
            dg_ref[...] = jnp.sum(upstream * unit, axis=0, keepdims=True)

    by_image = spec((PATCHES, width), lambda j: (image, 0))
    out_image = spec((PATCHES, width), lambda j: (0, 0))
    return pl.pallas_call(
        kernel,
        name="attention_backward",
        cost_estimate=cost(1000),
        grid=(pairs,),
        in_specs=[
            scalar_space, by_image, any_space, any_space,
            spec((PATCHES, 384), lambda j: (image, j)),
            spec((1, 2, PATCHES, PATCHES), lambda j: (image, j, 0, 0)),
            spec((PATCHES, 128), lambda j: (image, j)),
            by_image,
            any_space, any_space,
            fixed(gain[0].shape),
        ],
        out_specs=[
            spec((PATCHES, 384), lambda j: (0, j)), out_image,
            spec((1, width), lambda j: (0, 0)),
        ],
        out_shape=[
            shaped((PATCHES, 3 * width), bf16), shaped((PATCHES, width), bf16),
            shaped((1, width), f32),
        ],
        scratch_shapes=[
            pltpu.VMEM((pairs, PATCHES, 128), bf16),
            pltpu.VMEM((PATCHES, width), f32),
            pltpu.VMEM((width, width), bf16),
            pltpu.VMEM((width, 3 * width), bf16),
            pltpu.SemaphoreType.DMA((2, out_weight[1].shape[0])),
            pltpu.SemaphoreType.DMA((2, out_weight[1].shape[0])),
        ],
        compiler_params=params,
    )(out_weight[0], dh, *out_weight[1:], qkv, probs, attended, tokens, *qkv_weight[1:], gain[0])


def load_halves(core, mine_ref, other_ref, whole_ref, sem, start, cols):
    groups, rows, _ = mine_ref.shape
    copies = []
    for z in range(groups):
        for side, ref in enumerate((mine_ref, other_ref)):
            place = core if side == 0 else 1 - core
            base = pl.multiple_of((2 * z + place) * rows, 16)
            copies.append(
                pltpu.make_async_copy(
                    ref.at[z, :, pl.ds(start, cols)],
                    whole_ref.at[pl.ds(base, rows), :],
                    sem.at[side, z],
                )
            )
    for copy in copies:
        copy.start()
    for copy in copies:
        copy.wait()


def assemble(place, parts, layout, total):
    groups, rows, _ = parts[0].shape

    def kernel(r_ref, own_ref, x_ref, y_ref, far_ref, o_ref):
        down, right = r_ref[0] // 2, r_ref[0] % 2

        def put(ref, row_half, col_half):
            at = pl.multiple_of(row_half * rows, 16)
            for start, wide, base, step in layout:
                to = pl.multiple_of(base + col_half * step, 128)
                o_ref[:, pl.ds(at, rows), pl.ds(to, wide)] = ref[:, :, start : start + wide]

        put(own_ref, down, right)
        put(x_ref, down, 1 - right)
        put(y_ref, 1 - down, right)
        put(far_ref, 1 - down, 1 - right)

    return pl.pallas_call(
        kernel,
        name="assemble",
        cost_estimate=cost(4),
        in_specs=[scalar_space] + [pl.BlockSpec(memory_space=pltpu.VMEM)] * 4,
        out_specs=pl.BlockSpec(memory_space=pltpu.VMEM),
        out_shape=shaped((groups, 2 * rows, total), bf16),
        compiler_params=params,
    )(place, *parts)


def by_rows(block, cols):
    return spec((block, cols), lambda i: (i, 0))


def whole(shape):
    return spec(shape, lambda i: (0,) * len(shape))


def dense_up(attended, tokens, weights, gain, extra):
    rows, width = tokens.shape
    hidden = weights[1].shape[2] - width
    block, chunk = 288, 512
    tall, wide = extra.shape
    tall = tall * block // rows

    def kernel(
        core_ref, o_ref, x_ref, hw_ref, kw_ref, g_ref, e_ref,
        h_ref, b_ref, z_ref, s_ref, low_ref, w_ref, sem,
    ):
        @pl.when(pl.program_id(0) == 0)
        def _():
            load_halves(core_ref[0], hw_ref, kw_ref, w_ref, sem, 0, width + hidden)

        low_ref[...] = e_ref[...].astype(bf16)
        h = x_ref[...].astype(f32) + dot(o_ref[...], w_ref[:, :width])
        h = h.astype(bf16)
        h_ref[...] = h
        h = h.astype(f32)
        b = (unit_norm(h)[0] * g_ref[gain[1] : gain[1] + 1, :]).astype(bf16)
        b_ref[...] = b
        ahead = dot(b, w_ref[:, width : width + chunk])
        for c in range(0, hidden, chunk):
            u = ahead
            if c + chunk < hidden:
                ahead = dot(b, w_ref[:, width + c + chunk : width + c + 2 * chunk])
            z, slope = gelu_pair(u)
            z_ref[:, c : c + chunk] = z.astype(bf16)
            s_ref[:, c : c + chunk] = slope.astype(bf16)

    return pl.pallas_call(
        kernel,
        name="dense_up",
        cost_estimate=cost(18),
        grid=(rows // block,),
        in_specs=[
            scalar_space, by_rows(block, width), by_rows(block, width), any_space, any_space,
            fixed(gain[0].shape), by_rows(tall, wide),
        ],
        out_specs=[
            by_rows(block, width), by_rows(block, width), by_rows(block, hidden),
            by_rows(block, hidden), by_rows(tall, wide),
        ],
        out_shape=[
            shaped((rows, width), bf16), shaped((rows, width), bf16),
            shaped((rows, hidden), bf16), shaped((rows, hidden), bf16),
            shaped(extra.shape, bf16),
        ],
        scratch_shapes=[
            pltpu.VMEM((width, width + hidden), bf16),
            pltpu.SemaphoreType.DMA((2, weights[1].shape[0])),
        ],
        compiler_params=params,
    )(weights[0], attended, tokens, *weights[1:], gain[0], extra)


def dense_down(activ, hidden_rows, ids, weights, experts, gain):
    rows, width = hidden_rows.shape
    hidden = activ.shape[1]
    block = 288

    def kernel(
        core_ref, z_ref, h_ref, id_ref, hw_ref, kw_ref, g_ref,
        y_ref, m_ref, gate_ref, w_ref, sem,
    ):
        @pl.when(pl.program_id(0) == 0)
        def _():
            load_halves(core_ref[0], hw_ref, kw_ref, w_ref, sem, 0, width)

        y = h_ref[...].astype(f32) + dot(z_ref[...], w_ref[...])
        y_ref[...] = y.astype(bf16)
        m = (unit_norm(y)[0] * g_ref[gain[1] : gain[1] + 1, :]).astype(bf16)
        m_ref[...] = m
        logits = dot_nt(g_ref[:experts, :].astype(bf16), m)
        e = jnp.exp(logits - jnp.max(logits, axis=0, keepdims=True))
        p = e / jnp.sum(e, axis=0, keepdims=True)
        line = lax.broadcasted_iota(jnp.int32, (experts, block), 0)
        for k in range(2):
            hot = line == id_ref[0, k : k + 1, :]
            gate_ref[0, k : k + 1, :] = jnp.sum(jnp.where(hot, p, 0.0), axis=0, keepdims=True)

    return pl.pallas_call(
        kernel,
        name="dense_down",
        cost_estimate=cost(15),
        grid=(rows // block,),
        in_specs=[
            scalar_space, by_rows(block, hidden), by_rows(block, width),
            spec((1, 2, block), lambda i: (i, 0, 0)),
            any_space, any_space, fixed(gain[0].shape),
        ],
        out_specs=[
            by_rows(block, width), by_rows(block, width),
            spec((1, 2, block), lambda i: (i, 0, 0)),
        ],
        out_shape=[
            shaped((rows, width), bf16), shaped((rows, width), bf16),
            shaped((rows // block, 2, block), f32),
        ],
        scratch_shapes=[
            pltpu.VMEM((hidden, width), bf16),
            pltpu.SemaphoreType.DMA((2, weights[1].shape[0])),
        ],
        compiler_params=params,
    )(weights[0], activ, hidden_rows, ids, *weights[1:], gain[0])


def gated_rows(slot_ref, gate_ref, slots_refs, block):
    total, base = None, 0
    for ref in slots_refs:
        count = ref.shape[0]
        lane = base + lax.broadcasted_iota(jnp.int32, (block, count), 1)
        weighted = jnp.zeros((block, count), f32)
        for k in range(2):
            hot = lane == slot_ref[:, k : k + 1]
            weighted = weighted + jnp.where(hot, gate_ref[:, k : k + 1], 0.0)
        part = dot(weighted.astype(bf16), ref[...])
        total = part if total is None else total + part
        base += count
    return total


def norm_three_backward(dx_slots, slots, gates, cotangent, middle, gain):
    rows, width = cotangent.shape
    block = 288

    def kernel(da_ref, db_ref, slot_ref, gate_ref, cot_ref, y_ref, g_ref, dzl_ref, dg_ref):
        dm = gated_rows(slot_ref, gate_ref, (da_ref, db_ref), block)
        unit, inverse = unit_norm(y_ref[...].astype(f32))
        part = jnp.sum(dm * unit, axis=0, keepdims=True)
        dy = cot_ref[...].astype(f32) + norm_inward(dm, unit, inverse, g_ref[gain[1] : gain[1] + 1, :])
        dzl_ref[...] = dy.astype(bf16)
        first = pl.program_id(0) == 0

        @pl.when(first)
        def _():
            dg_ref[...] = part

        @pl.when(jnp.logical_not(first))
        def _():
            dg_ref[...] += part

    return pl.pallas_call(
        kernel,
        name="norm_three_backward",
        cost_estimate=cost(10),
        grid=(rows // block,),
        in_specs=[
            fixed(dx_slots[0].shape), fixed(dx_slots[1].shape), by_rows(block, 2),
            by_rows(block, 2), by_rows(block, width), by_rows(block, width), fixed(gain[0].shape),
        ],
        out_specs=[by_rows(block, width), whole((1, width))],
        out_shape=[shaped((rows, width), bf16), shaped((1, width), f32)],
        compiler_params=params,
    )(*dx_slots, slots, gates, cotangent, middle, gain[0])


def dense_backward(dzl, slope, hidden_rows, up_weight, down_weight, gain):
    rows, width = dzl.shape
    hidden = slope.shape[1]
    block, chunk = 288, 512

    def kernel(
        core_ref, dzl_ref, s_ref, h_ref, hu_ref, ku_ref, hd_ref, kd_ref, g_ref,
        du_ref, dhl_ref, dg_ref, w1_ref, w2_ref, sem,
    ):
        first = pl.program_id(0) == 0

        @pl.when(first)
        def _():
            load_halves(core_ref[0], hd_ref, kd_ref, w2_ref, sem, 0, width)
            load_halves(core_ref[0], hu_ref, ku_ref, w1_ref, sem, width, hidden)

        dzl = dzl_ref[...]
        db = jnp.zeros((block, width), f32)
        ahead = dot_nt(dzl, w2_ref[:chunk, :])
        for c in range(0, hidden, chunk):
            dz = ahead
            if c + chunk < hidden:
                ahead = dot_nt(dzl, w2_ref[c + chunk : c + 2 * chunk, :])
            du = (dz * s_ref[:, c : c + chunk].astype(f32)).astype(bf16)
            du_ref[:, c : c + chunk] = du
            db = db + dot_nt(du, w1_ref[:, c : c + chunk])
        unit, inverse = unit_norm(h_ref[...].astype(f32))
        part = jnp.sum(db * unit, axis=0, keepdims=True)
        dh = dzl.astype(f32) + norm_inward(db, unit, inverse, g_ref[gain[1] : gain[1] + 1, :])
        dhl_ref[...] = dh.astype(bf16)

        @pl.when(first)
        def _():
            dg_ref[...] = part

        @pl.when(jnp.logical_not(first))
        def _():
            dg_ref[...] += part

    return pl.pallas_call(
        kernel,
        name="dense_backward",
        cost_estimate=cost(24),
        grid=(rows // block,),
        in_specs=[
            scalar_space, by_rows(block, width), by_rows(block, hidden),
            by_rows(block, width), any_space, any_space, any_space, any_space, fixed(gain[0].shape),
        ],
        out_specs=[
            by_rows(block, hidden), by_rows(block, width), whole((1, width)),
        ],
        out_shape=[
            shaped((rows, hidden), bf16), shaped((rows, width), bf16), shaped((1, width), f32),
        ],
        scratch_shapes=[
            pltpu.VMEM((width, hidden), bf16), pltpu.VMEM((hidden, width), bf16),
            pltpu.SemaphoreType.DMA((2, up_weight[1].shape[0])),
        ],
        compiler_params=params,
    )(up_weight[0], dzl, slope, hidden_rows, *up_weight[1:], *down_weight[1:], gain[0])


def combine(y_slots, slots, gates, middle):
    rows, width = middle.shape
    block = 288

    def kernel(ya_ref, slot_ref, gate_ref, y_ref, o_ref):
        o_ref[...] = (
            y_ref[...].astype(f32) + gated_rows(slot_ref, gate_ref, (ya_ref,), block)
        ).astype(bf16)

    return pl.pallas_call(
        kernel,
        name="combine",
        cost_estimate=cost(8),
        grid=(rows // block,),
        in_specs=[
            fixed(y_slots.shape), by_rows(block, 2), by_rows(block, 2), by_rows(block, width),
        ],
        out_specs=by_rows(block, width),
        out_shape=shaped((rows, width), bf16),
        compiler_params=params,
    )(y_slots, slots, gates, middle)


def expert_main(me, rows_in, widen_low, cot_wide, small_t, experts):
    rows, width = rows_in.shape
    hidden = widen_low.shape[1]
    chunk, part = 1024, 512
    steps = hidden // chunk

    def kernel(
        me_ref, x_ref, a_ref, u_ref, wr_ref,
        z_ref, v_ref, dx_ref, gate_ref, dwr_ref, acc_ref, dg_ref,
    ):
        step = pl.program_id(0)

        @pl.when(step == 0)
        def _():
            acc_ref[...] = jnp.zeros_like(acc_ref)
            dg_ref[...] = jnp.zeros_like(dg_ref)

        x = x_ref[...]
        ahead = dot(x, a_ref[:, :part])
        sums = jnp.zeros((rows, 128), f32)
        for c in range(0, chunk, part):
            cols = slice(c, c + part)
            r = ahead
            if c + part < chunk:
                ahead = dot(x, a_ref[:, c + part : c + 2 * part])
            z, slope = gelu_pair(r)
            u = u_ref[:, cols].astype(f32)
            v = (u * slope).astype(bf16)
            z_ref[:, cols] = z.astype(bf16)
            v_ref[:, cols] = v
            dg = u * z
            sums = sums + sum(dg[:, q : q + 128] for q in range(0, part, 128))
            acc_ref[...] += dot_nt(v, a_ref[:, cols])
        dg_ref[...] += sums

        @pl.when(step == steps - 1)
        def _():
            wr = wr_ref[:experts, :].astype(bf16)
            logits = dot_nt(wr, x)
            e = jnp.exp(logits - jnp.max(logits, axis=0, keepdims=True))
            p = e / jnp.sum(e, axis=0, keepdims=True)
            own = lax.broadcasted_iota(jnp.int32, (experts, rows), 0) == me_ref[0]
            gate = jnp.sum(jnp.where(own, p, 0.0), axis=0, keepdims=True)
            gate_ref[...] = jnp.broadcast_to(gate, (128, rows)).T[:, :1]
            dgate = jnp.sum(dg_ref[...].T, axis=0, keepdims=True)
            spread = dgate * (own.astype(f32) - p)
            dx_ref[...] = (acc_ref[...] + dot_tn(spread.astype(bf16), wr)).astype(bf16)
            dwr_ref[...] = dot((gate * spread).astype(bf16), x)

    by_col = spec((rows, chunk), lambda i: (0, i))
    return pl.pallas_call(
        kernel,
        name="expert_main",
        cost_estimate=cost(15),
        grid=(steps,),
        in_specs=[
            scalar_space, fixed((rows, width)), spec((width, chunk), lambda i: (0, i)), by_col,
            fixed(small_t.shape),
        ],
        out_specs=[by_col, by_col, whole((rows, width)), whole((rows, 1)), whole((experts, width))],
        out_shape=[
            shaped((rows, hidden), bf16), shaped((rows, hidden), bf16),
            shaped((rows, width), bf16), shaped((rows, 1), f32), shaped((experts, width), f32),
        ],
        scratch_shapes=[pltpu.VMEM((rows, width), f32), pltpu.VMEM((rows, 128), f32)],
        compiler_params=params,
    )(me, rows_in, widen_low, cot_wide, small_t)


def narrow_outer(activs, cots, gates):
    rows, width = cots[0].shape
    hidden = activs[0].shape[1]
    chunk = 1024

    def kernel(za_ref, zb_ref, ca_ref, cb_ref, ga_ref, gb_ref, o_ref, da_ref, db_ref):
        @pl.when(pl.program_id(0) == 0)
        def _():
            da_ref[...] = (ca_ref[...].astype(f32) * ga_ref[...]).astype(bf16)
            db_ref[...] = (cb_ref[...].astype(f32) * gb_ref[...]).astype(bf16)

        o_ref[...] = (
            dot_tn(za_ref[...], da_ref[...]) + dot_tn(zb_ref[...], db_ref[...])
        ).astype(bf16)

    by_col = spec((rows, chunk), lambda i: (0, i))
    return pl.pallas_call(
        kernel,
        name="narrow_outer",
        cost_estimate=cost(12),
        grid=(hidden // chunk,),
        in_specs=[by_col, by_col] + [fixed((rows, width))] * 2 + [fixed((rows, 1))] * 2,
        out_specs=spec((chunk, width), lambda i: (i, 0)),
        out_shape=shaped((hidden, width), bf16),
        scratch_shapes=[pltpu.VMEM((rows, width), bf16)] * 2,
        compiler_params=params,
    )(*activs, *cots, *gates)


def widen_outer(rows_in, slopes, gates):
    rows, width = rows_in[0].shape
    hidden = slopes[0].shape[1]
    chunk = 1024

    def kernel(xa_ref, xb_ref, va_ref, vb_ref, ga_ref, gb_ref, o_ref, da_ref, db_ref):
        @pl.when(pl.program_id(0) == 0)
        def _():
            da_ref[...] = (xa_ref[...].astype(f32) * ga_ref[...]).astype(bf16)
            db_ref[...] = (xb_ref[...].astype(f32) * gb_ref[...]).astype(bf16)

        o_ref[...] = (
            dot_tn(da_ref[...], va_ref[...]) + dot_tn(db_ref[...], vb_ref[...])
        ).astype(bf16)

    by_col = spec((rows, chunk), lambda i: (0, i))
    return pl.pallas_call(
        kernel,
        name="widen_outer",
        cost_estimate=cost(12),
        grid=(hidden // chunk,),
        in_specs=[fixed((rows, width))] * 2 + [by_col, by_col] + [fixed((rows, 1))] * 2,
        out_specs=spec((width, chunk), lambda i: (0, i)),
        out_shape=shaped((width, hidden), bf16),
        scratch_shapes=[pltpu.VMEM((rows, width), bf16)] * 2,
        compiler_params=params,
    )(*rows_in, *slopes, *gates)


def narrow_product(activ, narrow_low):
    rows, hidden = activ.shape
    width = narrow_low.shape[1]
    block = rows // 2

    def kernel(z_ref, w_ref, o_ref):
        o_ref[...] = dot(z_ref[...], w_ref[...]).astype(bf16)

    return pl.pallas_call(
        kernel,
        name="narrow_product",
        cost_estimate=cost(6),
        grid=(2,),
        in_specs=[by_rows(block, hidden), fixed((hidden, width))],
        out_specs=by_rows(block, width),
        out_shape=shaped((rows, width), bf16),
        compiler_params=params,
    )(activ, narrow_low)


def outer_pair(left, rights, small_parts, chunk):
    half, cols = rights[0].shape
    mine = left.shape[1]
    blocks = cols // chunk
    routers, firsts, second, third = small_parts
    experts = routers[0].shape[0]

    def kernel(l_ref, a_ref, b_ref, ra_ref, rb_ref, fa_ref, fb_ref, s_ref, t_ref, o_ref, rows_ref):
        step = pl.program_id(0)

        @pl.when(step < blocks)
        def _():
            o_ref[...] = (
                dot_tn(l_ref[:half], a_ref[...]) + dot_tn(l_ref[half:], b_ref[...])
            ).astype(bf16)

        @pl.when(step == blocks)
        def _():
            rows_ref[...] = jnp.zeros_like(rows_ref)
            rows_ref[:experts] = ra_ref[...] + rb_ref[...]
            rows_ref[experts : experts + 1] = fa_ref[...] + fb_ref[...]
            rows_ref[experts + 1 : experts + 2] = s_ref[...]
            rows_ref[experts + 2 : experts + 3] = t_ref[...]
            o_ref[:, :128] = rows_ref[...].T.astype(bf16)
            o_ref[:, 128:] = jnp.zeros((mine, chunk - 128), bf16)

    by_col = spec((half, chunk), lambda i: (0, jnp.minimum(i, blocks - 1)))
    return pl.pallas_call(
        kernel,
        name="outer_pair",
        cost_estimate=cost(10),
        grid=(blocks + 1,),
        in_specs=[fixed((2 * half, mine)), by_col, by_col]
        + [fixed((experts, mine))] * 2 + [fixed((1, mine))] * 4,
        out_specs=spec((mine, chunk), lambda i: (0, i)),
        out_shape=shaped((mine, cols + chunk), bf16),
        scratch_shapes=[pltpu.VMEM((128, mine), f32)],
        compiler_params=params,
    )(left, *rights, *routers, *firsts, second, third)


def place_pieces(place, pieces, total):
    rows, cols = pieces[0].shape
    amount = len(pieces)

    def kernel(place_ref, *refs):
        for k in range(amount):

            @pl.when(pl.program_id(0) == k)
            def _():
                refs[amount][...] = refs[k][...].astype(f32)

    return pl.pallas_call(
        kernel,
        name="place_pieces",
        cost_estimate=cost(5),
        grid_spec=pltpu.PrefetchScalarGridSpec(
            num_scalar_prefetch=1,
            grid=(amount,),
            in_specs=[pl.BlockSpec((rows, cols), lambda i, p: (0, 0))] * amount,
            out_specs=pl.BlockSpec((rows, cols), lambda i, p: (p[i], 0)),
        ),
        out_shape=shaped((total, cols), f32),
        compiler_params=params,
    )(place, *pieces)


def cast_first(array, earlier):
    rows, cols = array.shape
    block = rows // 4

    def kernel(a_ref, _, o_ref):
        o_ref[...] = a_ref[...].astype(f32)

    return pl.pallas_call(
        kernel,
        name="cast_first",
        cost_estimate=cost(3),
        grid=(4,),
        in_specs=[by_rows(block, cols), any_space],
        out_specs=by_rows(block, cols),
        out_shape=shaped(earlier.shape, f32),
        input_output_aliases={1: 0},
        compiler_params=params,
    )(array, earlier)


def to_slots_cast(rows_in, slot_rows, count, weight):
    rows, width = rows_in.shape
    block = 288
    steps = count // block
    tall, wide = weight.shape

    def kernel(r_ref, s_ref, w_ref, o_ref, low_ref):
        base = pl.program_id(0) * block
        line = base + lax.broadcasted_iota(jnp.int32, (block, rows), 0)
        hot = (line == s_ref[0:1, :]) | (line == s_ref[1:2, :])
        o_ref[...] = dot(hot.astype(bf16), r_ref[...]).astype(bf16)
        low_ref[...] = w_ref[...].astype(bf16)

    return pl.pallas_call(
        kernel,
        name="to_slots_cast",
        cost_estimate=cost(20),
        grid=(steps,),
        in_specs=[fixed((rows, width)), fixed((2, rows)), by_rows(tall // steps, wide)],
        out_specs=[by_rows(block, width), by_rows(tall // steps, wide)],
        out_shape=[shaped((count, width), bf16), shaped((tall, wide), bf16)],
        compiler_params=params,
    )(rows_in, slot_rows, weight)


def outer_two(left, right, left_last, right_last):
    rows, mine = left.shape
    chunk = right_last.shape[1]
    blocks = right.shape[1] // chunk

    def kernel(l_ref, r_ref, ll_ref, rl_ref, o_ref):
        step = pl.program_id(0)

        @pl.when(step < blocks)
        def _():
            o_ref[...] = dot_tn(l_ref[...], r_ref[...]).astype(bf16)

        @pl.when(step == blocks)
        def _():
            o_ref[...] = dot_tn(ll_ref[...], rl_ref[...]).astype(bf16)

    return pl.pallas_call(
        kernel,
        name="outer_two",
        cost_estimate=cost(15),
        grid=(blocks + 1,),
        in_specs=[
            fixed((rows, mine)),
            spec((rows, chunk), lambda i: (0, jnp.minimum(i, blocks - 1))),
            fixed((rows, mine)), fixed((rows, chunk)),
        ],
        out_specs=spec((mine, chunk), lambda i: (0, i)),
        out_shape=shaped((mine, chunk * (blocks + 1)), bf16),
        compiler_params=params,
    )(left, right, left_last, right_last)


def to_slots(rows_in, slot_rows, count):
    rows, width = rows_in.shape
    block = 288

    def kernel(r_ref, s_ref, o_ref):
        base = pl.program_id(0) * block
        line = base + lax.broadcasted_iota(jnp.int32, (block, rows), 0)
        hot = (line == s_ref[0:1, :]) | (line == s_ref[1:2, :])
        o_ref[...] = dot(hot.astype(bf16), r_ref[...]).astype(bf16)

    return pl.pallas_call(
        kernel,
        name="to_slots",
        cost_estimate=cost(4),
        grid=(count // block,),
        in_specs=[fixed((rows, width)), fixed((2, rows))],
        out_specs=spec((block, width), lambda i: (i, 0)),
        out_shape=shaped((count, width), bf16),
        compiler_params=params,
    )(rows_in, slot_rows)


def product_wide(left, right_t, chunk=1024):
    rows, depth = left.shape
    cols = right_t.shape[0]

    def kernel(l_ref, r_ref, o_ref):
        o_ref[...] = dot_nt(l_ref[...], r_ref[...]).astype(bf16)

    return pl.pallas_call(
        kernel,
        name="product_wide",
        cost_estimate=cost(7),
        grid=(cols // chunk,),
        in_specs=[fixed((rows, depth)), spec((chunk, depth), lambda i: (i, 0))],
        out_specs=spec((rows, chunk), lambda i: (0, i)),
        out_shape=shaped((rows, cols), bf16),
        compiler_params=params,
    )(left, right_t)


def outer_by_right(left, right, chunk):
    rows, mine = left.shape
    cols = right.shape[1]

    def kernel(l_ref, r_ref, o_ref):
        o_ref[...] = dot_tn(l_ref[...], r_ref[...]).astype(bf16)

    return pl.pallas_call(
        kernel,
        name="outer_by_right",
        cost_estimate=cost(10),
        grid=(cols // chunk,),
        in_specs=[fixed((rows, mine)), spec((rows, chunk), lambda i: (0, i))],
        out_specs=spec((mine, chunk), lambda i: (0, i)),
        out_shape=shaped((mine, cols), bf16),
        compiler_params=params,
    )(left, right)


def outer_by_left(left, right, chunk):
    rows, mine = left.shape
    cols = right.shape[1]

    def kernel(l_ref, r_ref, o_ref):
        o_ref[...] = dot_tn(l_ref[...], r_ref[...]).astype(bf16)

    return pl.pallas_call(
        kernel,
        name="outer_by_left",
        cost_estimate=cost(10),
        grid=(mine // chunk,),
        in_specs=[spec((rows, chunk), lambda i: (0, i)), fixed((rows, cols))],
        out_specs=spec((chunk, cols), lambda i: (i, 0)),
        out_shape=shaped((mine, cols), bf16),
        compiler_params=params,
    )(left, right)


def plane_neighbours(array, by):
    return lax.ppermute(array, "rep", [(i, i ^ by) for i in range(4)])


def after(value, *others):
    return lax.optimization_barrier((value, *others))[0]


def add_low(left, right):
    return (left.astype(f32) + right.astype(f32)).astype(bf16)


class PlaneSum:
    def __init__(self, array, first):
        self.first, self.second = first, 3 - first
        rep = lax.axis_index("rep")
        self.near, self.far = lax.rem(rep // first, 2), lax.rem(rep // self.second, 2)
        self.kept, self.got = self.exchange_half(array, self.near, first)

    def exchange_half(self, whole, bit, by):
        halves = whole.reshape(2, whole.shape[0] // 2, whole.shape[1])
        kept = lax.dynamic_index_in_dim(halves, bit, 0, False)
        sent = lax.dynamic_index_in_dim(halves, 1 - bit, 0, False)
        return kept, plane_neighbours(sent, by)

    def fold(self, *before):
        self.kept, self.got = after((self.kept, self.got), *before)
        half = add_low(self.kept, self.got)
        self.kept, self.got = self.exchange_half(half, self.far, self.second)
        return half

    def spread(self, *before):
        self.kept, self.got = after((self.kept, self.got), *before)
        self.own = add_low(self.kept, self.got)
        self.beside = plane_neighbours(self.own, self.second)
        return self.own

    def cross(self, *before):
        self.beside = after(self.beside, *before)
        self.across = [plane_neighbours(p, self.first) for p in (self.own, self.beside)]
        return self.beside

    def pieces(self):
        low, high = 2 * self.near + self.far, 2 * (1 - self.near) + self.far
        flip = 1 - 2 * self.far
        return [low, low + flip, high, high + flip], [self.own, self.beside, *self.across]


class PlanePair:
    def __init__(self, array):
        half = array.shape[0] // 2
        self.parts = [PlaneSum(array[:half], 1), PlaneSum(array[half:], 2)]

    def fold(self, *before):
        return [p.fold(*before) for p in self.parts]

    def spread(self, *before):
        return [p.spread(*before) for p in self.parts]

    def cross(self, *before):
        return [p.cross(*before) for p in self.parts]

    def finish(self, total):
        places, pieces = [], []
        base = total // self.parts[0].own.shape[0] - 8
        for start, part in zip((base, base + 4), self.parts):
            where, what = part.pieces()
            places += [start + w for w in where]
            pieces += what
        return place_pieces(jnp.stack(places).astype(jnp.int32), pieces, total)


def plane_sum_small(array, *before):
    parts = jnp.split(array, 2, axis=0)
    firsts = [add_low(p, plane_neighbours(p, by)) for p, by in zip(parts, (1, 2))]
    others = [plane_neighbours(p, by) for p, by in zip(firsts, (2, 1))]
    if before:
        others = after(others, *before)
    lasts = [p.astype(f32) + q.astype(f32) for p, q in zip(firsts, others)]
    return jnp.concatenate(lasts, axis=0)


def plane_piece(shards, tail=None):
    rep = lax.axis_index("rep")
    pieces = []
    for shard in shards:
        rows, cols = shard.shape[0] // 2, shard.shape[1] // 2
        pieces.append(
            lax.dynamic_slice(shard, ((rep // 2) * rows, (rep % 2) * cols), (rows, cols))
        )
    if tail is not None:
        rows = tail.shape[0] // 2
        pieces.append(lax.dynamic_slice(tail, ((rep // 2) * rows, 0), (rows, tail.shape[1])))
    return jnp.concatenate(pieces, axis=1).astype(bf16)


def gather_line(piece):
    groups = lax.axis_size("exp") // 2
    lines = [[2 * z + c for z in range(groups)] for c in range(2)]
    return lax.all_to_all(
        jnp.broadcast_to(piece[None], (groups,) + piece.shape),
        "exp", split_axis=0, concat_axis=0, axis_index_groups=lines,
    )


def gather_plane(own):
    return own, *[plane_neighbours(own, by) for by in (1, 2, 3)]


def gather_cores(parts, layout, total):
    ranks = lax.axis_size("exp")
    mine = assemble(lax.axis_index("rep").reshape(1), parts, layout, total)
    other = lax.ppermute(mine, "exp", [(i, i ^ 1) for i in range(ranks)])
    return lax.rem(lax.axis_index("exp"), 2).reshape(1), mine, other


def gather_plain(shards):
    whole_rows = [lax.all_gather(s.astype(bf16), "exp", axis=0, tiled=True) for s in shards]
    joined = jnp.concatenate(whole_rows, axis=1)
    halves = joined.reshape(4, 2, joined.shape[0] // 8, joined.shape[1])
    return jnp.zeros((1,), jnp.int32), halves[:, 0], halves[:, 1]


def body(
    tokens, qkv_weight, out_weight, up_weight, down_weight, router_weight,
    first_gain, second_gain, third_gain, widening, narrowing, expert_ids, priority, cotangent,
):
    rows, width = tokens.shape
    hidden_width = up_weight.shape[1]
    ranks, reps = lax.axis_size("exp"), lax.axis_size("rep")
    experts = widening.shape[0] * ranks
    capacity = (rows + experts - 1) // experts
    half = capacity // 2
    count = experts * capacity
    pairs = width // 128
    me = lax.axis_index("exp").reshape(1)

    def reduce_dense(array):
        return lax.psum_scatter(array, "exp", scatter_dimension=0, tiled=True)

    plane = ranks == 8 and reps == 4

    choice_hot = (expert_ids[:, :, None] == jnp.arange(experts, dtype=jnp.int32)).astype(f32)
    rank_row = priority[0]
    earlier = (rank_row[None, :] < rank_row[:, None]).astype(bf16)
    ahead = dot(earlier, choice_hot.reshape(rows, -1).astype(bf16)).reshape(choice_hot.shape)
    totals = jnp.sum(choice_hot, axis=0)
    prior = jnp.cumsum(totals, axis=0) - totals
    position = jnp.sum((ahead + prior[None]) * choice_hot, axis=-1).astype(jnp.int32)
    kept = position < capacity
    slots = jnp.where(kept, expert_ids * capacity + position, -1)
    later = position >= half
    split_slots = expert_ids * half + position + jnp.where(later, experts * half - half, 0)
    split_slots = jnp.where(kept, split_slots, -1)
    slot_rows = split_slots.T
    ids_rows = expert_ids.reshape(rows // 288, 288, 2).swapaxes(1, 2)
    whole_rows = slots.T

    def exchange(array, amount):
        return lax.all_to_all(
            array.reshape(experts, amount, width), "exp", split_axis=0, concat_axis=0, tiled=True
        ).reshape(experts * amount, width)

    def both_halves(rows_in):
        return [to_slots(rows_in, slot_rows - j * (count // 2), count // 2) for j in range(2)]

    small = jnp.concatenate(
        [router_weight, first_gain[:, None], second_gain[:, None], third_gain[:, None]], axis=1
    )
    small = jnp.pad(small, ((0, 0), (0, 128 - experts - 3)))
    by_pair = qkv_weight.reshape(-1, 3, pairs, 128).swapaxes(1, 2).reshape(-1, 3 * width)
    wide, deep = width // 2, hidden_width // 2
    if plane:
        own = gather_line(plane_piece((by_pair,), small))
        pieces = gather_plane(own)
        sent_cots, narrow_low = to_slots_cast(
            after(cotangent, own, slot_rows, ids_rows, slots, split_slots),
            whole_rows, count, narrowing[0],
        )
        piece, piece_down = plane_piece((out_weight, up_weight)), plane_piece((down_weight,))
        tall = piece.shape[0]
        piece = piece.reshape(tall, -1, wide).swapaxes(0, 1).reshape(-1, wide)
        own_both = gather_line(after(jnp.concatenate([piece, piece_down], axis=0), own))
        own_next = own_both[:, : piece.shape[0]].reshape(ranks // 2, -1, tall, wide)
        own_next = own_next.swapaxes(1, 2).reshape(ranks // 2, tall, -1)
        own_down = own_both[:, piece.shape[0] :]
        qkv_w = gather_cores(
            after(pieces, own_both, sent_cots),
            ((0, 3 * wide, 0, 3 * wide), (3 * wide, 128, 3 * width, 0)), 3 * width + 128,
        )
        pieces = gather_plane(after(own_next, pieces))
        pieces_down = gather_plane(after(own_down, pieces))
    else:
        sent_cots, narrow_low = to_slots_cast(cotangent, whole_rows, count, narrowing[0])
        qkv_w = gather_plain((by_pair, small))
        out_up = gather_plain((out_weight, up_weight))
        down = gather_plain((down_weight,))

    split = pairs - 1
    qkv, probs, attended, first_low, small_t = attention_forward(
        tokens, qkv_w, experts, 0, split, pairs, None
    )
    if plane:
        out_up = gather_cores(
            after(pieces, small_t), ((0, wide, 0, wide), (wide, deep, width, deep)),
            width + hidden_width,
        )
    cots = exchange(after(sent_cots, small_t), capacity)
    gain_one, gain_two, gain_three = [(small_t, experts + k) for k in range(3)]
    qkv, probs, attended = attention_forward(
        first_low, qkv_w, experts, split, pairs - split, pairs, (qkv, probs, attended)
    )
    hidden, second_low, activ, slope, widen_low = dense_up(
        attended, tokens, out_up, gain_two, widening[0]
    )
    if plane:
        down = gather_cores(after(pieces_down, hidden), ((0, wide, 0, wide),), width)
    middle, third_low, gate_rows = dense_down(
        after(activ, cots), hidden, ids_rows, down, experts, gain_three
    )
    gates = gate_rows.swapaxes(1, 2).reshape(rows, 2)

    sent_rows = both_halves(third_low)
    cots = after(cots, third_low).reshape(experts, 2, half, width)
    cots = [cots[:, j].reshape(-1, width) for j in range(2)]
    cot_wide = [product_wide(c, narrow_low) for c in cots]
    sent_rows[1] = after(sent_rows[1], cot_wide)
    arrived = [exchange(x, half) for x in sent_rows]
    mains, y_rows = [], []
    for j in range(2):
        ready = after(arrived[j], y_rows, *[m[2] for m in mains])
        mains.append(expert_main(me, ready, widen_low, cot_wide[j], small_t, experts))
        if j == 0:
            y_rows.append(narrow_product(after(mains[j][0], mains[j][2]), narrow_low))
    z_rows, v_rows, dx_rows, slot_gates, router_parts = zip(*mains)
    dx_slots = [exchange(after(dx_rows[0], y_rows), half)]
    dx_slots.append(exchange(after(dx_rows[1], dx_slots[0]), half))
    y_rows.append(narrow_product(after(z_rows[1], dx_slots[0]), narrow_low))
    narrow_grads = narrow_outer(z_rows, after(cots, y_rows), slot_gates)
    widen_grads = widen_outer(after(arrived, narrow_grads), v_rows, slot_gates)
    narrow_sum = lax.psum(narrow_grads, "rep")
    y_sent = jnp.stack([y.reshape(experts, half, width) for y in y_rows], axis=1)

    y_slots = exchange(after(y_sent, dx_slots), capacity)

    dzl, third_part = norm_three_backward(
        after(dx_slots, widen_grads), split_slots, gates, cotangent, middle, gain_three
    )
    du, dh, second_part = dense_backward(
        dzl, slope, hidden, out_up, down, gain_two
    )
    down_grads = outer_by_left(after(activ, y_slots, du), dzl, 1024)
    down_shard = reduce_dense(down_grads)
    up_out_grads = outer_two(after(second_low, down_grads), du, attended, dh)
    up_out_shard = reduce_dense(up_out_grads)
    dh = after(dh, up_out_grads)
    halves = []
    for image in range(2):
        halves.append(attention_backward(
            image, dh, out_up, qkv, probs, attended, tokens, qkv_w, gain_one
        ))
        if image == 0:
            cut = width // 2
            order = list(range(reps))
            widen_top = lax.psum(
                widen_grads[:cut], "rep", axis_index_groups=[order[:2] + order[:1:-1]]
            )
            widen_rest = after(widen_grads, halves[0], narrow_sum)[cut:]
            widen_rest = (PlanePair if plane else lambda s: lax.psum(s, "rep"))(widen_rest)
            dh = after(dh, halves[0], narrow_sum, down_shard)
    dqkv, token_grads, first_parts = zip(*halves)
    widen_step = widen_rest.fold(dqkv) if plane else widen_rest
    token_grads = jnp.concatenate(token_grads, axis=0)
    qkv_grads = outer_pair(
        after(first_low, widen_step), dqkv, (router_parts, first_parts, second_part, third_part), 256
    )
    qkv_shard = reduce_dense(qkv_grads)
    if plane:
        widen_step = widen_rest.spread(qkv_grads)
        widen_rest.cross()
    output = combine(after(y_slots, qkv_grads, widen_step), slots, gates, middle)

    small_total = plane_sum_small if plane else (lambda s, *_: lax.psum(s, "rep").astype(f32))
    down_sum = small_total(after(down_shard, dqkv))
    beside = [p.beside for p in widen_rest.parts] if plane else widen_rest
    narrow_out = after(narrow_sum, qkv_grads, output).astype(f32)
    if plane:
        widen_out = widen_rest.finish(width)
        qkv_shard = after(qkv_shard, output, narrow_out, down_sum, widen_top, widen_out)
        widen_out = cast_first(after(widen_top, qkv_shard), after(widen_out, qkv_shard))
    else:
        widen_out = jnp.concatenate([widen_top, widen_rest], axis=0).astype(f32)
    qkv_sum = small_total(qkv_shard)
    up_out_sum = small_total(after(up_out_shard, qkv_grads, beside), qkv_shard)
    up_sum, out_sum = up_out_sum[:, :hidden_width], up_out_sum[:, hidden_width:]
    small_sum = qkv_sum[:, 3 * width :]
    qkv_sum = qkv_sum[:, : 3 * width].reshape(-1, pairs, 3, 128).swapaxes(1, 2)
    qkv_sum = qkv_sum.reshape(-1, 3 * width)
    return (
        output, token_grads,
        qkv_sum, out_sum, up_sum, down_sum,
        small_sum[:, :experts], small_sum[:, experts], small_sum[:, experts + 1],
        small_sum[:, experts + 2],
        widen_out[None], narrow_out[None],
    )


def solution(mesh):
    rows_spec, exp_spec = P(("rep", "exp"), None), P("exp", None)
    return jax.shard_map(
        body,
        mesh=mesh,
        in_specs=(
            rows_spec, exp_spec, exp_spec, exp_spec, exp_spec, exp_spec,
            P("exp"), P("exp"), P("exp"), P("exp", None, None), P("exp", None, None),
            rows_spec, rows_spec, rows_spec,
        ),
        out_specs=(
            rows_spec, rows_spec, exp_spec, exp_spec, exp_spec, exp_spec, exp_spec,
            P("exp"), P("exp"), P("exp"), P("exp", None, None), P("exp", None, None),
        ),
        check_vma=False,
    )
```

```python
import jax
import jax.numpy as jnp
from jax import lax
from jax.experimental import pallas as pl
from jax.experimental.pallas import tpu as pltpu
from jax.sharding import PartitionSpec as P

PATCHES = 576
HEAD_DIM = 64
EPSILON = 1e-6
LOG2E = 1.4426950408889634
ROOT_HALF = 0.7071067811865476
INV_ROOT_2PI = 0.3989422804014327
bf16 = jnp.bfloat16
f32 = jnp.float32
params = pltpu.CompilerParams(vmem_limit_bytes=58 << 20)


def dot(left, right):
    return jnp.dot(left, right, preferred_element_type=f32)


def dot_nt(left, right):
    return lax.dot_general(left, right, (((1,), (1,)), ((), ())), preferred_element_type=f32)


def dot_tn(left, right):
    return lax.dot_general(left, right, (((0,), (0,)), ((), ())), preferred_element_type=f32)


def unit_norm(values):
    centred = values - jnp.mean(values, axis=-1, keepdims=True)
    inverse = lax.rsqrt(jnp.mean(centred * centred, axis=-1, keepdims=True) + EPSILON)
    return centred * inverse, inverse


def norm_inward(upstream, unit, inverse, gain):
    scaled = upstream * gain
    return inverse * (
        scaled
        - jnp.mean(scaled, axis=-1, keepdims=True)
        - unit * jnp.mean(scaled * unit, axis=-1, keepdims=True)
    )


def gelu_pair(u):
    half = 0.5 + 0.5 * lax.erf(u * ROOT_HALF)
    density = jnp.exp2(u * u * (-0.5 * LOG2E)) * INV_ROOT_2PI
    return u * half, half + u * density


def cost(microseconds):
    return pl.CostEstimate(
        flops=int(microseconds * 8e+08), bytes_accessed=int(microseconds * 2e+06), transcendentals=0
    )


def spec(shape, index):
    return pl.BlockSpec(shape, index)


def fixed(shape):
    zeros = (0,) * len(shape)
    return pl.BlockSpec(shape, lambda *_: zeros, pipeline_mode=pl.Buffered(1))


def shaped(shape, dtype):
    return jax.ShapeDtypeStruct(shape, dtype)


any_space = pl.BlockSpec(memory_space=pl.ANY)
scalar_space = pl.BlockSpec(memory_space=pltpu.SMEM)


def attention_forward(rows_in, weight, small, first_pair, pairs, pairs_all, earlier):
    rows, width = rows_in.shape
    images, first = rows // PATCHES, earlier is None
    cols = 384 * pairs

    def kernel(*refs):
        if first:
            (core_ref, x_ref, hw_ref, kw_ref, qkv_ref, p_ref, o_ref, a_ref, st_ref,
             w_ref, sem, sm_ref, sem_small) = refs
        else:
            (core_ref, a_ref, hw_ref, kw_ref, _, _, _, qkv_ref, p_ref, o_ref, w_ref, sem) = refs
        image, pair = pl.program_id(0), pl.program_id(1)

        @pl.when((pair == 0) & (image == 0))
        def _():
            load_halves(core_ref[0], hw_ref, kw_ref, w_ref, sem, 384 * first_pair, cols)
            if first:
                load_halves(core_ref[0], hw_ref, kw_ref, sm_ref, sem_small, 3 * width, 128)
                st_ref[...] = sm_ref[...].astype(f32).T

        if first:
            @pl.when(pair == 0)
            def _():
                unit, _ = unit_norm(x_ref[...].astype(f32))
                a_ref[...] = (unit * st_ref[small : small + 1, :]).astype(bf16)

        qkv = dot(a_ref[...], w_ref[:, pl.ds(pl.multiple_of(pair * 384, 128), 384)]).astype(bf16)
        qkv_ref[...] = qkv
        q, k, v = qkv[:, :128], qkv[:, 128:256], qkv[:, 256:]
        q = (q.astype(f32) * HEAD_DIM ** (-0.5)).astype(bf16)
        low_lane = lax.broadcasted_iota(jnp.int32, (PATCHES, 128), 1) < HEAD_DIM
        v_t = v.T
        outs = []
        for h in range(2):
            k_head = jnp.where(low_lane == (h == 0), k, jnp.zeros_like(k))
            s = dot_nt(k_head, q)
            top = jnp.max(s, axis=0, keepdims=True)
            e = jnp.exp2((s - top) * LOG2E)
            total = jnp.sum(e, axis=0, keepdims=True)
            p = (e * (1.0 / total)).astype(bf16)
            p_ref[0, h] = p
            outs.append(dot(v_t[h * HEAD_DIM : (h + 1) * HEAD_DIM], p))
        o_ref[...] = jnp.concatenate(outs, axis=0).T.astype(bf16)

    groups = weight[1].shape[0]
    by_image = spec((PATCHES, width), lambda i, j: (i, 0))
    out_specs = [
        spec((PATCHES, 384), lambda i, j: (i, j + first_pair)),
        spec((1, 2, PATCHES, PATCHES), lambda i, j: (i, j + first_pair, 0, 0)),
        spec((PATCHES, 128), lambda i, j: (i, j + first_pair)),
    ]
    out_shape = [
        shaped((rows, 384 * pairs_all), bf16),
        shaped((images, 2 * pairs_all, PATCHES, PATCHES), bf16),
        shaped((rows, 128 * pairs_all), bf16),
    ]
    in_specs = [scalar_space, by_image, any_space, any_space]
    scratch = [pltpu.VMEM((width, cols), bf16), pltpu.SemaphoreType.DMA((2, groups))]
    if first:
        out_specs += [by_image, spec((128, width), lambda i, j: (0, 0))]
        out_shape += [shaped((rows, width), bf16), shaped((128, width), f32)]
        scratch += [pltpu.VMEM((width, 128), bf16), pltpu.SemaphoreType.DMA((2, groups))]
        operands, aliases = (weight[0], rows_in, *weight[1:]), {}
    else:
        in_specs += [any_space] * 3
        operands, aliases = (weight[0], rows_in, *weight[1:], *earlier), {4: 0, 5: 1, 6: 2}
    return pl.pallas_call(
        kernel,
        name="attention_forward",
        cost_estimate=cost(8 * images * pairs // 4),
        grid=(images, pairs),
        in_specs=in_specs,
        out_specs=out_specs,
        out_shape=out_shape,
        scratch_shapes=scratch,
        input_output_aliases=aliases,
        compiler_params=params,
    )(*operands)


def attention_backward(image, dh, out_weight, qkv, probs, attended, tokens, qkv_weight, gain):
    width = dh.shape[1]
    pairs = width // 128

    def kernel(
        core_ref, dh_ref, ho_ref, ko_ref, qkv_ref, p_ref, o_ref, x_ref, hw_ref, kw_ref, g_ref,
        dq_ref, dx_ref, dg_ref, do_ref, db_ref, wo_ref, w_ref, sem, sem_w,
    ):
        pair = pl.program_id(0)

        @pl.when(pair == 0)
        def _():
            load_halves(core_ref[0], ho_ref, ko_ref, wo_ref, sem, 0, width)
            load_halves(core_ref[0], hw_ref, kw_ref, w_ref, sem_w, 0, 3 * width)

        @pl.when(pair == 0)
        def _():
            do = dot_nt(dh_ref[...], wo_ref[...]).astype(bf16)
            for j in range(pairs):
                do_ref[j] = do[:, j * 128 : (j + 1) * 128]

        q, k, v = qkv_ref[:, :128], qkv_ref[:, 128:256], qkv_ref[:, 256:]
        q = (q.astype(f32) * HEAD_DIM ** (-0.5)).astype(bf16)
        do = do_ref[pair]
        low_lane = lax.broadcasted_iota(jnp.int32, (PATCHES, 128), 1) < HEAD_DIM
        prod = do.astype(f32) * o_ref[...].astype(f32)
        prod_high = prod.astype(bf16)
        prod_low = (prod - prod_high.astype(f32)).astype(bf16)
        pick_row = lax.broadcasted_iota(jnp.int32, (16, 128), 0)
        pick_lane = lax.broadcasted_iota(jnp.int32, (16, 128), 1)
        pick = (pick_lane // HEAD_DIM == pick_row).astype(bf16)
        row_sums = dot_nt(pick, prod_high) + dot_nt(pick, prod_low)
        k_t = k.T
        dqs, dks, dvs = [], [], []
        for h in range(2):
            v_head = jnp.where(low_lane == (h == 0), v, jnp.zeros_like(v))
            dp = dot_nt(v_head, do)
            p = p_ref[0, h]
            ds = (p.astype(f32) * (dp - row_sums[h : h + 1])).astype(bf16)
            dvs.append(dot(p, do))
            dks.append(dot(ds, q))
            dqs.append(dot(k_t[h * HEAD_DIM : (h + 1) * HEAD_DIM], ds))
        dq = (jnp.concatenate(dqs, axis=0) * HEAD_DIM ** (-0.5)).T
        dqkv = jnp.concatenate(
            [dq, jnp.where(low_lane, dks[0], dks[1]), jnp.where(low_lane, dvs[0], dvs[1])], axis=1
        ).astype(bf16)
        dq_ref[...] = dqkv

        w_pair = w_ref[:, pl.ds(pl.multiple_of(pair * 384, 128), 384)]

        @pl.when(pair == 0)
        def _():
            db_ref[...] = dot_nt(dqkv, w_pair)

        @pl.when(pair > 0)
        def _():
            db_ref[...] += dot_nt(dqkv, w_pair)

        @pl.when(pair == pairs - 1)
        def _():
            upstream = db_ref[...]
            unit, inverse = unit_norm(x_ref[...].astype(f32))
            inward = norm_inward(upstream, unit, inverse, g_ref[gain[1] : gain[1] + 1, :])
            dx_ref[...] = (dh_ref[...].astype(f32) + inward).astype(bf16)
            dg_ref[...] = jnp.sum(upstream * unit, axis=0, keepdims=True)

    by_image = spec((PATCHES, width), lambda j: (image, 0))
    out_image = spec((PATCHES, width), lambda j: (0, 0))
    return pl.pallas_call(
        kernel,
        name="attention_backward",
        cost_estimate=cost(1000),
        grid=(pairs,),
        in_specs=[
            scalar_space, by_image, any_space, any_space,
            spec((PATCHES, 384), lambda j: (image, j)),
            spec((1, 2, PATCHES, PATCHES), lambda j: (image, j, 0, 0)),
            spec((PATCHES, 128), lambda j: (image, j)),
            by_image,
            any_space, any_space,
            fixed(gain[0].shape),
        ],
        out_specs=[
            spec((PATCHES, 384), lambda j: (0, j)), out_image,
            spec((1, width), lambda j: (0, 0)),
        ],
        out_shape=[
            shaped((PATCHES, 3 * width), bf16), shaped((PATCHES, width), bf16),
            shaped((1, width), f32),
        ],
        scratch_shapes=[
            pltpu.VMEM((pairs, PATCHES, 128), bf16),
            pltpu.VMEM((PATCHES, width), f32),
            pltpu.VMEM((width, width), bf16),
            pltpu.VMEM((width, 3 * width), bf16),
            pltpu.SemaphoreType.DMA((2, out_weight[1].shape[0])),
            pltpu.SemaphoreType.DMA((2, out_weight[1].shape[0])),
        ],
        compiler_params=params,
    )(out_weight[0], dh, *out_weight[1:], qkv, probs, attended, tokens, *qkv_weight[1:], gain[0])


def load_halves(core, mine_ref, other_ref, whole_ref, sem, start, cols):
    groups, rows, _ = mine_ref.shape
    copies = []
    for z in range(groups):
        for side, ref in enumerate((mine_ref, other_ref)):
            place = core if side == 0 else 1 - core
            base = pl.multiple_of((2 * z + place) * rows, 16)
            copies.append(
                pltpu.make_async_copy(
                    ref.at[z, :, pl.ds(start, cols)],
                    whole_ref.at[pl.ds(base, rows), :],
                    sem.at[side, z],
                )
            )
    for copy in copies:
        copy.start()
    for copy in copies:
        copy.wait()


def assemble(place, parts, layout, total):
    groups, rows, _ = parts[0].shape

    def kernel(r_ref, own_ref, x_ref, y_ref, far_ref, o_ref):
        down, right = r_ref[0] // 2, r_ref[0] % 2

        def put(ref, row_half, col_half):
            at = pl.multiple_of(row_half * rows, 16)
            for start, wide, base, step in layout:
                to = pl.multiple_of(base + col_half * step, 128)
                o_ref[:, pl.ds(at, rows), pl.ds(to, wide)] = ref[:, :, start : start + wide]

        put(own_ref, down, right)
        put(x_ref, down, 1 - right)
        put(y_ref, 1 - down, right)
        put(far_ref, 1 - down, 1 - right)

    return pl.pallas_call(
        kernel,
        name="assemble",
        cost_estimate=cost(4),
        in_specs=[scalar_space] + [pl.BlockSpec(memory_space=pltpu.VMEM)] * 4,
        out_specs=pl.BlockSpec(memory_space=pltpu.VMEM),
        out_shape=shaped((groups, 2 * rows, total), bf16),
        compiler_params=params,
    )(place, *parts)


def by_rows(block, cols):
    return spec((block, cols), lambda i: (i, 0))


def whole(shape):
    return spec(shape, lambda i: (0,) * len(shape))


def dense_up(attended, tokens, weights, gain, extra):
    rows, width = tokens.shape
    hidden = weights[1].shape[2] - width
    block, chunk = 288, 512
    tall, wide = extra.shape
    tall = tall * block // rows

    def kernel(
        core_ref, o_ref, x_ref, hw_ref, kw_ref, g_ref, e_ref,
        h_ref, b_ref, z_ref, s_ref, low_ref, w_ref, sem,
    ):
        @pl.when(pl.program_id(0) == 0)
        def _():
            load_halves(core_ref[0], hw_ref, kw_ref, w_ref, sem, 0, width + hidden)

        low_ref[...] = e_ref[...].astype(bf16)
        h = x_ref[...].astype(f32) + dot(o_ref[...], w_ref[:, :width])
        h = h.astype(bf16)
        h_ref[...] = h
        h = h.astype(f32)
        b = (unit_norm(h)[0] * g_ref[gain[1] : gain[1] + 1, :]).astype(bf16)
        b_ref[...] = b
        ahead = dot(b, w_ref[:, width : width + chunk])
        for c in range(0, hidden, chunk):
            u = ahead
            if c + chunk < hidden:
                ahead = dot(b, w_ref[:, width + c + chunk : width + c + 2 * chunk])
            z, slope = gelu_pair(u)
            z_ref[:, c : c + chunk] = z.astype(bf16)
            s_ref[:, c : c + chunk] = slope.astype(bf16)

    return pl.pallas_call(
        kernel,
        name="dense_up",
        cost_estimate=cost(18),
        grid=(rows // block,),
        in_specs=[
            scalar_space, by_rows(block, width), by_rows(block, width), any_space, any_space,
            fixed(gain[0].shape), by_rows(tall, wide),
        ],
        out_specs=[
            by_rows(block, width), by_rows(block, width), by_rows(block, hidden),
            by_rows(block, hidden), by_rows(tall, wide),
        ],
        out_shape=[
            shaped((rows, width), bf16), shaped((rows, width), bf16),
            shaped((rows, hidden), bf16), shaped((rows, hidden), bf16),
            shaped(extra.shape, bf16),
        ],
        scratch_shapes=[
            pltpu.VMEM((width, width + hidden), bf16),
            pltpu.SemaphoreType.DMA((2, weights[1].shape[0])),
        ],
        compiler_params=params,
    )(weights[0], attended, tokens, *weights[1:], gain[0], extra)


def dense_down(activ, hidden_rows, ids, weights, experts, gain):
    rows, width = hidden_rows.shape
    hidden = activ.shape[1]
    block = 288

    def kernel(
        core_ref, z_ref, h_ref, id_ref, hw_ref, kw_ref, g_ref,
        y_ref, m_ref, gate_ref, w_ref, sem,
    ):
        @pl.when(pl.program_id(0) == 0)
        def _():
            load_halves(core_ref[0], hw_ref, kw_ref, w_ref, sem, 0, width)

        y = h_ref[...].astype(f32) + dot(z_ref[...], w_ref[...])
        y_ref[...] = y.astype(bf16)
        m = (unit_norm(y)[0] * g_ref[gain[1] : gain[1] + 1, :]).astype(bf16)
        m_ref[...] = m
        logits = dot_nt(g_ref[:experts, :].astype(bf16), m)
        e = jnp.exp(logits - jnp.max(logits, axis=0, keepdims=True))
        p = e / jnp.sum(e, axis=0, keepdims=True)
        line = lax.broadcasted_iota(jnp.int32, (experts, block), 0)
        for k in range(2):
            hot = line == id_ref[0, k : k + 1, :]
            gate_ref[0, k : k + 1, :] = jnp.sum(jnp.where(hot, p, 0.0), axis=0, keepdims=True)

    return pl.pallas_call(
        kernel,
        name="dense_down",
        cost_estimate=cost(15),
        grid=(rows // block,),
        in_specs=[
            scalar_space, by_rows(block, hidden), by_rows(block, width),
            spec((1, 2, block), lambda i: (i, 0, 0)),
            any_space, any_space, fixed(gain[0].shape),
        ],
        out_specs=[
            by_rows(block, width), by_rows(block, width),
            spec((1, 2, block), lambda i: (i, 0, 0)),
        ],
        out_shape=[
            shaped((rows, width), bf16), shaped((rows, width), bf16),
            shaped((rows // block, 2, block), f32),
        ],
        scratch_shapes=[
            pltpu.VMEM((hidden, width), bf16),
            pltpu.SemaphoreType.DMA((2, weights[1].shape[0])),
        ],
        compiler_params=params,
    )(weights[0], activ, hidden_rows, ids, *weights[1:], gain[0])


def gated_rows(slot_ref, gate_ref, slots_refs, block):
    total, base = None, 0
    for ref in slots_refs:
        count = ref.shape[0]
        lane = base + lax.broadcasted_iota(jnp.int32, (block, count), 1)
        weighted = jnp.zeros((block, count), f32)
        for k in range(2):
            hot = lane == slot_ref[:, k : k + 1]
            weighted = weighted + jnp.where(hot, gate_ref[:, k : k + 1], 0.0)
        part = dot(weighted.astype(bf16), ref[...])
        total = part if total is None else total + part
        base += count
    return total


def norm_three_backward(dx_slots, slots, gates, cotangent, middle, gain):
    rows, width = cotangent.shape
    block = 288

    def kernel(da_ref, db_ref, slot_ref, gate_ref, cot_ref, y_ref, g_ref, dzl_ref, dg_ref):
        dm = gated_rows(slot_ref, gate_ref, (da_ref, db_ref), block)
        unit, inverse = unit_norm(y_ref[...].astype(f32))
        part = jnp.sum(dm * unit, axis=0, keepdims=True)
        dy = cot_ref[...].astype(f32) + norm_inward(dm, unit, inverse, g_ref[gain[1] : gain[1] + 1, :])
        dzl_ref[...] = dy.astype(bf16)
        first = pl.program_id(0) == 0

        @pl.when(first)
        def _():
            dg_ref[...] = part

        @pl.when(jnp.logical_not(first))
        def _():
            dg_ref[...] += part

    return pl.pallas_call(
        kernel,
        name="norm_three_backward",
        cost_estimate=cost(10),
        grid=(rows // block,),
        in_specs=[
            fixed(dx_slots[0].shape), fixed(dx_slots[1].shape), by_rows(block, 2),
            by_rows(block, 2), by_rows(block, width), by_rows(block, width), fixed(gain[0].shape),
        ],
        out_specs=[by_rows(block, width), whole((1, width))],
        out_shape=[shaped((rows, width), bf16), shaped((1, width), f32)],
        compiler_params=params,
    )(*dx_slots, slots, gates, cotangent, middle, gain[0])


def dense_backward(dzl, slope, hidden_rows, up_weight, down_weight, gain):
    rows, width = dzl.shape
    hidden = slope.shape[1]
    block, chunk = 288, 512

    def kernel(
        core_ref, dzl_ref, s_ref, h_ref, hu_ref, ku_ref, hd_ref, kd_ref, g_ref,
        du_ref, dhl_ref, dg_ref, w1_ref, w2_ref, sem,
    ):
        first = pl.program_id(0) == 0

        @pl.when(first)
        def _():
            load_halves(core_ref[0], hd_ref, kd_ref, w2_ref, sem, 0, width)
            load_halves(core_ref[0], hu_ref, ku_ref, w1_ref, sem, width, hidden)

        dzl = dzl_ref[...]
        db = jnp.zeros((block, width), f32)
        ahead = dot_nt(dzl, w2_ref[:chunk, :])
        for c in range(0, hidden, chunk):
            dz = ahead
            if c + chunk < hidden:
                ahead = dot_nt(dzl, w2_ref[c + chunk : c + 2 * chunk, :])
            du = (dz * s_ref[:, c : c + chunk].astype(f32)).astype(bf16)
            du_ref[:, c : c + chunk] = du
            db = db + dot_nt(du, w1_ref[:, c : c + chunk])
        unit, inverse = unit_norm(h_ref[...].astype(f32))
        part = jnp.sum(db * unit, axis=0, keepdims=True)
        dh = dzl.astype(f32) + norm_inward(db, unit, inverse, g_ref[gain[1] : gain[1] + 1, :])
        dhl_ref[...] = dh.astype(bf16)

        @pl.when(first)
        def _():
            dg_ref[...] = part

        @pl.when(jnp.logical_not(first))
        def _():
            dg_ref[...] += part

    return pl.pallas_call(
        kernel,
        name="dense_backward",
        cost_estimate=cost(24),
        grid=(rows // block,),
        in_specs=[
            scalar_space, by_rows(block, width), by_rows(block, hidden),
            by_rows(block, width), any_space, any_space, any_space, any_space, fixed(gain[0].shape),
        ],
        out_specs=[
            by_rows(block, hidden), by_rows(block, width), whole((1, width)),
        ],
        out_shape=[
            shaped((rows, hidden), bf16), shaped((rows, width), bf16), shaped((1, width), f32),
        ],
        scratch_shapes=[
            pltpu.VMEM((width, hidden), bf16), pltpu.VMEM((hidden, width), bf16),
            pltpu.SemaphoreType.DMA((2, up_weight[1].shape[0])),
        ],
        compiler_params=params,
    )(up_weight[0], dzl, slope, hidden_rows, *up_weight[1:], *down_weight[1:], gain[0])


def combine(y_slots, slots, gates, middle):
    rows, width = middle.shape
    block = 288

    def kernel(ya_ref, slot_ref, gate_ref, y_ref, o_ref):
        o_ref[...] = (
            y_ref[...].astype(f32) + gated_rows(slot_ref, gate_ref, (ya_ref,), block)
        ).astype(bf16)

    return pl.pallas_call(
        kernel,
        name="combine",
        cost_estimate=cost(8),
        grid=(rows // block,),
        in_specs=[
            fixed(y_slots.shape), by_rows(block, 2), by_rows(block, 2), by_rows(block, width),
        ],
        out_specs=by_rows(block, width),
        out_shape=shaped((rows, width), bf16),
        compiler_params=params,
    )(y_slots, slots, gates, middle)


def expert_main(me, rows_in, widen_low, cot_wide, small_t, experts):
    rows, width = rows_in.shape
    hidden = widen_low.shape[1]
    chunk, part = 1024, 512
    steps = hidden // chunk

    def kernel(
        me_ref, x_ref, a_ref, u_ref, wr_ref,
        z_ref, v_ref, dx_ref, gate_ref, dwr_ref, acc_ref, dg_ref,
    ):
        step = pl.program_id(0)

        @pl.when(step == 0)
        def _():
            acc_ref[...] = jnp.zeros_like(acc_ref)
            dg_ref[...] = jnp.zeros_like(dg_ref)

        x = x_ref[...]
        ahead = dot(x, a_ref[:, :part])
        sums = jnp.zeros((rows, 128), f32)
        for c in range(0, chunk, part):
            cols = slice(c, c + part)
            r = ahead
            if c + part < chunk:
                ahead = dot(x, a_ref[:, c + part : c + 2 * part])
            z, slope = gelu_pair(r)
            u = u_ref[:, cols].astype(f32)
            v = (u * slope).astype(bf16)
            z_ref[:, cols] = z.astype(bf16)
            v_ref[:, cols] = v
            dg = u * z
            sums = sums + sum(dg[:, q : q + 128] for q in range(0, part, 128))
            acc_ref[...] += dot_nt(v, a_ref[:, cols])
        dg_ref[...] += sums

        @pl.when(step == steps - 1)
        def _():
            wr = wr_ref[:experts, :].astype(bf16)
            logits = dot_nt(wr, x)
            e = jnp.exp(logits - jnp.max(logits, axis=0, keepdims=True))
            p = e / jnp.sum(e, axis=0, keepdims=True)
            own = lax.broadcasted_iota(jnp.int32, (experts, rows), 0) == me_ref[0]
            gate = jnp.sum(jnp.where(own, p, 0.0), axis=0, keepdims=True)
            gate_ref[...] = jnp.broadcast_to(gate, (128, rows)).T[:, :1]
            dgate = jnp.sum(dg_ref[...].T, axis=0, keepdims=True)
            spread = dgate * (own.astype(f32) - p)
            dx_ref[...] = (acc_ref[...] + dot_tn(spread.astype(bf16), wr)).astype(bf16)
            dwr_ref[...] = dot((gate * spread).astype(bf16), x)

    by_col = spec((rows, chunk), lambda i: (0, i))
    return pl.pallas_call(
        kernel,
        name="expert_main",
        cost_estimate=cost(15),
        grid=(steps,),
        in_specs=[
            scalar_space, fixed((rows, width)), spec((width, chunk), lambda i: (0, i)), by_col,
            fixed(small_t.shape),
        ],
        out_specs=[by_col, by_col, whole((rows, width)), whole((rows, 1)), whole((experts, width))],
        out_shape=[
            shaped((rows, hidden), bf16), shaped((rows, hidden), bf16),
            shaped((rows, width), bf16), shaped((rows, 1), f32), shaped((experts, width), f32),
        ],
        scratch_shapes=[pltpu.VMEM((rows, width), f32), pltpu.VMEM((rows, 128), f32)],
        compiler_params=params,
    )(me, rows_in, widen_low, cot_wide, small_t)


def narrow_outer(activs, cots, gates):
    rows, width = cots[0].shape
    hidden = activs[0].shape[1]
    chunk = 1024

    def kernel(za_ref, zb_ref, ca_ref, cb_ref, ga_ref, gb_ref, o_ref, da_ref, db_ref):
        @pl.when(pl.program_id(0) == 0)
        def _():
            da_ref[...] = (ca_ref[...].astype(f32) * ga_ref[...]).astype(bf16)
            db_ref[...] = (cb_ref[...].astype(f32) * gb_ref[...]).astype(bf16)

        o_ref[...] = (
            dot_tn(za_ref[...], da_ref[...]) + dot_tn(zb_ref[...], db_ref[...])
        ).astype(bf16)

    by_col = spec((rows, chunk), lambda i: (0, i))
    return pl.pallas_call(
        kernel,
        name="narrow_outer",
        cost_estimate=cost(12),
        grid=(hidden // chunk,),
        in_specs=[by_col, by_col] + [fixed((rows, width))] * 2 + [fixed((rows, 1))] * 2,
        out_specs=spec((chunk, width), lambda i: (i, 0)),
        out_shape=shaped((hidden, width), bf16),
        scratch_shapes=[pltpu.VMEM((rows, width), bf16)] * 2,
        compiler_params=params,
    )(*activs, *cots, *gates)


def widen_outer(rows_in, slopes, gates):
    rows, width = rows_in[0].shape
    hidden = slopes[0].shape[1]
    chunk = 1024

    def kernel(xa_ref, xb_ref, va_ref, vb_ref, ga_ref, gb_ref, o_ref, da_ref, db_ref):
        @pl.when(pl.program_id(0) == 0)
        def _():
            da_ref[...] = (xa_ref[...].astype(f32) * ga_ref[...]).astype(bf16)
            db_ref[...] = (xb_ref[...].astype(f32) * gb_ref[...]).astype(bf16)

        o_ref[...] = (
            dot_tn(da_ref[...], va_ref[...]) + dot_tn(db_ref[...], vb_ref[...])
        ).astype(bf16)

    by_col = spec((rows, chunk), lambda i: (0, i))
    return pl.pallas_call(
        kernel,
        name="widen_outer",
        cost_estimate=cost(12),
        grid=(hidden // chunk,),
        in_specs=[fixed((rows, width))] * 2 + [by_col, by_col] + [fixed((rows, 1))] * 2,
        out_specs=spec((width, chunk), lambda i: (0, i)),
        out_shape=shaped((width, hidden), bf16),
        scratch_shapes=[pltpu.VMEM((rows, width), bf16)] * 2,
        compiler_params=params,
    )(*rows_in, *slopes, *gates)


def narrow_product(activ, narrow_low):
    rows, hidden = activ.shape
    width = narrow_low.shape[1]
    block = rows // 2

    def kernel(z_ref, w_ref, o_ref):
        o_ref[...] = dot(z_ref[...], w_ref[...]).astype(bf16)

    return pl.pallas_call(
        kernel,
        name="narrow_product",
        cost_estimate=cost(6),
        grid=(2,),
        in_specs=[by_rows(block, hidden), fixed((hidden, width))],
        out_specs=by_rows(block, width),
        out_shape=shaped((rows, width), bf16),
        compiler_params=params,
    )(activ, narrow_low)


def outer_pair(left, rights, small_parts, chunk):
    half, cols = rights[0].shape
    mine = left.shape[1]
    blocks = cols // chunk
    routers, firsts, second, third = small_parts
    experts = routers[0].shape[0]

    def kernel(l_ref, a_ref, b_ref, ra_ref, rb_ref, fa_ref, fb_ref, s_ref, t_ref, o_ref, rows_ref):
        step = pl.program_id(0)

        @pl.when(step < blocks)
        def _():
            o_ref[...] = (
                dot_tn(l_ref[:half], a_ref[...]) + dot_tn(l_ref[half:], b_ref[...])
            ).astype(bf16)

        @pl.when(step == blocks)
        def _():
            rows_ref[...] = jnp.zeros_like(rows_ref)
            rows_ref[:experts] = ra_ref[...] + rb_ref[...]
            rows_ref[experts : experts + 1] = fa_ref[...] + fb_ref[...]
            rows_ref[experts + 1 : experts + 2] = s_ref[...]
            rows_ref[experts + 2 : experts + 3] = t_ref[...]
            o_ref[:, :128] = rows_ref[...].T.astype(bf16)
            o_ref[:, 128:] = jnp.zeros((mine, chunk - 128), bf16)

    by_col = spec((half, chunk), lambda i: (0, jnp.minimum(i, blocks - 1)))
    return pl.pallas_call(
        kernel,
        name="outer_pair",
        cost_estimate=cost(10),
        grid=(blocks + 1,),
        in_specs=[fixed((2 * half, mine)), by_col, by_col]
        + [fixed((experts, mine))] * 2 + [fixed((1, mine))] * 4,
        out_specs=spec((mine, chunk), lambda i: (0, i)),
        out_shape=shaped((mine, cols + chunk), bf16),
        scratch_shapes=[pltpu.VMEM((128, mine), f32)],
        compiler_params=params,
    )(left, *rights, *routers, *firsts, second, third)


def place_pieces(place, pieces, total):
    rows, cols = pieces[0].shape
    amount = len(pieces)

    def kernel(place_ref, *refs):
        for k in range(amount):

            @pl.when(pl.program_id(0) == k)
            def _():
                refs[amount][...] = refs[k][...].astype(f32)

    return pl.pallas_call(
        kernel,
        name="place_pieces",
        cost_estimate=cost(5),
        grid_spec=pltpu.PrefetchScalarGridSpec(
            num_scalar_prefetch=1,
            grid=(amount,),
            in_specs=[pl.BlockSpec((rows, cols), lambda i, p: (0, 0))] * amount,
            out_specs=pl.BlockSpec((rows, cols), lambda i, p: (p[i], 0)),
        ),
        out_shape=shaped((total, cols), f32),
        compiler_params=params,
    )(place, *pieces)


def cast_first(array, earlier):
    rows, cols = array.shape
    block = rows // 4

    def kernel(a_ref, _, o_ref):
        o_ref[...] = a_ref[...].astype(f32)

    return pl.pallas_call(
        kernel,
        name="cast_first",
        cost_estimate=cost(3),
        grid=(4,),
        in_specs=[by_rows(block, cols), any_space],
        out_specs=by_rows(block, cols),
        out_shape=shaped(earlier.shape, f32),
        input_output_aliases={1: 0},
        compiler_params=params,
    )(array, earlier)


def to_slots_cast(rows_in, slot_rows, count, weight):
    rows, width = rows_in.shape
    block = 288
    steps = count // block
    tall, wide = weight.shape

    def kernel(r_ref, s_ref, w_ref, o_ref, low_ref):
        base = pl.program_id(0) * block
        line = base + lax.broadcasted_iota(jnp.int32, (block, rows), 0)
        hot = (line == s_ref[0:1, :]) | (line == s_ref[1:2, :])
        o_ref[...] = dot(hot.astype(bf16), r_ref[...]).astype(bf16)
        low_ref[...] = w_ref[...].astype(bf16)

    return pl.pallas_call(
        kernel,
        name="to_slots_cast",
        cost_estimate=cost(20),
        grid=(steps,),
        in_specs=[fixed((rows, width)), fixed((2, rows)), by_rows(tall // steps, wide)],
        out_specs=[by_rows(block, width), by_rows(tall // steps, wide)],
        out_shape=[shaped((count, width), bf16), shaped((tall, wide), bf16)],
        compiler_params=params,
    )(rows_in, slot_rows, weight)


def outer_two(left, right, left_last, right_last):
    rows, mine = left.shape
    chunk = right_last.shape[1]
    blocks = right.shape[1] // chunk

    def kernel(l_ref, r_ref, ll_ref, rl_ref, o_ref):
        step = pl.program_id(0)

        @pl.when(step < blocks)
        def _():
            o_ref[...] = dot_tn(l_ref[...], r_ref[...]).astype(bf16)

        @pl.when(step == blocks)
        def _():
            o_ref[...] = dot_tn(ll_ref[...], rl_ref[...]).astype(bf16)

    return pl.pallas_call(
        kernel,
        name="outer_two",
        cost_estimate=cost(15),
        grid=(blocks + 1,),
        in_specs=[
            fixed((rows, mine)),
            spec((rows, chunk), lambda i: (0, jnp.minimum(i, blocks - 1))),
            fixed((rows, mine)), fixed((rows, chunk)),
        ],
        out_specs=spec((mine, chunk), lambda i: (0, i)),
        out_shape=shaped((mine, chunk * (blocks + 1)), bf16),
        compiler_params=params,
    )(left, right, left_last, right_last)


def to_slots(rows_in, slot_rows, count):
    rows, width = rows_in.shape
    block = 288

    def kernel(r_ref, s_ref, o_ref):
        base = pl.program_id(0) * block
        line = base + lax.broadcasted_iota(jnp.int32, (block, rows), 0)
        hot = (line == s_ref[0:1, :]) | (line == s_ref[1:2, :])
        o_ref[...] = dot(hot.astype(bf16), r_ref[...]).astype(bf16)

    return pl.pallas_call(
        kernel,
        name="to_slots",
        cost_estimate=cost(4),
        grid=(count // block,),
        in_specs=[fixed((rows, width)), fixed((2, rows))],
        out_specs=spec((block, width), lambda i: (i, 0)),
        out_shape=shaped((count, width), bf16),
        compiler_params=params,
    )(rows_in, slot_rows)


def product_wide(left, right_t, chunk=1024):
    rows, depth = left.shape
    cols = right_t.shape[0]

    def kernel(l_ref, r_ref, o_ref):
        o_ref[...] = dot_nt(l_ref[...], r_ref[...]).astype(bf16)

    return pl.pallas_call(
        kernel,
        name="product_wide",
        cost_estimate=cost(7),
        grid=(cols // chunk,),
        in_specs=[fixed((rows, depth)), spec((chunk, depth), lambda i: (i, 0))],
        out_specs=spec((rows, chunk), lambda i: (0, i)),
        out_shape=shaped((rows, cols), bf16),
        compiler_params=params,
    )(left, right_t)


def outer_by_right(left, right, chunk):
    rows, mine = left.shape
    cols = right.shape[1]

    def kernel(l_ref, r_ref, o_ref):
        o_ref[...] = dot_tn(l_ref[...], r_ref[...]).astype(bf16)

    return pl.pallas_call(
        kernel,
        name="outer_by_right",
        cost_estimate=cost(10),
        grid=(cols // chunk,),
        in_specs=[fixed((rows, mine)), spec((rows, chunk), lambda i: (0, i))],
        out_specs=spec((mine, chunk), lambda i: (0, i)),
        out_shape=shaped((mine, cols), bf16),
        compiler_params=params,
    )(left, right)


def outer_by_left(left, right, chunk):
    rows, mine = left.shape
    cols = right.shape[1]

    def kernel(l_ref, r_ref, o_ref):
        o_ref[...] = dot_tn(l_ref[...], r_ref[...]).astype(bf16)

    return pl.pallas_call(
        kernel,
        name="outer_by_left",
        cost_estimate=cost(10),
        grid=(mine // chunk,),
        in_specs=[spec((rows, chunk), lambda i: (0, i)), fixed((rows, cols))],
        out_specs=spec((chunk, cols), lambda i: (i, 0)),
        out_shape=shaped((mine, cols), bf16),
        compiler_params=params,
    )(left, right)


def plane_neighbours(array, by):
    return lax.ppermute(array, "rep", [(i, i ^ by) for i in range(4)])


def after(value, *others):
    return lax.optimization_barrier((value, *others))[0]


def add_low(left, right):
    return (left.astype(f32) + right.astype(f32)).astype(bf16)


class PlaneSum:
    def __init__(self, array, first):
        self.first, self.second = first, 3 - first
        rep = lax.axis_index("rep")
        self.near, self.far = lax.rem(rep // first, 2), lax.rem(rep // self.second, 2)
        self.kept, self.got = self.exchange_half(array, self.near, first)

    def exchange_half(self, whole, bit, by):
        halves = whole.reshape(2, whole.shape[0] // 2, whole.shape[1])
        kept = lax.dynamic_index_in_dim(halves, bit, 0, False)
        sent = lax.dynamic_index_in_dim(halves, 1 - bit, 0, False)
        return kept, plane_neighbours(sent, by)

    def fold(self, *before):
        self.kept, self.got = after((self.kept, self.got), *before)
        half = add_low(self.kept, self.got)
        self.kept, self.got = self.exchange_half(half, self.far, self.second)
        return half

    def spread(self, *before):
        self.kept, self.got = after((self.kept, self.got), *before)
        self.own = add_low(self.kept, self.got)
        self.beside = plane_neighbours(self.own, self.second)
        return self.own

    def cross(self, *before):
        self.beside = after(self.beside, *before)
        self.across = [plane_neighbours(p, self.first) for p in (self.own, self.beside)]
        return self.beside

    def pieces(self):
        low, high = 2 * self.near + self.far, 2 * (1 - self.near) + self.far
        flip = 1 - 2 * self.far
        return [low, low + flip, high, high + flip], [self.own, self.beside, *self.across]


class PlanePair:
    def __init__(self, array):
        half = array.shape[0] // 2
        self.parts = [PlaneSum(array[:half], 1), PlaneSum(array[half:], 2)]

    def fold(self, *before):
        return [p.fold(*before) for p in self.parts]

    def spread(self, *before):
        return [p.spread(*before) for p in self.parts]

    def cross(self, *before):
        return [p.cross(*before) for p in self.parts]

    def finish(self, total):
        places, pieces = [], []
        base = total // self.parts[0].own.shape[0] - 8
        for start, part in zip((base, base + 4), self.parts):
            where, what = part.pieces()
            places += [start + w for w in where]
            pieces += what
        return place_pieces(jnp.stack(places).astype(jnp.int32), pieces, total)


def plane_sum_small(array, *before, between=None):
    parts = jnp.split(array, 2, axis=0)
    got = [plane_neighbours(p, by) for p, by in zip(parts, (1, 2))]
    if between is not None:
        got = after(got, between)
    firsts = [add_low(p, q) for p, q in zip(parts, got)]
    others = [plane_neighbours(p, by) for p, by in zip(firsts, (2, 1))]
    if before:
        others = after(others, *before)
    lasts = [p.astype(f32) + q.astype(f32) for p, q in zip(firsts, others)]
    return jnp.concatenate(lasts, axis=0)


def plane_piece(shards, tail=None):
    rep = lax.axis_index("rep")
    pieces = []
    for shard in shards:
        rows, cols = shard.shape[0] // 2, shard.shape[1] // 2
        pieces.append(
            lax.dynamic_slice(shard, ((rep // 2) * rows, (rep % 2) * cols), (rows, cols))
        )
    if tail is not None:
        rows = tail.shape[0] // 2
        pieces.append(lax.dynamic_slice(tail, ((rep // 2) * rows, 0), (rows, tail.shape[1])))
    return jnp.concatenate(pieces, axis=1).astype(bf16)


def gather_line(piece):
    groups = lax.axis_size("exp") // 2
    lines = [[2 * z + c for z in range(groups)] for c in range(2)]
    return lax.all_to_all(
        jnp.broadcast_to(piece[None], (groups,) + piece.shape),
        "exp", split_axis=0, concat_axis=0, axis_index_groups=lines,
    )


def gather_plane(own):
    return own, *[plane_neighbours(own, by) for by in (1, 2, 3)]


def gather_cores(parts, layout, total):
    ranks = lax.axis_size("exp")
    mine = assemble(lax.axis_index("rep").reshape(1), parts, layout, total)
    other = lax.ppermute(mine, "exp", [(i, i ^ 1) for i in range(ranks)])
    return lax.rem(lax.axis_index("exp"), 2).reshape(1), mine, other


def gather_plain(shards):
    whole_rows = [lax.all_gather(s.astype(bf16), "exp", axis=0, tiled=True) for s in shards]
    joined = jnp.concatenate(whole_rows, axis=1)
    halves = joined.reshape(4, 2, joined.shape[0] // 8, joined.shape[1])
    return jnp.zeros((1,), jnp.int32), halves[:, 0], halves[:, 1]


def body(
    tokens, qkv_weight, out_weight, up_weight, down_weight, router_weight,
    first_gain, second_gain, third_gain, widening, narrowing, expert_ids, priority, cotangent,
):
    rows, width = tokens.shape
    hidden_width = up_weight.shape[1]
    ranks, reps = lax.axis_size("exp"), lax.axis_size("rep")
    experts = widening.shape[0] * ranks
    capacity = (rows + experts - 1) // experts
    half = capacity // 2
    count = experts * capacity
    pairs = width // 128
    me = lax.axis_index("exp").reshape(1)

    def reduce_dense(array):
        return lax.psum_scatter(array, "exp", scatter_dimension=0, tiled=True)

    plane = ranks == 8 and reps == 4

    choice_hot = (expert_ids[:, :, None] == jnp.arange(experts, dtype=jnp.int32)).astype(f32)
    rank_row = priority[0]
    earlier = (rank_row[None, :] < rank_row[:, None]).astype(bf16)
    ahead = dot(earlier, choice_hot.reshape(rows, -1).astype(bf16)).reshape(choice_hot.shape)
    totals = jnp.sum(choice_hot, axis=0)
    prior = jnp.cumsum(totals, axis=0) - totals
    position = jnp.sum((ahead + prior[None]) * choice_hot, axis=-1).astype(jnp.int32)
    kept = position < capacity
    slots = jnp.where(kept, expert_ids * capacity + position, -1)
    later = position >= half
    split_slots = expert_ids * half + position + jnp.where(later, experts * half - half, 0)
    split_slots = jnp.where(kept, split_slots, -1)
    slot_rows = split_slots.T
    ids_rows = expert_ids.reshape(rows // 288, 288, 2).swapaxes(1, 2)
    whole_rows = slots.T

    def exchange(array, amount):
        return lax.all_to_all(
            array.reshape(experts, amount, width), "exp", split_axis=0, concat_axis=0, tiled=True
        ).reshape(experts * amount, width)

    def both_halves(rows_in):
        return [to_slots(rows_in, slot_rows - j * (count // 2), count // 2) for j in range(2)]

    small = jnp.concatenate(
        [router_weight, first_gain[:, None], second_gain[:, None], third_gain[:, None]], axis=1
    )
    small = jnp.pad(small, ((0, 0), (0, 128 - experts - 3)))
    by_pair = qkv_weight.reshape(-1, 3, pairs, 128).swapaxes(1, 2).reshape(-1, 3 * width)
    wide, deep = width // 2, hidden_width // 2
    if plane:
        own = gather_line(plane_piece((by_pair,), small))
        pieces = gather_plane(own)
        sent_cots, narrow_low = to_slots_cast(
            after(cotangent, own, slot_rows, ids_rows, slots, split_slots),
            whole_rows, count, narrowing[0],
        )
        piece, piece_down = plane_piece((out_weight, up_weight)), plane_piece((down_weight,))
        tall = piece.shape[0]
        piece = piece.reshape(tall, -1, wide).swapaxes(0, 1).reshape(-1, wide)
        own_both = gather_line(after(jnp.concatenate([piece, piece_down], axis=0), own))
        own_next = own_both[:, : piece.shape[0]].reshape(ranks // 2, -1, tall, wide)
        own_next = own_next.swapaxes(1, 2).reshape(ranks // 2, tall, -1)
        own_down = own_both[:, piece.shape[0] :]
        qkv_w = gather_cores(
            after(pieces, own_both, sent_cots),
            ((0, 3 * wide, 0, 3 * wide), (3 * wide, 128, 3 * width, 0)), 3 * width + 128,
        )
        pieces = gather_plane(after(own_next, pieces))
        pieces_down = gather_plane(after(own_down, pieces))
    else:
        sent_cots, narrow_low = to_slots_cast(cotangent, whole_rows, count, narrowing[0])
        qkv_w = gather_plain((by_pair, small))
        out_up = gather_plain((out_weight, up_weight))
        down = gather_plain((down_weight,))

    split = pairs - 1
    qkv, probs, attended, first_low, small_t = attention_forward(
        tokens, qkv_w, experts, 0, split, pairs, None
    )
    if plane:
        out_up = gather_cores(
            after(pieces, small_t), ((0, wide, 0, wide), (wide, deep, width, deep)),
            width + hidden_width,
        )
    cots = exchange(after(sent_cots, small_t), capacity)
    gain_one, gain_two, gain_three = [(small_t, experts + k) for k in range(3)]
    qkv, probs, attended = attention_forward(
        first_low, qkv_w, experts, split, pairs - split, pairs, (qkv, probs, attended)
    )
    hidden, second_low, activ, slope, widen_low = dense_up(
        attended, tokens, out_up, gain_two, widening[0]
    )
    if plane:
        down = gather_cores(after(pieces_down, hidden), ((0, wide, 0, wide),), width)
    middle, third_low, gate_rows = dense_down(
        after(activ, cots), hidden, ids_rows, down, experts, gain_three
    )
    gates = gate_rows.swapaxes(1, 2).reshape(rows, 2)

    sent_rows = both_halves(third_low)
    cots = after(cots, third_low).reshape(experts, 2, half, width)
    cots = [cots[:, j].reshape(-1, width) for j in range(2)]
    cot_wide = [product_wide(c, narrow_low) for c in cots]
    sent_rows[1] = after(sent_rows[1], cot_wide)
    arrived = [exchange(x, half) for x in sent_rows]
    mains, y_rows = [], []
    for j in range(2):
        ready = after(arrived[j], y_rows, *[m[2] for m in mains])
        mains.append(expert_main(me, ready, widen_low, cot_wide[j], small_t, experts))
        if j == 0:
            y_rows.append(narrow_product(after(mains[j][0], mains[j][2]), narrow_low))
    z_rows, v_rows, dx_rows, slot_gates, router_parts = zip(*mains)
    dx_slots = [exchange(after(dx_rows[0], y_rows), half)]
    dx_slots.append(exchange(after(dx_rows[1], dx_slots[0]), half))
    y_rows.append(narrow_product(after(z_rows[1], dx_slots[0]), narrow_low))
    narrow_grads = narrow_outer(z_rows, after(cots, y_rows), slot_gates)
    widen_grads = widen_outer(after(arrived, narrow_grads), v_rows, slot_gates)
    narrow_sum = lax.psum(narrow_grads, "rep")
    y_sent = jnp.stack([y.reshape(experts, half, width) for y in y_rows], axis=1)

    y_slots = exchange(after(y_sent, dx_slots), capacity)

    dzl, third_part = norm_three_backward(
        after(dx_slots, widen_grads), split_slots, gates, cotangent, middle, gain_three
    )
    du, dh, second_part = dense_backward(
        dzl, slope, hidden, out_up, down, gain_two
    )
    down_grads = outer_by_left(after(activ, y_slots, du), dzl, 1024)
    down_shard = reduce_dense(down_grads)
    up_out_grads = outer_two(after(second_low, down_grads), du, attended, dh)
    up_out_shard = reduce_dense(up_out_grads)
    dh = after(dh, up_out_grads)
    halves = []
    for image in range(2):
        halves.append(attention_backward(
            image, dh, out_up, qkv, probs, attended, tokens, qkv_w, gain_one
        ))
        if image == 0:
            cut = width // 2
            order = list(range(reps))
            widen_top = lax.psum(
                widen_grads[:cut], "rep", axis_index_groups=[order[:2] + order[:1:-1]]
            )
            widen_rest = after(widen_grads, halves[0], narrow_sum)[cut:]
            widen_rest = (PlanePair if plane else lambda s: lax.psum(s, "rep"))(widen_rest)
            dh = after(dh, halves[0], narrow_sum, down_shard)
    dqkv, token_grads, first_parts = zip(*halves)
    widen_step = widen_rest.fold(dqkv) if plane else widen_rest
    token_grads = jnp.concatenate(token_grads, axis=0)
    qkv_grads = outer_pair(
        after(first_low, widen_step), dqkv, (router_parts, first_parts, second_part, third_part), 256
    )
    qkv_shard = reduce_dense(qkv_grads)
    if plane:
        widen_step = widen_rest.spread(qkv_grads)
        widen_rest.cross()
    output = combine(after(y_slots, qkv_grads, widen_step), slots, gates, middle)

    small_total = plane_sum_small if plane else (lambda s, *_, **__: lax.psum(s, "rep").astype(f32))
    down_sum = small_total(after(down_shard, dqkv))
    beside = [p.beside for p in widen_rest.parts] if plane else widen_rest
    narrow_out = after(narrow_sum, qkv_grads, output).astype(f32)
    if plane:
        widen_out = widen_rest.finish(width)
        qkv_shard = after(qkv_shard, output, narrow_out, down_sum, widen_top, widen_out)
        widen_out = cast_first(after(widen_top, qkv_shard), after(widen_out, qkv_shard))
    else:
        widen_out = jnp.concatenate([widen_top, widen_rest], axis=0).astype(f32)
    qkv_sum = small_total(qkv_shard, between=widen_out)
    up_out_sum = small_total(after(up_out_shard, qkv_grads, beside), qkv_shard)
    up_sum, out_sum = up_out_sum[:, :hidden_width], up_out_sum[:, hidden_width:]
    small_sum = qkv_sum[:, 3 * width :]
    qkv_sum = qkv_sum[:, : 3 * width].reshape(-1, pairs, 3, 128).swapaxes(1, 2)
    qkv_sum = qkv_sum.reshape(-1, 3 * width)
    return (
        output, token_grads,
        qkv_sum, out_sum, up_sum, down_sum,
        small_sum[:, :experts], small_sum[:, experts], small_sum[:, experts + 1],
        small_sum[:, experts + 2],
        widen_out[None], narrow_out[None],
    )


def solution(mesh):
    rows_spec, exp_spec = P(("rep", "exp"), None), P("exp", None)
    return jax.shard_map(
        body,
        mesh=mesh,
        in_specs=(
            rows_spec, exp_spec, exp_spec, exp_spec, exp_spec, exp_spec,
            P("exp"), P("exp"), P("exp"), P("exp", None, None), P("exp", None, None),
            rows_spec, rows_spec, rows_spec,
        ),
        out_specs=(
            rows_spec, rows_spec, exp_spec, exp_spec, exp_spec, exp_spec, exp_spec,
            P("exp"), P("exp"), P("exp"), P("exp", None, None), P("exp", None, None),
        ),
        check_vma=False,
    )
```
